32 devices in a mesh: pair: 4 (over y, x), task: 8 (over z, core).
Axes of the slice: x: 2, y: 2, z: 4, core: 2. Of those that a mesh axis runs over, the one named last changes fastest.
Arguments:
- factor_blocks: bfloat16 [16, 1536, 625], P('task', 'pair'), may hold values from -1.25 to 1.25
- amplitudes: bfloat16 [16, 512, 625], P('task', 'pair'), may hold values from -0.15625 to 0.15625
- residual_in: float32 [16, 512, 625], P('task', 'pair'), may hold values from -6 to 6
- task_owners: int32 [32, 3], replicated, may hold values from 0 to 7, all different within a row; in each aligned block of 4 rows (0 to 3, 4 to 7, ...) at most 2 rows name the same one
- task_local: int32 [32, 4], replicated, may hold values from 0 to 1
Outputs:
- residual_out: float32 [16, 512, 625], P('task', 'pair')
The draws below stay inside these ranges and needn't reach their ends.
Inputs may be any that keep to these rules, and one draw needn't show every extreme that they name: `task_owners`: the three numbers of a row differ; in each aligned block of 4 rows no number appears more than 2 times.
All inputs are finite; a program needn't handle non-finite values.
Results may differ from the reference program's by a relative error of at most 0.012.
Values may be sent and summed in bfloat16 or wider, within the bound.
No kernel may reach another device: no remote copies, remote signals or barrier semaphores. Data moves between devices by JAX's collectives and lax.ppermute only.
A program may use at most 64 MiB of HBM per device.

```python
import math
import jax
import jax.numpy as jnp
import numpy as np
from jax import lax

TV = 25
TT = 625
NAUX = 1536
NPAIR = 512
BLK_DEV = 2
MOST = 2
NBLK = 16
NTASK = 32
N_PAIR = 4
N_TASK = 8


def with_ends(array, rng, smallest, high):
    dims = array.shape
    spot = [jax.random.randint(jax.random.fold_in(rng, axis), (), 0, dims[axis]) for axis in range(len(dims))]
    array = array.at[tuple(spot)].set(smallest)
    longest = dims.index(max(dims))
    spot[longest] = (spot[longest] + 1) % dims[longest]
    return array.at[tuple(spot)].set(high)


def block_levels(key, shape, split, least, high):
    def one(axis_at, blocks):
        steps = jax.random.uniform(jax.random.fold_in(jax.random.fold_in(key, 6), axis_at), (blocks,), jnp.float32, least / len(split), high / len(split))
        return jnp.repeat(jnp.exp(steps), shape[axis_at] // blocks).reshape((-1,) + (1,) * (len(shape) - axis_at - 1))

    factor_of = one(*split[0])
    for cut in split[1:]:
        factor_of = factor_of * one(*cut)
    return factor_of


def shared_out(stream_key, own, number, rows, amount, top, bound, skew):
    order = jax.random.permutation(stream_key, amount)
    packed, ordinary = shares(amount, rows * top, bound, skew, True), shares(amount, rows * top, bound, skew, False)
    places = jnp.arange(amount)

    def named(lengths, turn):
        used = int((lengths > 0).sum())
        fixed = max(1, used // 4)
        shifted = fixed + (places - fixed + turn * (used - fixed)) % max(1, amount - fixed)
        return jnp.zeros((amount,), jnp.int32).at[order[jnp.where(places < fixed, places, shifted)]].set(jnp.asarray(lengths, jnp.int32))

    lengths = jnp.where(number % 4 == 0, named(packed, number // 4), named(ordinary, number - number // 4 - 1))
    mixed = jax.random.permutation(jax.random.fold_in(own, 3), amount)
    giver, sink = mixed[0:amount // 2 * 2:2], mixed[1:amount // 2 * 2:2]
    margin = jnp.minimum(lengths[giver] - 1, bound - lengths[sink]) // 2
    margin = jnp.where((giver == order[0]) | (sink == order[0]) | (lengths[sink] == 0), 0, jnp.maximum(margin, 0))
    shifted = jax.random.randint(jax.random.fold_in(own, 4), (amount // 2,), 0, 1 << 20) % (margin + 1)
    lengths = lengths.at[giver].add(-shifted).at[sink].add(shifted)
    labels = jnp.searchsorted(jnp.cumsum(lengths), jnp.arange(rows * top), side="right").astype(jnp.int32)
    table = labels.reshape(top, rows).T
    table = table[jax.random.permutation(jax.random.fold_in(own, 1), rows)]
    turn = jax.random.randint(jax.random.fold_in(own, 2), (rows, 1), 0, top)
    return jnp.take_along_axis(table, (jnp.arange(top)[None, :] + turn) % top, axis=1)


def shares(count, total, bound, skew, full):
    portions = [(1 << 20) // math.isqrt(rank ** skew) + 1 for rank in range(1, count + 1)]
    largest = bound if full else min(bound, max(-(-total // count), total * portions[0] // sum(portions)))
    least = 1 if total - largest >= count - 1 else 0
    holding, surplus = [largest] + [least] * (count - 1), total - largest - least * (count - 1)
    while surplus > 0:
        free = [i for i in range(1, count) if holding[i] < largest] or [i for i in range(1, count) if holding[i] < bound]
        mass, remaining = sum([portions[i] for i in free]), surplus
        for i in free:
            more = min(bound - holding[i], max(1, remaining * portions[i] // mass), surplus)
            holding[i] = holding[i] + more
            surplus = surplus - more
    return np.array(holding)


def centred(stream_key, shape, deviation, most, pieces=(), held_as=jnp.bfloat16):
    level = block_levels(stream_key, shape, pieces, -0.22, 0.18) if pieces else 1.0
    entries = jax.random.normal(stream_key, shape, jnp.float32) * deviation * level
    return jnp.minimum(jnp.maximum(entries, -most), most).astype(held_as)


def setup_inputs(seed: int = 0) -> dict:
    keys = jax.random.split(jax.random.key(seed), 6)
    factor_blocks = centred(keys[0], (NBLK, NAUX, TT), TV ** -0.5, 1.25, ((0, 8), (1, 4)))
    amplitudes = centred(keys[1], (NBLK, NPAIR, TT), NAUX ** -0.5, 0.15625, ((0, 8), (1, 4)))
    residual_in = centred(keys[2], (NBLK, NPAIR, TT), 1.0, 6.0, ((0, 8), (1, 4)), jnp.float32)
    task_owners_keys = jax.random.split(jax.random.fold_in(keys[3], 1), NTASK // N_PAIR)
    task_owners_turns = jax.random.permutation(jax.random.fold_in(keys[3], 3), NTASK // N_PAIR)
    task_owners = jax.vmap(lambda own, number: shared_out(jax.random.fold_in(keys[3], 2), own, number, N_PAIR, N_TASK, 3, MOST, 2))(task_owners_keys, task_owners_turns).reshape((NTASK, 3))
    task_local = with_ends(jax.random.randint(keys[4], (NTASK, 4), 0, BLK_DEV), jax.random.fold_in(keys[4], 1), 0, BLK_DEV - 1).astype(jnp.int32)
    return {"factor_blocks": factor_blocks, "amplitudes": amplitudes, "residual_in": residual_in, "task_owners": task_owners, "task_local": task_local}


def reference(factor_blocks, amplitudes, residual_in, task_owners, task_local):
    task_total = task_owners.shape[0]
    columns = (jnp.arange(task_total, dtype=jnp.int32) // N_PAIR).astype(jnp.int32)
    row_ids = (task_owners[:, 0] * BLK_DEV + task_local[:, 0]).astype(jnp.int32)
    col_ids = (task_owners[:, 1] * BLK_DEV + task_local[:, 1]).astype(jnp.int32)
    amp_ids = (task_owners[:, 2] * BLK_DEV + task_local[:, 2]).astype(jnp.int32)
    out_ids = (columns * BLK_DEV + task_local[:, 3]).astype(jnp.int32)

    def one_task(accumulated, indices):
        row_id, col_id, amp_id, out_id = indices
        row_factor = lax.dynamic_index_in_dim(factor_blocks, row_id, 0, keepdims=False)
        col_factor = lax.dynamic_index_in_dim(factor_blocks, col_id, 0, keepdims=False)
        amp_block = lax.dynamic_index_in_dim(amplitudes, amp_id, 0, keepdims=False)
        integral_tile = jnp.dot(row_factor.T, col_factor, preferred_element_type=jnp.float32).astype(jnp.bfloat16)
        ladder = jnp.einsum('icd,acbd->iab', amp_block.reshape(NPAIR, TV, TV).astype(jnp.float32), integral_tile.reshape(TV, TV, TV, TV).astype(jnp.float32))
        ladder = ladder.astype(jnp.bfloat16).reshape(NPAIR, TT)
        current = lax.dynamic_index_in_dim(accumulated, out_id, 0, keepdims=False)
        updated = current + ladder.astype(accumulated.dtype)
        accumulated = lax.dynamic_update_index_in_dim(accumulated, updated, out_id, 0)
        return accumulated, None

    result, ignored = lax.scan(one_task, residual_in, (row_ids, col_ids, amp_ids, out_ids))
    return result
```

```python
import functools

import jax
import jax.numpy as jnp
import numpy as np
from jax import lax
from jax.experimental import pallas as pl
from jax.experimental.pallas import tpu as pltpu
from jax.sharding import PartitionSpec as P

TV = 25
PAD = 32
GROUP = 4
LANES = PAD * GROUP
GROUPS = -(-TV // GROUP)
ROWS = TV * PAD
WIDE = GROUPS * LANES
STEP = 2 * LANES
BF = jnp.bfloat16
F32 = jnp.float32
VMEM_BYTES = 48 * 1024 * 1024


def placement(major_first, width):
    x, y = np.divmod(np.arange(TV * TV), TV)
    spots = x * PAD + y if major_first else y * PAD + x
    return (spots[:, None] == np.arange(width)[None, :]).astype(jnp.bfloat16)


def prepare_kernel(tile_ref, rows_of_ref, lanes_of_ref, *refs):
    rows_ref, lanes_ref = refs[-2:]
    tile = tile_ref[0]
    rows_ref[0] = lax.dot_general(
        rows_of_ref[...], tile, (((1,), (1,)), ((), ())), preferred_element_type=F32
    ).astype(BF)
    lanes_ref[0] = jnp.dot(tile, lanes_of_ref[...], preferred_element_type=F32).astype(BF)


def prepare(tiles, first, total, rows_of, lanes_of, held):
    count, depth, width = tiles.shape
    whole = lambda shape: pl.BlockSpec(shape, lambda i: (0,) * len(shape))
    out_shape = (
        jax.ShapeDtypeStruct((total, ROWS, depth), BF),
        jax.ShapeDtypeStruct((total, depth, WIDE), BF),
    )
    out_specs = (
        pl.BlockSpec((1, ROWS, depth), lambda i: (first + i, 0, 0)),
        pl.BlockSpec((1, depth, WIDE), lambda i: (first + i, 0, 0)),
    )
    in_specs = [
        pl.BlockSpec((1, depth, width), lambda i: (i, 0, 0)),
        whole(rows_of.shape),
        whole(lanes_of.shape),
    ]
    operands = [tiles, rows_of, lanes_of]
    aliases = {}
    if held is not None:
        in_specs += [pl.BlockSpec(memory_space=pl.ANY)] * 2
        operands += list(held)
        aliases = {3: 0, 4: 1}
    return pl.pallas_call(
        prepare_kernel,
        out_shape=out_shape,
        grid=(count,),
        in_specs=in_specs,
        out_specs=out_specs,
        input_output_aliases=aliases,
        compiler_params=pltpu.CompilerParams(vmem_limit_bytes=VMEM_BYTES),
        cost_estimate=pl.CostEstimate(
            flops=4 * count * depth * width * ROWS,
            bytes_accessed=2 * count * depth * (width + ROWS + WIDE),
            transcendentals=0,
        ),
    )(*operands)


def swap_blocks(blocks, low, even):
    r0, r1, r2, r3 = blocks
    turn = lambda block, by: pltpu.roll(block, by, 1)
    s0 = jnp.where(low, r0, turn(r2, LANES // 2))
    s2 = jnp.where(low, turn(r0, LANES // 2), r2)
    s1 = jnp.where(low, r1, turn(r3, LANES // 2))
    s3 = jnp.where(low, turn(r1, LANES // 2), r3)
    return (
        jnp.where(even, s0, turn(s1, PAD)),
        jnp.where(even, turn(s0, LANES - PAD), s1),
        jnp.where(even, s2, turn(s3, PAD)),
        jnp.where(even, turn(s2, LANES - PAD), s3),
    )


def ladder_kernel(r_at, c_at, t_at, o_at, rows_ref, lanes_ref, amp_ref, back_ref, out_ref, v_ref, w_ref, acc_ref):
    step, steps = pl.program_id(1), pl.num_programs(1)
    at = pl.program_id(0) * steps + step

    @pl.when(step == 0)
    def _():
        acc_ref[...] = jnp.zeros_like(acc_ref)

    lane = lax.broadcasted_iota(jnp.int32, (PAD, LANES), 1)
    low = lane < LANES // 2
    even = (lane // PAD) % 2 == 0
    nothing = jnp.zeros((PAD, LANES), F32)
    ladder = None
    for part, start in enumerate(range(0, WIDE, STEP)):
        size = min(STEP, WIDE - start)
        slot = part % 2
        v_ref[slot, :, :size] = jnp.dot(
            rows_ref[0], lanes_ref[0, :, start : start + size], preferred_element_type=F32
        )
        for inner in range(0, size, LANES):
            first = (start + inner) // PAD
            for group in range(GROUPS):
                blocks = [
                    v_ref[slot, b * PAD : (b + 1) * PAD, inner : inner + LANES] if b < TV else nothing
                    for b in range(group * GROUP, (group + 1) * GROUP)
                ]
                for c, block in enumerate(swap_blocks(blocks, low, even), first):
                    if c < TV:
                        w_ref[c * PAD : (c + 1) * PAD, group * LANES : (group + 1) * LANES] = block.astype(BF)
        stop = min(start + size, ROWS)
        term = jnp.dot(amp_ref[0, :, start:stop], w_ref[start:stop, :], preferred_element_type=F32)
        ladder = term if ladder is None else ladder + term
    acc_ref[o_at[at]] += ladder

    @pl.when(step == steps - 1)
    def _():
        for m in range(acc_ref.shape[0]):
            out_ref[0, m] = jnp.dot(acc_ref[m].astype(BF), back_ref[...], preferred_element_type=F32).astype(BF)


def ladders(places, rows, lanes, amps, back, blocks_here):
    columns, tasks, _ = places.shape
    depth, pairs = lanes.shape[1], amps.shape[1]
    tables = [places[:, :, i].reshape(-1) for i in range(4)]
    return pl.pallas_call(
        ladder_kernel,
        out_shape=jax.ShapeDtypeStruct((columns, blocks_here, pairs, TV * TV), BF),
        grid_spec=pltpu.PrefetchScalarGridSpec(
            num_scalar_prefetch=4,
            grid=(columns, tasks),
            in_specs=[
                pl.BlockSpec((1, ROWS, depth), lambda i, j, r, c, t, o: (c[i * tasks + j], 0, 0)),
                pl.BlockSpec((1, depth, WIDE), lambda i, j, r, c, t, o: (r[i * tasks + j], 0, 0)),
                pl.BlockSpec((1, pairs, WIDE), lambda i, j, r, c, t, o: (t[i * tasks + j], 0, 0)),
                pl.BlockSpec(back.shape, lambda i, j, r, c, t, o: (0, 0)),
            ],
            out_specs=pl.BlockSpec((1, blocks_here, pairs, TV * TV), lambda i, j, r, c, t, o: (i, 0, 0, 0)),
            scratch_shapes=[
                pltpu.VMEM((2, ROWS, STEP), F32),
                pltpu.VMEM((ROWS, WIDE), BF),
                pltpu.VMEM((blocks_here, pairs, WIDE), F32),
            ],
        ),
        compiler_params=pltpu.CompilerParams(vmem_limit_bytes=VMEM_BYTES),
        cost_estimate=pl.CostEstimate(
            flops=2 * columns * tasks * ROWS * WIDE * (depth + pairs),
            bytes_accessed=2 * columns * tasks * ((ROWS + WIDE) * depth + pairs * WIDE),
            transcendentals=0,
        ),
    )(*tables, rows, lanes, amps, back)


def gather_pairs(part, pair_count):
    if pair_count != 4 or part.shape[0] != 2:
        return lax.all_gather(part, "pair", axis=1, tiled=True)
    beside = lambda x, bit: lax.ppermute(x, "pair", [(p, p ^ bit) for p in range(pair_count)])
    across, along = beside(part, 1), beside(part, 2)
    corner = jnp.concatenate([beside(along[:1], 1), beside(across[1:], 2)], axis=0)
    return jnp.concatenate([part, across, along, corner], axis=1)


def per_device(factor_blocks, amplitudes, residual_in, task_owners, task_local):
    pair_count = lax.axis_size("pair")
    task_count = lax.axis_size("task")
    column = lax.axis_index("task")
    blocks_here, depth_here, _ = factor_blocks.shape
    levels = task_count // 2
    level, core = column // 2, column % 2
    depth = depth_here // levels
    other_core = lambda x: lax.ppermute(x, "task", [(c, c ^ 1) for c in range(task_count)])

    def up(x, by):
        return lax.ppermute(x, "task", [(c, (c + 2 * by) % task_count) for c in range(task_count)])

    rows_of = jnp.asarray(placement(True, ROWS).T)
    lanes_of = jnp.asarray(placement(False, WIDE))
    amp_lanes = jnp.asarray(placement(True, WIDE))
    back = jnp.asarray(placement(False, WIDE).T)

    slices = factor_blocks.reshape(blocks_here, levels, depth, -1)
    mine = [
        lax.dynamic_index_in_dim(slices, (level + by) % levels, 1, keepdims=False) for by in range(levels)
    ]
    parts = [mine[0]] + [up(mine[by], by) for by in range(1, levels)]
    amp_parts = [amplitudes] + [up(amplitudes, by) for by in range(1, levels)]

    total = 2 * levels * blocks_here
    held = None
    for by, part in enumerate(parts):
        tiles = gather_pairs(part, pair_count)
        held = prepare(tiles, 2 * by * blocks_here, total, rows_of, lanes_of, held)
        held = prepare(other_core(tiles), (2 * by + 1) * blocks_here, total, rows_of, lanes_of, held)
    amps_mine = jnp.stack(amp_parts, axis=0)
    amps = jnp.stack([amps_mine, other_core(amps_mine)], axis=1)
    amps = amps.reshape(total, *amplitudes.shape[1:])
    amps = jnp.einsum("tiw,wv->tiv", amps, amp_lanes, preferred_element_type=F32).astype(BF)

    owners = task_owners.reshape(levels, 2, -1, 3)
    local = task_local.reshape(levels, 2, -1, 4)
    owners = lax.dynamic_index_in_dim(owners, core, 1, keepdims=False)
    local = lax.dynamic_index_in_dim(local, core, 1, keepdims=False)
    spot = (((level - owners // 2) % levels) * 2 + (owners % 2 != core)) * blocks_here + local[:, :, :3]
    places = jnp.concatenate([spot, local[:, :, 3:]], axis=2).astype(jnp.int32)
    order = (level + jnp.arange(levels)) % levels
    places = places[order]

    total_sum = residual_in
    calls = min(levels, 4)
    width = levels // calls
    for call in reversed(range(calls)):
        sums = ladders(places[call * width : (call + 1) * width], *held, amps, back, blocks_here)
        for i in range(width):
            by = call * width + i
            total_sum = total_sum + (up(sums[i], by) if by else sums[i]).astype(F32)
    return total_sum


def solution(mesh):
    placed = (P("task", "pair", None), P("task", "pair", None), P("task", "pair", None), P(), P())
    return jax.shard_map(
        per_device, mesh=mesh, in_specs=placed, out_specs=P("task", "pair", None), check_vma=False
    )
```

```python
import functools

import jax
import jax.numpy as jnp
import numpy as np
from jax import lax
from jax.experimental import pallas as pl
from jax.experimental.pallas import tpu as pltpu
from jax.sharding import PartitionSpec as P

TV = 25
PAD = 32
GROUP = 4
LANES = PAD * GROUP
GROUPS = -(-TV // GROUP)
ROWS = TV * PAD
WIDE = GROUPS * LANES
ORDER = [x for g in range(GROUP) for x in range(g, TV, GROUP)]
START = [ORDER.index(g) * PAD for g in range(GROUP)] + [ROWS]
PLACE = np.argsort(ORDER)
PREPARE_STEPS = 5
BF = jnp.bfloat16
F32 = jnp.float32
VMEM_BYTES = 48 * 1024 * 1024


def spread(spots, rows):
    return (np.arange(rows)[:, None] == spots[None, :]).astype(jnp.bfloat16)


def forms_matrix():
    x, y = np.divmod(np.arange(TV * TV), TV)
    return np.concatenate([spread(PLACE[y] * PAD + x, ROWS), spread(x * PAD + y, ROWS)], axis=0)


def back_matrix():
    a, b = np.divmod(np.arange(TV * TV), TV)
    return spread(PLACE[a] * PAD + b, ROWS).T


def prepare_kernel(pieces, *refs):
    tile_refs, matrix_ref = refs[:pieces], refs[pieces]
    forms_ref, all_ref = refs[-2:]
    count, size, _ = tile_refs[0].shape
    depth = forms_ref.shape[2]

    @pl.when(pl.program_id(0) == 0)
    def _():
        for m in range(count):
            for i, ref in enumerate(tile_refs):
                start = m * depth + i * size
                all_ref[start : start + size, :] = ref[m]

    wide = count if depth % LANES == 0 else 1
    for first in range(0, count, wide):
        made = lax.dot_general(
            matrix_ref[...],
            all_ref[first * depth : (first + wide) * depth, :],
            (((1,), (1,)), ((), ())),
            preferred_element_type=F32,
        ).astype(BF)
        for m in range(wide):
            forms_ref[first + m] = made[:, m * depth : (m + 1) * depth]


def prepare(parts, first, total, matrix, held):
    count, size, width = parts[0].shape
    depth = size * len(parts)
    rows = matrix.shape[0] // PREPARE_STEPS
    in_specs = [pl.BlockSpec(part.shape, lambda i: (0, 0, 0)) for part in parts]
    in_specs.append(pl.BlockSpec((rows, width), lambda i: (i, 0)))
    operands = [*parts, matrix]
    aliases = {}
    if held is not None:
        aliases = {len(operands): 0}
        in_specs.append(pl.BlockSpec(memory_space=pl.ANY))
        operands.append(held)
    return pl.pallas_call(
        functools.partial(prepare_kernel, len(parts)),
        out_shape=jax.ShapeDtypeStruct((total, matrix.shape[0], depth), BF),
        grid=(PREPARE_STEPS,),
        in_specs=in_specs,
        out_specs=pl.BlockSpec((count, rows, depth), lambda i: (first, i, 0)),
        scratch_shapes=[pltpu.VMEM((count * depth, width), BF)],
        input_output_aliases=aliases,
        compiler_params=pltpu.CompilerParams(vmem_limit_bytes=VMEM_BYTES),
        cost_estimate=pl.CostEstimate(
            flops=2 * count * depth * width * matrix.shape[0],
            bytes_accessed=2 * count * depth * (width + matrix.shape[0]),
            transcendentals=0,
        ),
    )(*operands)


def turned(ref, groups, by):
    numbers = [min(A * GROUP + (p - by) % GROUP, TV - 1) for A in groups for p in range(GROUP)]
    return jnp.concatenate([ref[x * PAD : (x + 1) * PAD, :] for x in numbers], axis=0)


def ladder_kernel(
    c_at, r_at, t_at, core_at, o_at, c_ref, r_ref, mine_ref, other_ref, back_ref, matrix_ref, out_ref, *scratch
):
    v_ref, u_ref, amp_ref, acc_ref = scratch[:4]
    step, steps = pl.program_id(1), pl.num_programs(1)
    at = pl.program_id(0) * steps + step

    @pl.when(step == 0)
    def _():
        acc_ref[...] = jnp.zeros_like(acc_ref)

    @pl.when(core_at[at] == 0)
    def _():
        amp_ref[...] = mine_ref[0]

    @pl.when(core_at[at] != 0)
    def _():
        amp_ref[...] = other_ref[0]

    if len(scratch) > 4:
        forms = scratch[4]
        for i, tile_ref in enumerate((c_ref, r_ref)):
            forms[i] = lax.dot_general(
                matrix_ref[i * ROWS : (i + 1) * ROWS, :],
                tile_ref[0],
                (((1,), (1,)), ((), ())),
                preferred_element_type=F32,
            ).astype(BF)
        c_form, r_form = forms.at[0], forms.at[1]
    else:
        c_form, r_form = c_ref.at[0], r_ref.at[0]

    spot = lax.broadcasted_iota(jnp.int32, (PAD, LANES), 1) // PAD
    at_spot = [spot == p for p in range(GROUP)]
    nothing = jnp.zeros((PAD, LANES), F32)
    for first in range(0, GROUPS, 2):
        groups = range(first, min(first + 2, GROUPS))
        lanes = slice(groups[0] * LANES, (groups[-1] + 1) * LANES)
        for g in range(GROUP):
            v_ref[START[g] : START[g + 1], lanes] = lax.dot_general(
                c_form[START[g] : START[g + 1], :],
                turned(r_form, groups, g),
                (((1,), (1,)), ((), ())),
                preferred_element_type=F32,
            )
        for A in groups:
            for D in range(GROUPS):
                blocks = [
                    v_ref[START[g] + D * PAD : START[g] + (D + 1) * PAD, A * LANES : (A + 1) * LANES]
                    if D * GROUP + g < TV
                    else nothing
                    for g in range(GROUP)
                ]
                for i in range(min(GROUP, TV - A * GROUP)):
                    block = blocks[-i % GROUP]
                    for p in range(1, GROUP):
                        block = jnp.where(at_spot[p], blocks[(p - i) % GROUP], block)
                    u_ref[START[i] + A * PAD : START[i] + (A + 1) * PAD, D * LANES : (D + 1) * LANES] = block.astype(BF)
    for i in range(GROUP):
        acc_ref[o_at[at], START[i] : START[i + 1], :] += jnp.dot(
            u_ref[START[i] : START[i + 1], :], turned(amp_ref, range(GROUPS), i), preferred_element_type=F32
        )

    @pl.when(step == steps - 1)
    def _():
        for m in range(acc_ref.shape[0]):
            out_ref[0, m] = jnp.dot(back_ref[...], acc_ref[m].astype(BF), preferred_element_type=F32).astype(BF)


def ladders(places, tiles, amps, back, matrix, blocks_here):
    columns, tasks, kinds = places.shape
    pairs = amps[0].shape[2]
    made = tiles.shape[1] == 2 * ROWS
    depth = tiles.shape[2] if made else tiles.shape[1]
    held = (1, ROWS, depth) if made else (1, *tiles.shape[1:])
    more = [] if made else [pltpu.VMEM((2, ROWS, depth), BF)]
    matrix = matrix[:PAD] if made else matrix
    tables = [places[:, :, i].reshape(-1) for i in range(kinds)]
    amp_spec = pl.BlockSpec((1, ROWS, pairs), lambda i, j, c, r, t, k, o: (t[i * tasks + j], 0, 0))
    return pl.pallas_call(
        ladder_kernel,
        out_shape=jax.ShapeDtypeStruct((columns, blocks_here, TV * TV, pairs), BF),
        grid_spec=pltpu.PrefetchScalarGridSpec(
            num_scalar_prefetch=kinds,
            grid=(columns, tasks),
            in_specs=[
                pl.BlockSpec(held, lambda i, j, c, r, t, k, o: (c[i * tasks + j], 0, 0)),
                pl.BlockSpec(held, lambda i, j, c, r, t, k, o: (r[i * tasks + j], int(made), 0)),
                amp_spec,
                amp_spec,
                pl.BlockSpec(back.shape, lambda i, j, c, r, t, k, o: (0, 0)),
                pl.BlockSpec(matrix.shape, lambda i, j, c, r, t, k, o: (0, 0)),
            ],
            out_specs=pl.BlockSpec((1, blocks_here, TV * TV, pairs), lambda i, j, c, r, t, k, o: (i, 0, 0, 0)),
            scratch_shapes=[
                pltpu.VMEM((ROWS, WIDE), F32),
                pltpu.VMEM((ROWS, WIDE), BF),
                pltpu.VMEM((ROWS, pairs), BF),
                pltpu.VMEM((blocks_here, ROWS, pairs), F32),
                *more,
            ],
        ),
        compiler_params=pltpu.CompilerParams(vmem_limit_bytes=VMEM_BYTES),
        cost_estimate=pl.CostEstimate(
            flops=2 * columns * tasks * ROWS * WIDE * (depth + pairs),
            bytes_accessed=2 * columns * tasks * ROWS * 2 * (depth + pairs),
            transcendentals=0,
        ),
    )(*tables, tiles, tiles, *amps, back, matrix)


def gather_pairs(part, by, pair_count):
    beside = lambda x, bit: lax.ppermute(x, "pair", [(p, p ^ bit) for p in range(pair_count)])
    across, along = beside(part, 1), beside(part, 2)
    return [part, across, along, beside(along, 1) if by % 2 == 0 else beside(across, 2)]


def per_device(factor_blocks, amplitudes, residual_in, task_owners, task_local):
    pair_count = lax.axis_size("pair")
    task_count = lax.axis_size("task")
    column = lax.axis_index("task")
    blocks_here, depth_here, _ = factor_blocks.shape
    pairs = amplitudes.shape[1]
    levels = task_count // 2
    level, core = column // 2, column % 2
    depth = depth_here // levels
    other_core = lambda x: lax.ppermute(x, "task", [(c, c ^ 1) for c in range(task_count)])

    def up(x, by):
        return lax.ppermute(x, "task", [(c, (c + 2 * by) % task_count) for c in range(task_count)])

    same_core = [[2 * z + k for z in range(levels)] for k in range(2)]
    tiles = amplitudes.reshape(blocks_here, pairs, TV, TV).transpose(0, 3, 2, 1)
    tiles = jnp.pad(tiles, ((0, 0), (0, 0), (0, PAD - TV), (0, 0))).reshape(blocks_here, ROWS, pairs)
    amps = lax.all_gather(tiles, "task", axis=0, tiled=True, axis_index_groups=same_core)
    amps = (amps, other_core(amps))

    matrix = jnp.asarray(forms_matrix())
    back = jnp.asarray(back_matrix())
    slices = factor_blocks.reshape(blocks_here, levels, depth, -1)
    mine = [lax.dynamic_index_in_dim(slices, (level + by) % levels, 1, keepdims=False) for by in range(levels)]
    parts = [mine[0]] + [up(mine[by], by) for by in range(1, levels)]

    total = 2 * levels * blocks_here
    if pair_count == 4:
        held = None
        for by, part in enumerate(parts):
            pieces = gather_pairs(part, by, pair_count)
            held = prepare(pieces, 2 * by, total, matrix, held)
            held = prepare([other_core(piece) for piece in pieces], 2 * by + 1, total, matrix, held)
    else:
        held = lax.all_gather(jnp.stack(parts), "pair", axis=2, tiled=True)
        held = jnp.stack([held, other_core(held)], axis=1).reshape(total, depth * pair_count, -1)

    owners = lax.dynamic_index_in_dim(task_owners.reshape(levels, 2, -1, 3), core, 1, keepdims=False)
    local = lax.dynamic_index_in_dim(task_local.reshape(levels, 2, -1, 4), core, 1, keepdims=False)
    owner_level, far_core = owners // 2, (owners % 2 != core).astype(jnp.int32)
    factor_at = (((level - owner_level) % levels) * 2 + far_core) * blocks_here + local[:, :, :3]
    amp_at = owner_level[:, :, 2:] * blocks_here + local[:, :, 2:3]
    places = jnp.concatenate(
        [factor_at[:, :, 1:2], factor_at[:, :, :1], amp_at, far_core[:, :, 2:], local[:, :, 3:]], axis=2
    ).astype(jnp.int32)
    places = places[(level + jnp.arange(levels)) % levels]

    ladder = None
    calls = min(levels, 4)
    width = levels // calls
    for call in reversed(range(calls)):
        sums = ladders(places[call * width : (call + 1) * width], held, amps, back, matrix, blocks_here)
        for i in range(width):
            by = call * width + i
            term = (up(sums[i], by) if by else sums[i]).astype(F32)
            ladder = term if ladder is None else ladder + term
    return residual_in + ladder.transpose(0, 2, 1)


def solution(mesh):
    placed = (P("task", "pair", None), P("task", "pair", None), P("task", "pair", None), P(), P())
    return jax.shard_map(
        per_device, mesh=mesh, in_specs=placed, out_specs=P("task", "pair", None), check_vma=False
    )
```

```python
import functools

import jax
import jax.numpy as jnp
import numpy as np
from jax import lax
from jax.experimental import pallas as pl
from jax.experimental.pallas import tpu as pltpu
from jax.sharding import PartitionSpec as P

TV = 25
PAD = 32
GROUP = 4
LANES = PAD * GROUP
GROUPS = -(-TV // GROUP)
ROWS = TV * PAD
WIDE = GROUPS * LANES
ORDER = [x for g in range(GROUP) for x in range(g, TV, GROUP)]
START = [ORDER.index(g) * PAD for g in range(GROUP)] + [ROWS]
PLACE = np.argsort(ORDER)
PREPARE_STEPS = 2
BF = jnp.bfloat16
F32 = jnp.float32
VMEM_BYTES = 48 * 1024 * 1024


def spread(spots, rows):
    return (np.arange(rows)[:, None] == spots[None, :]).astype(jnp.bfloat16)


def forms_matrix():
    x, y = np.divmod(np.arange(TV * TV), TV)
    return np.concatenate([spread(PLACE[y] * PAD + x, ROWS), spread(x * PAD + y, ROWS)], axis=0)


def amp_matrix():
    c, d = np.divmod(np.arange(TV * TV), TV)
    return spread(d * PAD + c, ROWS)


def back_matrix():
    a, b = np.divmod(np.arange(TV * TV), TV)
    return spread(PLACE[a] * PAD + b, ROWS).T


def prepare_kernel(pieces, *refs):
    tile_refs, matrix_ref = refs[:pieces], refs[pieces]
    forms_ref, all_ref = refs[-2:]
    count, size, _ = tile_refs[0].shape
    depth = forms_ref.shape[2]

    @pl.when(pl.program_id(0) == 0)
    def _():
        for m in range(count):
            for i, ref in enumerate(tile_refs):
                start = m * depth + i * size
                all_ref[start : start + size, :] = ref[m]

    wide = count if depth % LANES == 0 else 1
    for first in range(0, count, wide):
        made = lax.dot_general(
            matrix_ref[...],
            all_ref[first * depth : (first + wide) * depth, :],
            (((1,), (1,)), ((), ())),
            preferred_element_type=F32,
        ).astype(BF)
        for m in range(wide):
            forms_ref[first + m] = made[:, m * depth : (m + 1) * depth]


def prepare(parts, first, total, matrix, held):
    count, size, width = parts[0].shape
    depth = size * len(parts)
    rows = matrix.shape[0] // PREPARE_STEPS
    in_specs = [pl.BlockSpec(part.shape, lambda i: (0, 0, 0)) for part in parts]
    in_specs.append(pl.BlockSpec((rows, width), lambda i: (i, 0)))
    operands = [*parts, matrix]
    aliases = {}
    if held is not None:
        aliases = {len(operands): 0}
        in_specs.append(pl.BlockSpec(memory_space=pl.ANY))
        operands.append(held)
    return pl.pallas_call(
        functools.partial(prepare_kernel, len(parts)),
        out_shape=jax.ShapeDtypeStruct((total, matrix.shape[0], depth), BF),
        grid=(PREPARE_STEPS,),
        in_specs=in_specs,
        out_specs=pl.BlockSpec((count, rows, depth), lambda i: (first, i, 0)),
        scratch_shapes=[pltpu.VMEM((count * depth, width), BF)],
        input_output_aliases=aliases,
        compiler_params=pltpu.CompilerParams(vmem_limit_bytes=VMEM_BYTES),
        cost_estimate=pl.CostEstimate(
            flops=2 * count * depth * width * matrix.shape[0],
            bytes_accessed=2 * count * depth * (width + matrix.shape[0]),
            transcendentals=0,
        ),
    )(*operands)


def amp_kernel(levels, matrix_ref, *refs):
    tile_refs, out_ref = refs[:-1], refs[-1]
    blocks_here = out_ref.shape[0] // levels
    pairs = out_ref.shape[2]
    for by in range(levels):
        tiles = tile_refs[0][...] if by == 0 else tile_refs[by][...] + tile_refs[2 * levels - 1 - by][...]
        made = jnp.dot(matrix_ref[...], tiles, preferred_element_type=F32).astype(BF)
        for m in range(blocks_here):
            out_ref[by * blocks_here + m] = made[:, m * pairs : (m + 1) * pairs]


def prepare_amps(own, ups, downs, blocks_here, matrix):
    levels = len(ups) + 1
    pairs = own.shape[1] // blocks_here
    return pl.pallas_call(
        functools.partial(amp_kernel, levels),
        out_shape=jax.ShapeDtypeStruct((levels * blocks_here, ROWS, pairs), BF),
        compiler_params=pltpu.CompilerParams(vmem_limit_bytes=VMEM_BYTES),
        cost_estimate=pl.CostEstimate(
            flops=2 * levels * own.size * ROWS,
            bytes_accessed=4 * levels * own.size,
            transcendentals=0,
        ),
    )(matrix, own, *ups, *downs)


def turned(ref, groups, by):
    numbers = [min(A * GROUP + (p - by) % GROUP, TV - 1) for A in groups for p in range(GROUP)]
    return jnp.concatenate([ref[x * PAD : (x + 1) * PAD, :] for x in numbers], axis=0)


def ladder_kernel(
    find, made, column_ref, owners_ref, local_ref, c_ref, r_ref, mine_ref, other_ref, back_ref, *refs
):
    matrix_ref = None if made else refs[0]
    out_ref, v_ref, u_ref, amp_ref, acc_ref = refs[:5] if made else refs[1:6]
    step, steps = pl.program_id(1), pl.num_programs(1)
    places = find(pl.program_id(0), step, column_ref, owners_ref, local_ref)

    @pl.when(step == 0)
    def _():
        acc_ref[...] = jnp.zeros_like(acc_ref)

    @pl.when(places["amp_core"] == 0)
    def _():
        amp_ref[...] = mine_ref[0]

    @pl.when(places["amp_core"] != 0)
    def _():
        amp_ref[...] = other_ref[0]

    if made:
        c_form, r_form = c_ref.at[0], r_ref.at[0]
    else:
        forms = refs[6]
        for i, tile_ref in enumerate((c_ref, r_ref)):
            forms[i] = lax.dot_general(
                matrix_ref[i * ROWS : (i + 1) * ROWS, :],
                tile_ref[0],
                (((1,), (1,)), ((), ())),
                preferred_element_type=F32,
            ).astype(BF)
        c_form, r_form = forms.at[0], forms.at[1]

    spot = lax.broadcasted_iota(jnp.int32, (PAD, LANES), 1) // PAD
    at_spot = [spot == p for p in range(GROUP)]
    nothing = jnp.zeros((PAD, LANES), F32)
    for first in range(0, GROUPS, 2):
        groups = range(first, min(first + 2, GROUPS))
        lanes = slice(groups[0] * LANES, (groups[-1] + 1) * LANES)
        for g in range(GROUP):
            v_ref[START[g] : START[g + 1], lanes] = lax.dot_general(
                c_form[START[g] : START[g + 1], :],
                turned(r_form, groups, g),
                (((1,), (1,)), ((), ())),
                preferred_element_type=F32,
            )
        for A in groups:
            for D in range(GROUPS):
                blocks = [
                    v_ref[START[g] + D * PAD : START[g] + (D + 1) * PAD, A * LANES : (A + 1) * LANES]
                    if D * GROUP + g < TV
                    else nothing
                    for g in range(GROUP)
                ]
                for i in range(min(GROUP, TV - A * GROUP)):
                    block = blocks[-i % GROUP]
                    for p in range(1, GROUP):
                        block = jnp.where(at_spot[p], blocks[(p - i) % GROUP], block)
                    u_ref[START[i] + A * PAD : START[i] + (A + 1) * PAD, D * LANES : (D + 1) * LANES] = block.astype(BF)
    for i in range(GROUP):
        acc_ref[places["out"], START[i] : START[i + 1], :] += jnp.dot(
            u_ref[START[i] : START[i + 1], :], turned(amp_ref, range(GROUPS), i), preferred_element_type=F32
        )

    @pl.when(step == steps - 1)
    def _():
        for m in range(acc_ref.shape[0]):
            out_ref[0, m] = jnp.dot(back_ref[...], acc_ref[m].astype(BF), preferred_element_type=F32).astype(BF)


def ladders(first, columns, levels, blocks_here, column, task_owners, task_local, tiles, amps, back, matrix):
    tasks = task_owners.shape[0] // (2 * levels)
    pairs = amps[0].shape[2]
    made = tiles.shape[1] == 2 * ROWS
    depth = tiles.shape[2] if made else tiles.shape[1]
    held = (1, ROWS, depth) if made else (1, *tiles.shape[1:])

    def find(i, j, column_ref, owners_ref, local_ref):
        level, core = column_ref[0] // 2, lax.rem(column_ref[0], 2)
        task = (2 * lax.rem(level + first + i, levels) + core) * tasks + j

        def place(kind):
            owner = owners_ref[task, kind]
            below = lax.rem(level - owner // 2 + levels, levels)
            far = jnp.where(lax.rem(owner, 2) != core, 1, 0)
            return below, far, local_ref[task, kind]

        (row_below, row_far, row_m), (col_below, col_far, col_m), (amp_below, amp_far, amp_m) = map(place, range(3))
        return {
            "row": (row_below * 2 + row_far) * blocks_here + row_m,
            "col": (col_below * 2 + col_far) * blocks_here + col_m,
            "amp": amp_below * blocks_here + amp_m,
            "amp_core": amp_far,
            "out": local_ref[task, 3],
        }

    fixed = lambda shape: pl.BlockSpec(shape, lambda i, j, *tables: (0,) * len(shape))
    amp_spec = pl.BlockSpec((1, ROWS, pairs), lambda i, j, *tables: (find(i, j, *tables)["amp"], 0, 0))
    in_specs = [
        pl.BlockSpec(held, lambda i, j, *tables: (find(i, j, *tables)["col"], 0, 0)),
        pl.BlockSpec(held, lambda i, j, *tables: (find(i, j, *tables)["row"], int(made), 0)),
        amp_spec,
        amp_spec,
        fixed(back.shape),
    ]
    scratch = [
        pltpu.VMEM((ROWS, WIDE), F32),
        pltpu.VMEM((ROWS, WIDE), BF),
        pltpu.VMEM((ROWS, pairs), BF),
        pltpu.VMEM((blocks_here, ROWS, pairs), F32),
    ]
    operands = [tiles, tiles, *amps, back]
    if not made:
        in_specs.append(fixed(matrix.shape))
        scratch.append(pltpu.VMEM((2, ROWS, depth), BF))
        operands.append(matrix)
    return pl.pallas_call(
        functools.partial(ladder_kernel, find, made),
        out_shape=jax.ShapeDtypeStruct((columns, blocks_here, TV * TV, pairs), BF),
        grid_spec=pltpu.PrefetchScalarGridSpec(
            num_scalar_prefetch=3,
            grid=(columns, tasks),
            in_specs=in_specs,
            out_specs=pl.BlockSpec((1, blocks_here, TV * TV, pairs), lambda i, j, *tables: (i, 0, 0, 0)),
            scratch_shapes=scratch,
        ),
        compiler_params=pltpu.CompilerParams(vmem_limit_bytes=VMEM_BYTES),
        cost_estimate=pl.CostEstimate(
            flops=2 * columns * tasks * ROWS * WIDE * (depth + pairs),
            bytes_accessed=2 * columns * tasks * ROWS * 2 * (depth + pairs),
            transcendentals=0,
        ),
    )(column, task_owners, task_local, *operands)


def gather_pairs(part, by, pair_count):
    beside = lambda x, bit: lax.ppermute(x, "pair", [(p, p ^ bit) for p in range(pair_count)])
    across, along = beside(part, 1), beside(part, 2)
    return [part, across, along, beside(along, 1) if by % 2 == 0 else beside(across, 2)]


def per_device(factor_blocks, amplitudes, residual_in, task_owners, task_local):
    pair_count = lax.axis_size("pair")
    task_count = lax.axis_size("task")
    column = lax.axis_index("task")
    blocks_here, depth_here, _ = factor_blocks.shape
    pairs = amplitudes.shape[1]
    levels = task_count // 2
    level = column // 2
    depth = depth_here // levels
    total = 2 * levels * blocks_here
    matrix = jnp.asarray(forms_matrix())
    back = jnp.asarray(back_matrix())
    other_core = lambda x: lax.ppermute(x, "task", [(c, c ^ 1) for c in range(task_count)])

    def around(x, by):
        return lax.ppermute(x, "task", [(c, (c + 2 * by) % task_count) for c in range(task_count)])

    def hop(x, by):
        return lax.ppermute(x, "task", [(c, c + by) for c in range(task_count) if 0 <= c + by < task_count])

    slices = factor_blocks.reshape(blocks_here, levels, depth, -1)
    mine = [lax.dynamic_index_in_dim(slices, (level + by) % levels, 1, keepdims=False) for by in range(levels)]
    parts = [mine[0]] + [around(mine[by], by) for by in range(1, levels)]
    if pair_count == 4:
        own = amplitudes.transpose(2, 0, 1).reshape(TV * TV, blocks_here * pairs)
        ups, downs = [hop(own, 2)], [hop(own, -2)]
        for by in range(2, levels):
            (up, down), _ = lax.optimization_barrier(((ups[-1], downs[-1]), parts[1:]))
            ups.append(hop(up, 2))
            downs.append(hop(down, -2))
        amps = prepare_amps(own, ups, downs, blocks_here, jnp.asarray(amp_matrix()))
        held = None
        for by, part in enumerate(parts):
            pieces = gather_pairs(part, by, pair_count)
            held = prepare(pieces, 2 * by, total, matrix, held)
            held = prepare([other_core(piece) for piece in pieces], 2 * by + 1, total, matrix, held)
    else:
        tiles = amplitudes.reshape(blocks_here, pairs, TV, TV).transpose(0, 3, 2, 1)
        tiles = jnp.pad(tiles, ((0, 0), (0, 0), (0, PAD - TV), (0, 0))).reshape(blocks_here, ROWS, pairs)
        same_core = [[2 * z + k for z in range(levels)] for k in range(2)]
        amps = lax.all_gather(tiles, "task", axis=0, axis_index_groups=same_core)
        amps = amps[(level - jnp.arange(levels)) % levels].reshape(levels * blocks_here, ROWS, pairs)
        held = lax.all_gather(jnp.stack(parts), "pair", axis=2, tiled=True)
        held = jnp.stack([held, other_core(held)], axis=1).reshape(total, depth * pair_count, -1)
    amps = (amps, other_core(amps))

    ladder = None
    calls = min(levels, 4)
    width = levels // calls
    order = [2, 3, 1, 0] if calls == 4 else list(reversed(range(calls)))
    for call in order:
        first = call * width
        sums = ladders(
            first, width, levels, blocks_here, column[None], task_owners, task_local, held, amps, back, matrix
        )
        for i in range(width):
            term = (around(sums[i], first + i) if first + i else sums[i]).astype(F32)
            ladder = term if ladder is None else ladder + term
    return residual_in + ladder.transpose(0, 2, 1)


def solution(mesh):
    placed = (P("task", "pair", None), P("task", "pair", None), P("task", "pair", None), P(), P())
    return jax.shard_map(
        per_device, mesh=mesh, in_specs=placed, out_specs=P("task", "pair", None), check_vma=False
    )
```

```python
import functools

import jax
import jax.numpy as jnp
import numpy as np
from jax import lax
from jax.experimental import pallas as pl
from jax.experimental.pallas import tpu as pltpu
from jax.sharding import PartitionSpec as P

TV = 25
PAD = 32
GROUP = 4
LANES = PAD * GROUP
GROUPS = -(-TV // GROUP)
ROWS = TV * PAD
WIDE = GROUPS * LANES
ORDER = [x for g in range(GROUP) for x in range(g, TV, GROUP)]
START = [ORDER.index(g) * PAD for g in range(GROUP)] + [ROWS]
PLACE = np.argsort(ORDER)
PREPARE_STEPS = 2
BF = jnp.bfloat16
F32 = jnp.float32
VMEM_BYTES = 48 * 1024 * 1024


def spread(spots, rows):
    return (np.arange(rows)[:, None] == spots[None, :]).astype(jnp.bfloat16)


def forms_matrix():
    x, y = np.divmod(np.arange(TV * TV), TV)
    return np.concatenate([spread(PLACE[y] * PAD + x, ROWS), spread(x * PAD + y, ROWS)], axis=0)


def amp_matrix():
    c, d = np.divmod(np.arange(TV * TV), TV)
    return spread(d * PAD + c, ROWS)


def back_matrix():
    a, b = np.divmod(np.arange(TV * TV), TV)
    return spread(PLACE[a] * PAD + b, ROWS).T


def prepare_kernel(pieces, *refs):
    tile_refs, matrix_ref = refs[:pieces], refs[pieces]
    forms_ref, all_ref = refs[-2:]
    count, size, _ = tile_refs[0].shape
    depth = forms_ref.shape[2]

    @pl.when(pl.program_id(0) == 0)
    def _():
        for m in range(count):
            for i, ref in enumerate(tile_refs):
                start = m * depth + i * size
                all_ref[start : start + size, :] = ref[m]

    wide = count if depth % LANES == 0 else 1
    for first in range(0, count, wide):
        made = lax.dot_general(
            matrix_ref[...],
            all_ref[first * depth : (first + wide) * depth, :],
            (((1,), (1,)), ((), ())),
            preferred_element_type=F32,
        ).astype(BF)
        for m in range(wide):
            forms_ref[first + m] = made[:, m * depth : (m + 1) * depth]


def prepare(parts, matrix):
    count, size, width = parts[0].shape
    depth = size * len(parts)
    rows = matrix.shape[0] // PREPARE_STEPS
    in_specs = [pl.BlockSpec(part.shape, lambda i: (0, 0, 0)) for part in parts]
    in_specs.append(pl.BlockSpec((rows, width), lambda i: (i, 0)))
    return pl.pallas_call(
        functools.partial(prepare_kernel, len(parts)),
        out_shape=jax.ShapeDtypeStruct((count, matrix.shape[0], depth), BF),
        grid=(PREPARE_STEPS,),
        in_specs=in_specs,
        out_specs=pl.BlockSpec((count, rows, depth), lambda i: (0, i, 0)),
        scratch_shapes=[pltpu.VMEM((count * depth, width), BF)],
        compiler_params=pltpu.CompilerParams(vmem_limit_bytes=VMEM_BYTES),
        cost_estimate=pl.CostEstimate(
            flops=2 * count * depth * width * matrix.shape[0],
            bytes_accessed=2 * count * depth * (width + matrix.shape[0]),
            transcendentals=0,
        ),
    )(*parts, matrix)


def amp_kernel(levels, matrix_ref, *refs):
    tile_refs, out_ref = refs[:-1], refs[-1]
    blocks_here = out_ref.shape[0] // levels
    pairs = out_ref.shape[2]
    for by in range(levels):
        tiles = tile_refs[0][...] if by == 0 else tile_refs[by][...] + tile_refs[2 * levels - 1 - by][...]
        made = jnp.dot(matrix_ref[...], tiles, preferred_element_type=F32).astype(BF)
        for m in range(blocks_here):
            out_ref[by * blocks_here + m] = made[:, m * pairs : (m + 1) * pairs]


def prepare_amps(own, ups, downs, blocks_here, matrix):
    levels = len(ups) + 1
    pairs = own.shape[1] // blocks_here
    return pl.pallas_call(
        functools.partial(amp_kernel, levels),
        out_shape=jax.ShapeDtypeStruct((levels * blocks_here, ROWS, pairs), BF),
        compiler_params=pltpu.CompilerParams(vmem_limit_bytes=VMEM_BYTES),
        cost_estimate=pl.CostEstimate(
            flops=2 * levels * own.size * ROWS,
            bytes_accessed=4 * levels * own.size,
            transcendentals=0,
        ),
    )(matrix, own, *ups, *downs)


def turned(ref, groups, by):
    numbers = [min(A * GROUP + (p - by) % GROUP, TV - 1) for A in groups for p in range(GROUP)]
    return jnp.concatenate([ref[x * PAD : (x + 1) * PAD, :] for x in numbers], axis=0)


def ladder_kernel(find, made, sources, column_ref, owners_ref, local_ref, *refs):
    factor_refs, amp_refs, refs = refs[:sources], refs[sources : sources + 2], refs[sources + 2 :]
    back_ref, matrix_ref, refs = refs[0], None if made else refs[1], refs[1 if made else 2 :]
    out_ref, v_ref, u_ref, acc_ref, c_buf, r_buf, amp_buf, sems = refs[:8]
    column, columns = pl.program_id(0), pl.num_programs(0)
    step, steps = pl.program_id(1), pl.num_programs(1)
    at = column * steps + step
    slot = lax.rem(at, 2)

    def fetch(choices, source, index, part, buffer, to, sem):
        for n, ref in enumerate(choices):

            @pl.when(source == n)
            def _():
                tile = ref.at[index, pl.ds(part * ROWS, ROWS)] if part is not None else ref.at[index]
                pltpu.make_async_copy(tile, buffer.at[to], sem).start()

    def fetch_task(i, j, to):
        places = find(i, j, column_ref, owners_ref, local_ref)
        fetch(factor_refs, *places["col"], 0 if made else None, c_buf, to, sems.at[to, 0])
        fetch(factor_refs, *places["row"], 1 if made else None, r_buf, to, sems.at[to, 1])
        fetch(amp_refs, *places["amp"], None, amp_buf, to, sems.at[to, 2])

    @pl.when(at == 0)
    def _():
        fetch_task(0, 0, 0)

    @pl.when(at + 1 < columns * steps)
    def _():
        last = step == steps - 1
        fetch_task(jnp.where(last, column + 1, column), jnp.where(last, 0, step + 1), 1 - slot)

    @pl.when(step == 0)
    def _():
        acc_ref[...] = jnp.zeros_like(acc_ref)

    for n, buffer in enumerate((c_buf, r_buf, amp_buf)):
        pltpu.make_async_copy(buffer.at[slot], buffer.at[slot], sems.at[slot, n]).wait()
    c_form, r_form, amp_form = c_buf.at[slot], r_buf.at[slot], amp_buf.at[slot]
    if not made:
        forms = refs[8]
        for i, tile in enumerate((c_form, r_form)):
            forms[i] = lax.dot_general(
                matrix_ref[i * ROWS : (i + 1) * ROWS, :],
                tile[...],
                (((1,), (1,)), ((), ())),
                preferred_element_type=F32,
            ).astype(BF)
        c_form, r_form = forms.at[0], forms.at[1]

    spot = lax.broadcasted_iota(jnp.int32, (PAD, LANES), 1) // PAD
    at_spot = [spot == p for p in range(GROUP)]
    nothing = jnp.zeros((PAD, LANES), F32)
    for first in range(0, GROUPS, 2):
        groups = range(first, min(first + 2, GROUPS))
        lanes = slice(groups[0] * LANES, (groups[-1] + 1) * LANES)
        for g in range(GROUP):
            v_ref[START[g] : START[g + 1], lanes] = lax.dot_general(
                c_form[START[g] : START[g + 1], :],
                turned(r_form, groups, g),
                (((1,), (1,)), ((), ())),
                preferred_element_type=F32,
            )
        for A in groups:
            for D in range(GROUPS):
                blocks = [
                    v_ref[START[g] + D * PAD : START[g] + (D + 1) * PAD, A * LANES : (A + 1) * LANES]
                    if D * GROUP + g < TV
                    else nothing
                    for g in range(GROUP)
                ]
                for i in range(min(GROUP, TV - A * GROUP)):
                    block = blocks[-i % GROUP]
                    for p in range(1, GROUP):
                        block = jnp.where(at_spot[p], blocks[(p - i) % GROUP], block)
                    u_ref[START[i] + A * PAD : START[i] + (A + 1) * PAD, D * LANES : (D + 1) * LANES] = block.astype(BF)
    out = local_ref[find(column, step, column_ref, owners_ref, local_ref)["task"], 3]
    for i in range(GROUP):
        acc_ref[out, START[i] : START[i + 1], :] += jnp.dot(
            u_ref[START[i] : START[i + 1], :], turned(amp_form, range(GROUPS), i), preferred_element_type=F32
        )

    @pl.when(step == steps - 1)
    def _():
        for m in range(acc_ref.shape[0]):
            out_ref[0, m] = jnp.dot(back_ref[...], acc_ref[m].astype(BF), preferred_element_type=F32).astype(BF)


def ladders(first, columns, levels, blocks_here, column, task_owners, task_local, tiles, amps, back, matrix):
    tasks = task_owners.shape[0] // (2 * levels)
    pairs = amps[0].shape[2]
    made = tiles[0].shape[1] == 2 * ROWS
    depth = tiles[0].shape[2] if made else tiles[0].shape[1]
    held = (ROWS, depth) if made else tiles[0].shape[1:]

    def find(i, j, column_ref, owners_ref, local_ref):
        level, core = column_ref[0] // 2, lax.rem(column_ref[0], 2)
        task = (2 * lax.rem(level + first + i, levels) + core) * tasks + j

        def place(kind):
            owner = owners_ref[task, kind]
            below = lax.rem(level - owner // 2 + levels, levels)
            far = jnp.where(lax.rem(owner, 2) != core, 1, 0)
            return below, far, local_ref[task, kind]

        def factor(kind):
            below, far, m = place(kind)
            return (below * 2 + far, m) if made else (0, (below * 2 + far) * blocks_here + m)

        below, far, m = place(2)
        return {"task": task, "row": factor(0), "col": factor(1), "amp": (far, below * blocks_here + m)}

    anywhere = pl.BlockSpec(memory_space=pl.ANY)
    fixed = lambda shape: pl.BlockSpec(shape, lambda i, j, *tables: (0,) * len(shape))
    operands = [*tiles, *amps, back]
    in_specs = [anywhere] * (len(tiles) + 2) + [fixed(back.shape)]
    scratch = [
        pltpu.VMEM((ROWS, WIDE), F32),
        pltpu.VMEM((ROWS, WIDE), BF),
        pltpu.VMEM((blocks_here, ROWS, pairs), F32),
        pltpu.VMEM((2, *held), BF),
        pltpu.VMEM((2, *held), BF),
        pltpu.VMEM((2, ROWS, pairs), BF),
        pltpu.SemaphoreType.DMA((2, 3)),
    ]
    if not made:
        in_specs.append(fixed(matrix.shape))
        scratch.append(pltpu.VMEM((2, ROWS, depth), BF))
        operands.append(matrix)
    return pl.pallas_call(
        functools.partial(ladder_kernel, find, made, len(tiles)),
        out_shape=jax.ShapeDtypeStruct((columns, blocks_here, TV * TV, pairs), BF),
        grid_spec=pltpu.PrefetchScalarGridSpec(
            num_scalar_prefetch=3,
            grid=(columns, tasks),
            in_specs=in_specs,
            out_specs=pl.BlockSpec((1, blocks_here, TV * TV, pairs), lambda i, j, *tables: (i, 0, 0, 0)),
            scratch_shapes=scratch,
        ),
        compiler_params=pltpu.CompilerParams(vmem_limit_bytes=VMEM_BYTES),
        cost_estimate=pl.CostEstimate(
            flops=2 * columns * tasks * ROWS * WIDE * (depth + pairs),
            bytes_accessed=2 * columns * tasks * ROWS * 2 * (depth + pairs),
            transcendentals=0,
        ),
    )(column, task_owners, task_local, *operands)


def beside(x, bit, pair_count):
    return lax.ppermute(x, "pair", [(p, p ^ bit) for p in range(pair_count)])


def per_device(factor_blocks, amplitudes, residual_in, task_owners, task_local):
    pair_count = lax.axis_size("pair")
    task_count = lax.axis_size("task")
    column = lax.axis_index("task")
    blocks_here, depth_here, _ = factor_blocks.shape
    pairs = amplitudes.shape[1]
    levels = task_count // 2
    level = column // 2
    depth = depth_here // levels
    total = 2 * levels * blocks_here
    matrix = jnp.asarray(forms_matrix())
    back = jnp.asarray(back_matrix())
    other_core = lambda x: lax.ppermute(x, "task", [(c, c ^ 1) for c in range(task_count)])

    def around(x, by):
        return lax.ppermute(x, "task", [(c, (c + 2 * by) % task_count) for c in range(task_count)])

    def hop(x, by):
        return lax.ppermute(x, "task", [(c, c + by) for c in range(task_count) if 0 <= c + by < task_count])

    slices = factor_blocks.reshape(blocks_here, levels, depth, -1)
    mine = [lax.dynamic_index_in_dim(slices, (level + by) % levels, 1, keepdims=False) for by in range(levels)]
    parts = [mine[0]] + [around(mine[by], by) for by in range(1, levels)]
    if pair_count == 4:
        own = amplitudes.transpose(2, 0, 1).reshape(TV * TV, blocks_here * pairs)
        (own,), _ = lax.optimization_barrier(((own,), parts[1:]))
        ups, downs = [hop(own, 2)], [hop(own, -2)]
        for by in range(2, levels):
            ups.append(hop(ups[-1], 2))
            downs.append(hop(downs[-1], -2))
        amps = prepare_amps(own, ups, downs, blocks_here, jnp.asarray(amp_matrix()))
        held, flying = [], ()
        for by, part in enumerate(parts):
            part, flying = lax.optimization_barrier((part, flying))
            across, along = beside(part, 1, pair_count), beside(part, 2, pair_count)
            corner = beside(along, 1, pair_count) if by % 2 == 0 else beside(across, 2, pair_count)
            flying = (across, along)
            forms = prepare([part, across, along, corner], matrix)
            held += [forms, other_core(forms)]
    else:
        tiles = amplitudes.reshape(blocks_here, pairs, TV, TV).transpose(0, 3, 2, 1)
        tiles = jnp.pad(tiles, ((0, 0), (0, 0), (0, PAD - TV), (0, 0))).reshape(blocks_here, ROWS, pairs)
        same_core = [[2 * z + k for z in range(levels)] for k in range(2)]
        amps = lax.all_gather(tiles, "task", axis=0, axis_index_groups=same_core)
        amps = amps[(level - jnp.arange(levels)) % levels].reshape(levels * blocks_here, ROWS, pairs)
        held = lax.all_gather(jnp.stack(parts), "pair", axis=2, tiled=True)
        held = [jnp.stack([held, other_core(held)], axis=1).reshape(total, depth * pair_count, -1)]
    amps = (amps, other_core(amps))

    ladder = None
    calls = min(levels, 4)
    width = levels // calls
    order = [2, 3, 1, 0] if calls == 4 else list(reversed(range(calls)))
    for call in order:
        first = call * width
        sums = ladders(
            first, width, levels, blocks_here, column[None], task_owners, task_local, held, amps, back, matrix
        )
        for i in range(width):
            term = (around(sums[i], first + i) if first + i else sums[i]).astype(F32)
            ladder = term if ladder is None else ladder + term
    return residual_in + ladder.transpose(0, 2, 1)


def solution(mesh):
    placed = (P("task", "pair", None), P("task", "pair", None), P("task", "pair", None), P(), P())
    return jax.shard_map(
        per_device, mesh=mesh, in_specs=placed, out_specs=P("task", "pair", None), check_vma=False
    )
```

```python
import functools

import jax
import jax.numpy as jnp
import numpy as np
from jax import lax
from jax.experimental import pallas as pl
from jax.experimental.pallas import tpu as pltpu
from jax.sharding import PartitionSpec as P

TV = 25
PAD = 32
GROUP = 4
LANES = PAD * GROUP
GROUPS = -(-TV // GROUP)
ROWS = TV * PAD
WIDE = GROUPS * LANES
ORDER = [x for g in range(GROUP) for x in range(g, TV, GROUP)]
START = [ORDER.index(g) * PAD for g in range(GROUP)] + [ROWS]
PLACE = np.argsort(ORDER)
PREPARE_STEPS = 2
BF = jnp.bfloat16
F32 = jnp.float32
VMEM_BYTES = 48 * 1024 * 1024


def spread(spots, rows):
    return (np.arange(rows)[:, None] == spots[None, :]).astype(jnp.bfloat16)


def forms_matrix():
    x, y = np.divmod(np.arange(TV * TV), TV)
    return np.concatenate([spread(PLACE[y] * PAD + x, ROWS), spread(x * PAD + y, ROWS)], axis=0)


def amp_matrix():
    c, d = np.divmod(np.arange(TV * TV), TV)
    return spread(d * PAD + c, ROWS)


def back_matrix():
    a, b = np.divmod(np.arange(TV * TV), TV)
    return spread(PLACE[a] * PAD + b, ROWS).T


def prepare_kernel(pieces, *refs):
    tile_refs, matrix_ref = refs[:pieces], refs[pieces]
    forms_ref, all_ref = refs[-2:]
    count, size, _ = tile_refs[0].shape
    depth = forms_ref.shape[2]

    @pl.when(pl.program_id(0) == 0)
    def _():
        for m in range(count):
            for i, ref in enumerate(tile_refs):
                start = m * depth + i * size
                all_ref[start : start + size, :] = ref[m]

    wide = count if depth % LANES == 0 else 1
    for first in range(0, count, wide):
        made = lax.dot_general(
            matrix_ref[...],
            all_ref[first * depth : (first + wide) * depth, :],
            (((1,), (1,)), ((), ())),
            preferred_element_type=F32,
        ).astype(BF)
        for m in range(wide):
            forms_ref[first + m] = made[:, m * depth : (m + 1) * depth]


def prepare(parts, matrix):
    count, size, width = parts[0].shape
    depth = size * len(parts)
    rows = matrix.shape[0] // PREPARE_STEPS
    in_specs = [pl.BlockSpec(part.shape, lambda i: (0, 0, 0)) for part in parts]
    in_specs.append(pl.BlockSpec((rows, width), lambda i: (i, 0)))
    return pl.pallas_call(
        functools.partial(prepare_kernel, len(parts)),
        out_shape=jax.ShapeDtypeStruct((count, matrix.shape[0], depth), BF),
        grid=(PREPARE_STEPS,),
        in_specs=in_specs,
        out_specs=pl.BlockSpec((count, rows, depth), lambda i: (0, i, 0)),
        scratch_shapes=[pltpu.VMEM((count * depth, width), BF)],
        compiler_params=pltpu.CompilerParams(vmem_limit_bytes=VMEM_BYTES),
        cost_estimate=pl.CostEstimate(
            flops=2 * count * depth * width * matrix.shape[0],
            bytes_accessed=2 * count * depth * (width + matrix.shape[0]),
            transcendentals=0,
        ),
    )(*parts, matrix)


def amp_kernel(matrix_ref, *refs):
    tile_refs, out_ref = refs[:-1], refs[-1]
    blocks_here, pairs = out_ref.shape[0] // len(tile_refs), out_ref.shape[2]
    for by, ref in enumerate(tile_refs):
        made = jnp.dot(matrix_ref[...], ref[...], preferred_element_type=F32).astype(BF)
        for m in range(blocks_here):
            out_ref[by * blocks_here + m] = made[:, m * pairs : (m + 1) * pairs]


def prepare_amps(parts, blocks_here, matrix):
    levels, size = len(parts), parts[0].size
    pairs = parts[0].shape[1] // blocks_here
    return pl.pallas_call(
        amp_kernel,
        out_shape=jax.ShapeDtypeStruct((levels * blocks_here, ROWS, pairs), BF),
        compiler_params=pltpu.CompilerParams(vmem_limit_bytes=VMEM_BYTES),
        cost_estimate=pl.CostEstimate(
            flops=2 * levels * size * ROWS, bytes_accessed=4 * levels * size, transcendentals=0
        ),
    )(matrix, *parts)


def turned(ref, groups, by):
    numbers = [min(A * GROUP + (p - by) % GROUP, TV - 1) for A in groups for p in range(GROUP)]
    return jnp.concatenate([ref[x * PAD : (x + 1) * PAD, :] for x in numbers], axis=0)


def ladder_kernel(find, made, sources, column_ref, owners_ref, local_ref, *refs):
    factor_refs, amp_refs, refs = refs[:sources], refs[sources : sources + 2], refs[sources + 2 :]
    back_ref, matrix_ref, refs = refs[0], None if made else refs[1], refs[1 if made else 2 :]
    out_ref, v_ref, u_ref, acc_ref, c_buf, r_buf, amp_buf, sems = refs[:8]
    column, columns = pl.program_id(0), pl.num_programs(0)
    step, steps = pl.program_id(1), pl.num_programs(1)
    at = column * steps + step
    slot = lax.rem(at, 2)

    def fetch(choices, source, index, part, buffer, to, sem):
        for n, ref in enumerate(choices):

            @pl.when(source == n)
            def _():
                tile = ref.at[index, pl.ds(part * ROWS, ROWS)] if part is not None else ref.at[index]
                pltpu.make_async_copy(tile, buffer.at[to], sem).start()

    def fetch_task(i, j, to):
        places = find(i, j, column_ref, owners_ref, local_ref)
        fetch(factor_refs, *places["col"], 0 if made else None, c_buf, to, sems.at[to, 0])
        fetch(factor_refs, *places["row"], 1 if made else None, r_buf, to, sems.at[to, 1])
        fetch(amp_refs, *places["amp"], None, amp_buf, to, sems.at[to, 2])

    @pl.when(at == 0)
    def _():
        fetch_task(0, 0, 0)

    @pl.when(at + 1 < columns * steps)
    def _():
        last = step == steps - 1
        fetch_task(jnp.where(last, column + 1, column), jnp.where(last, 0, step + 1), 1 - slot)

    @pl.when(step == 0)
    def _():
        acc_ref[...] = jnp.zeros_like(acc_ref)

    for n, buffer in enumerate((c_buf, r_buf, amp_buf)):
        pltpu.make_async_copy(buffer.at[slot], buffer.at[slot], sems.at[slot, n]).wait()
    c_form, r_form, amp_form = c_buf.at[slot], r_buf.at[slot], amp_buf.at[slot]
    if not made:
        forms = refs[8]
        for i, tile in enumerate((c_form, r_form)):
            forms[i] = lax.dot_general(
                matrix_ref[i * ROWS : (i + 1) * ROWS, :],
                tile[...],
                (((1,), (1,)), ((), ())),
                preferred_element_type=F32,
            ).astype(BF)
        c_form, r_form = forms.at[0], forms.at[1]

    spot = lax.broadcasted_iota(jnp.int32, (PAD, LANES), 1) // PAD
    at_spot = [spot == p for p in range(GROUP)]
    nothing = jnp.zeros((PAD, LANES), F32)
    for first in range(0, GROUPS, 2):
        groups = range(first, min(first + 2, GROUPS))
        lanes = slice(groups[0] * LANES, (groups[-1] + 1) * LANES)
        for g in range(GROUP):
            v_ref[START[g] : START[g + 1], lanes] = lax.dot_general(
                c_form[START[g] : START[g + 1], :],
                turned(r_form, groups, g),
                (((1,), (1,)), ((), ())),
                preferred_element_type=F32,
            )
        for A in groups:
            for D in range(GROUPS):
                blocks = [
                    v_ref[START[g] + D * PAD : START[g] + (D + 1) * PAD, A * LANES : (A + 1) * LANES]
                    if D * GROUP + g < TV
                    else nothing
                    for g in range(GROUP)
                ]
                for i in range(min(GROUP, TV - A * GROUP)):
                    block = blocks[-i % GROUP]
                    for p in range(1, GROUP):
                        block = jnp.where(at_spot[p], blocks[(p - i) % GROUP], block)
                    u_ref[START[i] + A * PAD : START[i] + (A + 1) * PAD, D * LANES : (D + 1) * LANES] = block.astype(BF)
    out = local_ref[find(column, step, column_ref, owners_ref, local_ref)["task"], 3]
    for i in range(GROUP):
        acc_ref[out, START[i] : START[i + 1], :] += jnp.dot(
            u_ref[START[i] : START[i + 1], :], turned(amp_form, range(GROUPS), i), preferred_element_type=F32
        )

    @pl.when(step == steps - 1)
    def _():
        blocks_here, pairs = out_ref.shape[1], out_ref.shape[3]
        sums = jnp.concatenate([acc_ref[m].astype(BF) for m in range(blocks_here)], axis=1)
        sums = jnp.dot(back_ref[...], sums, preferred_element_type=F32).astype(BF)
        for m in range(blocks_here):
            out_ref[0, m] = sums[:, m * pairs : (m + 1) * pairs]


def ladders(first, columns, levels, blocks_here, column, task_owners, task_local, tiles, amps, back, matrix):
    tasks = task_owners.shape[0] // (2 * levels)
    pairs = amps[0].shape[2]
    made = tiles[0].shape[1] == 2 * ROWS
    depth = tiles[0].shape[2] if made else tiles[0].shape[1]
    held = (ROWS, depth) if made else tiles[0].shape[1:]

    def find(i, j, column_ref, owners_ref, local_ref):
        level, core = column_ref[0] // 2, lax.rem(column_ref[0], 2)
        task = (2 * lax.rem(level + first + i, levels) + core) * tasks + j

        def place(kind):
            owner = owners_ref[task, kind]
            below = lax.rem(level - owner // 2 + levels, levels)
            far = jnp.where(lax.rem(owner, 2) != core, 1, 0)
            return below, far, local_ref[task, kind]

        def factor(kind):
            below, far, m = place(kind)
            return (below * 2 + far, m) if made else (0, (below * 2 + far) * blocks_here + m)

        below, far, m = place(2)
        return {"task": task, "row": factor(0), "col": factor(1), "amp": (far, below * blocks_here + m)}

    anywhere = pl.BlockSpec(memory_space=pl.ANY)
    fixed = lambda shape: pl.BlockSpec(shape, lambda i, j, *tables: (0,) * len(shape))
    operands = [*tiles, *amps, back]
    in_specs = [anywhere] * (len(tiles) + 2) + [fixed(back.shape)]
    scratch = [
        pltpu.VMEM((ROWS, WIDE), F32),
        pltpu.VMEM((ROWS, WIDE), BF),
        pltpu.VMEM((blocks_here, ROWS, pairs), F32),
        pltpu.VMEM((2, *held), BF),
        pltpu.VMEM((2, *held), BF),
        pltpu.VMEM((2, ROWS, pairs), BF),
        pltpu.SemaphoreType.DMA((2, 3)),
    ]
    if not made:
        in_specs.append(fixed(matrix.shape))
        scratch.append(pltpu.VMEM((2, ROWS, depth), BF))
        operands.append(matrix)
    return pl.pallas_call(
        functools.partial(ladder_kernel, find, made, len(tiles)),
        out_shape=jax.ShapeDtypeStruct((columns, blocks_here, TV * TV, pairs), BF),
        grid_spec=pltpu.PrefetchScalarGridSpec(
            num_scalar_prefetch=3,
            grid=(columns, tasks),
            in_specs=in_specs,
            out_specs=pl.BlockSpec((1, blocks_here, TV * TV, pairs), lambda i, j, *tables: (i, 0, 0, 0)),
            scratch_shapes=scratch,
        ),
        compiler_params=pltpu.CompilerParams(vmem_limit_bytes=VMEM_BYTES),
        cost_estimate=pl.CostEstimate(
            flops=2 * columns * tasks * ROWS * WIDE * (depth + pairs),
            bytes_accessed=2 * columns * tasks * ROWS * 2 * (depth + pairs),
            transcendentals=0,
        ),
    )(column, task_owners, task_local, *operands)


def beside(x, bit, pair_count):
    return lax.ppermute(x, "pair", [(p, p ^ bit) for p in range(pair_count)])


def per_device(factor_blocks, amplitudes, residual_in, task_owners, task_local):
    pair_count = lax.axis_size("pair")
    task_count = lax.axis_size("task")
    column = lax.axis_index("task")
    blocks_here, depth_here, _ = factor_blocks.shape
    pairs = amplitudes.shape[1]
    levels = task_count // 2
    level = column // 2
    depth = depth_here // levels
    total = 2 * levels * blocks_here
    matrix = jnp.asarray(forms_matrix())
    back = jnp.asarray(back_matrix())
    other_core = lambda x: lax.ppermute(x, "task", [(c, c ^ 1) for c in range(task_count)])

    def around(x, by):
        return lax.ppermute(x, "task", [(c, (c + 2 * by) % task_count) for c in range(task_count)])

    slices = factor_blocks.reshape(blocks_here, levels, depth, -1)
    mine = [lax.dynamic_index_in_dim(slices, (level + by) % levels, 1, keepdims=False) for by in range(levels)]
    parts = [mine[0]] + [around(mine[by], by) for by in range(1, levels)]
    if pair_count == 4:
        own = amplitudes.transpose(2, 0, 1).reshape(TV * TV, blocks_here * pairs)
        (own,), _ = lax.optimization_barrier(((own,), parts[1:]))
        amps = [own] + [around(own, by) for by in range(1, levels)]
        amps = prepare_amps(amps, blocks_here, jnp.asarray(amp_matrix()))
        held, flying = [], ()
        for by, part in enumerate(parts):
            part, flying = lax.optimization_barrier((part, flying))
            across, along = beside(part, 1, pair_count), beside(part, 2, pair_count)
            corner = beside(along, 1, pair_count) if by % 2 == 0 else beside(across, 2, pair_count)
            flying = (across, along)
            forms = prepare([part, across, along, corner], matrix)
            held += [forms, other_core(forms)]
    else:
        tiles = amplitudes.reshape(blocks_here, pairs, TV, TV).transpose(0, 3, 2, 1)
        tiles = jnp.pad(tiles, ((0, 0), (0, 0), (0, PAD - TV), (0, 0))).reshape(blocks_here, ROWS, pairs)
        same_core = [[2 * z + k for z in range(levels)] for k in range(2)]
        amps = lax.all_gather(tiles, "task", axis=0, axis_index_groups=same_core)
        amps = amps[(level - jnp.arange(levels)) % levels].reshape(levels * blocks_here, ROWS, pairs)
        held = lax.all_gather(jnp.stack(parts), "pair", axis=2, tiled=True)
        held = [jnp.stack([held, other_core(held)], axis=1).reshape(total, depth * pair_count, -1)]
    amps = (amps, other_core(amps))

    ladder = None
    calls = min(levels, 4)
    width = levels // calls
    order = [2, 3, 1, 0] if calls == 4 else list(reversed(range(calls)))
    for call in order:
        first = call * width
        sums = ladders(
            first, width, levels, blocks_here, column[None], task_owners, task_local, held, amps, back, matrix
        )
        for i in range(width):
            term = (around(sums[i], first + i) if first + i else sums[i]).astype(F32)
            ladder = term if ladder is None else ladder + term
    return residual_in + ladder.transpose(0, 2, 1)


def solution(mesh):
    placed = (P("task", "pair", None), P("task", "pair", None), P("task", "pair", None), P(), P())
    return jax.shard_map(
        per_device, mesh=mesh, in_specs=placed, out_specs=P("task", "pair", None), check_vma=False
    )
```

```python
import functools

import jax
import jax.numpy as jnp
import numpy as np
from jax import lax
from jax.experimental import pallas as pl
from jax.experimental.pallas import tpu as pltpu
from jax.sharding import PartitionSpec as P

TV = 25
PAD = 32
GROUP = 4
LANES = PAD * GROUP
GROUPS = -(-TV // GROUP)
ROWS = TV * PAD
WIDE = GROUPS * LANES
ORDER = [x for g in range(GROUP) for x in range(g, TV, GROUP)]
START = [ORDER.index(g) * PAD for g in range(GROUP)] + [ROWS]
PLACE = np.argsort(ORDER)
PREPARE_STEPS = 2
BF = jnp.bfloat16
F32 = jnp.float32
VMEM_BYTES = 48 * 1024 * 1024


def spread(spots, rows):
    return (np.arange(rows)[:, None] == spots[None, :]).astype(jnp.bfloat16)


def forms_matrix():
    x, y = np.divmod(np.arange(TV * TV), TV)
    return np.concatenate([spread(PLACE[y] * PAD + x, ROWS), spread(x * PAD + y, ROWS)], axis=0)


def amp_matrix():
    c, d = np.divmod(np.arange(TV * TV), TV)
    return spread(d * PAD + c, ROWS)


def back_matrix():
    a, b = np.divmod(np.arange(TV * TV), TV)
    return spread(PLACE[a] * PAD + b, ROWS).T


def prepare_kernel(column_ref, *refs):
    tile_refs, matrix_ref, forms_ref, all_ref = refs[:4], refs[4], refs[5], refs[6]
    count, size, _ = tile_refs[0].shape
    depth = forms_ref.shape[2]

    @pl.when(pl.program_id(0) == 0)
    def _():
        core = lax.rem(column_ref[0], 2)
        for m in range(count):
            for place, ref in zip((0, 1 + core, 2 - core, 3), tile_refs):
                start = pl.multiple_of(m * depth + place * size, size)
                all_ref[pl.ds(start, size), :] = ref[m]

    wide = count if depth % LANES == 0 else 1
    for first in range(0, count, wide):
        made = lax.dot_general(
            matrix_ref[...],
            all_ref[first * depth : (first + wide) * depth, :],
            (((1,), (1,)), ((), ())),
            preferred_element_type=F32,
        ).astype(BF)
        for m in range(wide):
            forms_ref[first + m] = made[:, m * depth : (m + 1) * depth]


def prepare(parts, column, matrix):
    count, size, width = parts[0].shape
    depth = size * len(parts)
    rows = matrix.shape[0] // PREPARE_STEPS
    in_specs = [pl.BlockSpec(part.shape, lambda i, column: (0, 0, 0)) for part in parts]
    in_specs.append(pl.BlockSpec((rows, width), lambda i, column: (i, 0)))
    return pl.pallas_call(
        prepare_kernel,
        out_shape=jax.ShapeDtypeStruct((count, matrix.shape[0], depth), BF),
        grid_spec=pltpu.PrefetchScalarGridSpec(
            num_scalar_prefetch=1,
            grid=(PREPARE_STEPS,),
            in_specs=in_specs,
            out_specs=pl.BlockSpec((count, rows, depth), lambda i, column: (0, i, 0)),
            scratch_shapes=[pltpu.VMEM((count * depth, width), BF)],
        ),
        compiler_params=pltpu.CompilerParams(vmem_limit_bytes=VMEM_BYTES),
        cost_estimate=pl.CostEstimate(
            flops=2 * count * depth * width * matrix.shape[0],
            bytes_accessed=2 * count * depth * (width + matrix.shape[0]),
            transcendentals=0,
        ),
    )(column, *parts, matrix)


def amp_kernel(matrix_ref, tiles_ref, out_ref):
    pairs = out_ref.shape[2]
    made = jnp.dot(matrix_ref[...], tiles_ref[0], preferred_element_type=F32).astype(BF)
    for m in range(out_ref.shape[0]):
        out_ref[m] = made[:, m * pairs : (m + 1) * pairs]


def prepare_amps(tiles, blocks_here, matrix):
    levels, entries, width = tiles.shape
    pairs = width // blocks_here
    return pl.pallas_call(
        amp_kernel,
        out_shape=jax.ShapeDtypeStruct((levels * blocks_here, ROWS, pairs), BF),
        grid=(levels,),
        in_specs=[
            pl.BlockSpec(matrix.shape, lambda i: (0, 0)),
            pl.BlockSpec((1, entries, width), lambda i: (i, 0, 0)),
        ],
        out_specs=pl.BlockSpec((blocks_here, ROWS, pairs), lambda i: (i, 0, 0)),
        compiler_params=pltpu.CompilerParams(vmem_limit_bytes=VMEM_BYTES),
        cost_estimate=pl.CostEstimate(
            flops=2 * tiles.size * ROWS, bytes_accessed=4 * tiles.size, transcendentals=0
        ),
    )(matrix, tiles)


def turned(ref, groups, by):
    numbers = [min(A * GROUP + (p - by) % GROUP, TV - 1) for A in groups for p in range(GROUP)]
    return jnp.concatenate([ref[x * PAD : (x + 1) * PAD, :] for x in numbers], axis=0)


def ladder_kernel(find, made, sources, column_ref, owners_ref, local_ref, *refs):
    factor_refs, amp_refs, refs = refs[:sources], refs[sources : sources + 2], refs[sources + 2 :]
    back_ref, matrix_ref, refs = refs[0], None if made else refs[1], refs[1 if made else 2 :]
    out_ref, v_ref, u_ref, acc_ref, c_buf, r_buf, amp_buf, sems = refs[:8]
    column, columns = pl.program_id(0), pl.num_programs(0)
    step, steps = pl.program_id(1), pl.num_programs(1)
    at = column * steps + step
    slot = lax.rem(at, 2)

    def fetch(choices, source, index, part, buffer, to, sem):
        for n, ref in enumerate(choices):

            @pl.when(source == n)
            def _():
                tile = ref.at[index, pl.ds(part * ROWS, ROWS)] if part is not None else ref.at[index]
                pltpu.make_async_copy(tile, buffer.at[to], sem).start()

    def fetch_task(i, j, to):
        places = find(i, j, column_ref, owners_ref, local_ref)
        fetch(factor_refs, *places["col"], 0 if made else None, c_buf, to, sems.at[to, 0])
        fetch(factor_refs, *places["row"], 1 if made else None, r_buf, to, sems.at[to, 1])
        fetch(amp_refs, *places["amp"], None, amp_buf, to, sems.at[to, 2])

    @pl.when(at == 0)
    def _():
        fetch_task(0, 0, 0)

    @pl.when(at + 1 < columns * steps)
    def _():
        last = step == steps - 1
        fetch_task(jnp.where(last, column + 1, column), jnp.where(last, 0, step + 1), 1 - slot)

    @pl.when(step == 0)
    def _():
        acc_ref[...] = jnp.zeros_like(acc_ref)

    for n, buffer in enumerate((c_buf, r_buf, amp_buf)):
        pltpu.make_async_copy(buffer.at[slot], buffer.at[slot], sems.at[slot, n]).wait()
    c_form, r_form, amp_form = c_buf.at[slot], r_buf.at[slot], amp_buf.at[slot]
    if not made:
        forms = refs[8]
        for i, tile in enumerate((c_form, r_form)):
            forms[i] = lax.dot_general(
                matrix_ref[i * ROWS : (i + 1) * ROWS, :],
                tile[...],
                (((1,), (1,)), ((), ())),
                preferred_element_type=F32,
            ).astype(BF)
        c_form, r_form = forms.at[0], forms.at[1]

    spot = lax.broadcasted_iota(jnp.int32, (PAD, LANES), 1) // PAD
    at_spot = [spot == p for p in range(GROUP)]
    nothing = jnp.zeros((PAD, LANES), F32)
    for first in range(0, GROUPS, 2):
        groups = range(first, min(first + 2, GROUPS))
        lanes = slice(groups[0] * LANES, (groups[-1] + 1) * LANES)
        for g in range(GROUP):
            v_ref[START[g] : START[g + 1], lanes] = lax.dot_general(
                c_form[START[g] : START[g + 1], :],
                turned(r_form, groups, g),
                (((1,), (1,)), ((), ())),
                preferred_element_type=F32,
            )
        for A in groups:
            for D in range(GROUPS):
                blocks = [
                    v_ref[START[g] + D * PAD : START[g] + (D + 1) * PAD, A * LANES : (A + 1) * LANES]
                    if D * GROUP + g < TV
                    else nothing
                    for g in range(GROUP)
                ]
                for i in range(min(GROUP, TV - A * GROUP)):
                    block = blocks[-i % GROUP]
                    for p in range(1, GROUP):
                        block = jnp.where(at_spot[p], blocks[(p - i) % GROUP], block)
                    u_ref[START[i] + A * PAD : START[i] + (A + 1) * PAD, D * LANES : (D + 1) * LANES] = block.astype(BF)
    out = local_ref[find(column, step, column_ref, owners_ref, local_ref)["task"], 3]
    for i in range(GROUP):
        acc_ref[out, START[i] : START[i + 1], :] += jnp.dot(
            u_ref[START[i] : START[i + 1], :], turned(amp_form, range(GROUPS), i), preferred_element_type=F32
        )

    @pl.when(step == steps - 1)
    def _():
        blocks_here, pairs = out_ref.shape[1], out_ref.shape[3]
        sums = jnp.concatenate([acc_ref[m].astype(BF) for m in range(blocks_here)], axis=1)
        sums = jnp.dot(back_ref[...], sums, preferred_element_type=F32).astype(BF)
        for m in range(blocks_here):
            out_ref[0, m] = sums[:, m * pairs : (m + 1) * pairs]


def ladders(first, columns, levels, blocks_here, column, task_owners, task_local, tiles, amps, back, matrix):
    tasks = task_owners.shape[0] // (2 * levels)
    pairs = amps[0].shape[2]
    made = tiles[0].shape[1] == 2 * ROWS
    depth = tiles[0].shape[2] if made else tiles[0].shape[1]
    held = (ROWS, depth) if made else tiles[0].shape[1:]

    def find(i, j, column_ref, owners_ref, local_ref):
        level, core = column_ref[0] // 2, lax.rem(column_ref[0], 2)
        task = (2 * lax.rem(level + first + i, levels) + core) * tasks + j

        def place(kind):
            owner = owners_ref[task, kind]
            below = lax.rem(level - owner // 2 + levels, levels)
            far = jnp.where(lax.rem(owner, 2) != core, 1, 0)
            return below, far, local_ref[task, kind]

        def factor(kind):
            below, far, m = place(kind)
            return (below * 2 + far, m) if made else (0, (below * 2 + far) * blocks_here + m)

        _, far, m = place(2)
        amp = owners_ref[task, 2] // 2 * blocks_here + m
        return {"task": task, "row": factor(0), "col": factor(1), "amp": (far, amp)}

    anywhere = pl.BlockSpec(memory_space=pl.ANY)
    fixed = lambda shape: pl.BlockSpec(shape, lambda i, j, *tables: (0,) * len(shape))
    operands = [*tiles, *amps, back]
    in_specs = [anywhere] * (len(tiles) + 2) + [fixed(back.shape)]
    scratch = [
        pltpu.VMEM((ROWS, WIDE), F32),
        pltpu.VMEM((ROWS, WIDE), BF),
        pltpu.VMEM((blocks_here, ROWS, pairs), F32),
        pltpu.VMEM((2, *held), BF),
        pltpu.VMEM((2, *held), BF),
        pltpu.VMEM((2, ROWS, pairs), BF),
        pltpu.SemaphoreType.DMA((2, 3)),
    ]
    if not made:
        in_specs.append(fixed(matrix.shape))
        scratch.append(pltpu.VMEM((2, ROWS, depth), BF))
        operands.append(matrix)
    return pl.pallas_call(
        functools.partial(ladder_kernel, find, made, len(tiles)),
        out_shape=jax.ShapeDtypeStruct((columns, blocks_here, TV * TV, pairs), BF),
        grid_spec=pltpu.PrefetchScalarGridSpec(
            num_scalar_prefetch=3,
            grid=(columns, tasks),
            in_specs=in_specs,
            out_specs=pl.BlockSpec((1, blocks_here, TV * TV, pairs), lambda i, j, *tables: (i, 0, 0, 0)),
            scratch_shapes=scratch,
        ),
        compiler_params=pltpu.CompilerParams(vmem_limit_bytes=VMEM_BYTES),
        cost_estimate=pl.CostEstimate(
            flops=2 * columns * tasks * ROWS * WIDE * (depth + pairs),
            bytes_accessed=2 * columns * tasks * ROWS * 2 * (depth + pairs),
            transcendentals=0,
        ),
    )(column, task_owners, task_local, *operands)


def after(values, done):
    return lax.optimization_barrier((values, done))[0]


def per_device(factor_blocks, amplitudes, residual_in, task_owners, task_local):
    pair_count = lax.axis_size("pair")
    task_count = lax.axis_size("task")
    column = lax.axis_index("task")
    blocks_here, depth_here, _ = factor_blocks.shape
    pairs = amplitudes.shape[1]
    levels = task_count // 2
    level = column // 2
    depth = depth_here // levels
    total = 2 * levels * blocks_here
    matrix = jnp.asarray(forms_matrix())
    back = jnp.asarray(back_matrix())
    other_core = lambda x: lax.ppermute(x, "task", [(c, c ^ 1) for c in range(task_count)])

    def around(x, by):
        return lax.ppermute(x, "task", [(c, (c + 2 * by) % task_count) for c in range(task_count)])

    same_core = [[2 * z + k for z in range(levels)] for k in range(2)]
    slices = factor_blocks.reshape(blocks_here, levels, depth, -1)
    mine = [lax.dynamic_index_in_dim(slices, (level + by) % levels, 1, keepdims=False) for by in range(levels)]
    if pair_count == 4 and levels == 4:
        sides = [
            [(p * task_count + c, (p ^ (1 if c % 2 == turn else 2)) * task_count + c) for p in range(4) for c in range(task_count)]
            for turn in range(2)
        ]
        first_side = lambda x: lax.ppermute(x, ("pair", "task"), sides[0])
        second_side = lambda x: lax.ppermute(x, ("pair", "task"), sides[1])
        part0 = mine[0]
        a0, b0, part1, part3 = first_side(part0), second_side(part0), around(mine[1], 1), around(mine[3], 3)

        a0, b0, part0, part1, part3, to2 = after((a0, b0, part0, part1, part3, mine[2]), ())
        q0, a1, b1, a3, part2 = second_side(a0), first_side(part1), second_side(part1), first_side(part3), around(to2, 2)

        own = amplitudes.transpose(2, 0, 1).reshape(TV * TV, blocks_here * pairs)
        own = jnp.broadcast_to(own, (levels, *own.shape))
        own, q0, a1, b1, a3, part2, part3 = after((own, q0, a1, b1, a3, part2, part3), ())
        own = lax.all_to_all(own, "task", split_axis=0, concat_axis=0, axis_index_groups=same_core)
        q1, b3, a2, b2 = second_side(a1), second_side(part3), first_side(part2), second_side(part2)
        forms0 = prepare([part0, a0, b0, q0], column[None], matrix)
        far0 = other_core(forms0)

        q1, b3, a2, b2, a3 = after((q1, b3, a2, b2, a3), forms0)
        q2, q3 = second_side(a2), second_side(a3)
        forms1 = prepare([part1, a1, b1, q1], column[None], matrix)
        far1 = other_core(after(forms1, far0))

        q2, q3 = after((q2, q3), forms1)
        forms3 = prepare([part3, a3, b3, q3], column[None], matrix)
        far3 = other_core(after(forms3, far1))
        forms2 = prepare([part2, a2, b2, q2], column[None], matrix)
        far2 = other_core(after(forms2, far3))
        amps = prepare_amps(own, blocks_here, jnp.asarray(amp_matrix()))
        held = [forms0, far0, forms1, far1, forms2, far2, forms3, far3]
    else:
        parts = [mine[0]] + [around(mine[by], by) for by in range(1, levels)]
        tiles = amplitudes.reshape(blocks_here, pairs, TV, TV).transpose(0, 3, 2, 1)
        tiles = jnp.pad(tiles, ((0, 0), (0, 0), (0, PAD - TV), (0, 0))).reshape(blocks_here, ROWS, pairs)
        amps = lax.all_gather(tiles, "task", axis=0, tiled=True, axis_index_groups=same_core)
        held = lax.all_gather(jnp.stack(parts), "pair", axis=2, tiled=True)
        held = [jnp.stack([held, other_core(held)], axis=1).reshape(total, depth * pair_count, -1)]
    amps = (amps, other_core(amps))

    ladder = None
    calls = min(levels, 4)
    width = levels // calls
    order = [2, 3, 1, 0] if calls == 4 else list(reversed(range(calls)))
    for call in order:
        first = call * width
        sums = ladders(
            first, width, levels, blocks_here, column[None], task_owners, task_local, held, amps, back, matrix
        )
        for i in range(width):
            term = (around(sums[i], first + i) if first + i else sums[i]).astype(F32)
            ladder = term if ladder is None else ladder + term
    return residual_in + ladder.transpose(0, 2, 1)


def solution(mesh):
    placed = (P("task", "pair", None), P("task", "pair", None), P("task", "pair", None), P(), P())
    return jax.shard_map(
        per_device, mesh=mesh, in_specs=placed, out_specs=P("task", "pair", None), check_vma=False
    )
```

```python
import functools

import jax
import jax.numpy as jnp
import numpy as np
from jax import lax
from jax.experimental import pallas as pl
from jax.experimental.pallas import tpu as pltpu
from jax.sharding import PartitionSpec as P

TV = 25
PAD = 32
GROUP = 4
LANES = PAD * GROUP
GROUPS = -(-TV // GROUP)
ROWS = TV * PAD
WIDE = GROUPS * LANES
ORDER = [x for g in range(GROUP) for x in range(g, TV, GROUP)]
START = [ORDER.index(g) * PAD for g in range(GROUP)] + [ROWS]
PLACE = np.argsort(ORDER)
PREPARE_STEPS = 2
BF = jnp.bfloat16
F32 = jnp.float32
VMEM_BYTES = 48 * 1024 * 1024


def spread(spots, rows):
    return (np.arange(rows)[:, None] == spots[None, :]).astype(jnp.bfloat16)


def forms_matrix():
    x, y = np.divmod(np.arange(TV * TV), TV)
    return np.concatenate([spread(PLACE[y] * PAD + x, ROWS), spread(x * PAD + y, ROWS)], axis=0)


def amp_matrix():
    c, d = np.divmod(np.arange(TV * TV), TV)
    return spread(d * PAD + c, ROWS)


def back_matrix():
    a, b = np.divmod(np.arange(TV * TV), TV)
    return spread(PLACE[a] * PAD + b, ROWS).T


def prepare_kernel(column_ref, *refs):
    tile_refs, matrix_ref, forms_ref, all_ref = refs[:4], refs[4], refs[5], refs[6]
    count, size, _ = tile_refs[0].shape
    depth = forms_ref.shape[2]

    @pl.when(pl.program_id(0) == 0)
    def _():
        core = lax.rem(column_ref[0], 2)
        for m in range(count):
            for place, ref in zip((0, 1 + core, 2 - core, 3), tile_refs):
                start = pl.multiple_of(m * depth + place * size, size)
                all_ref[pl.ds(start, size), :] = ref[m]

    wide = 2 if depth % LANES == 0 and count % 2 == 0 else 1
    for first in range(0, count, wide):
        made = lax.dot_general(
            matrix_ref[...],
            all_ref[first * depth : (first + wide) * depth, :],
            (((1,), (1,)), ((), ())),
            preferred_element_type=F32,
        ).astype(BF)
        for m in range(wide):
            forms_ref[first + m] = made[:, m * depth : (m + 1) * depth]


def prepare(parts, column, matrix):
    count, size, width = parts[0].shape
    depth = size * len(parts)
    rows = matrix.shape[0] // PREPARE_STEPS
    in_specs = [pl.BlockSpec(part.shape, lambda i, column: (0, 0, 0)) for part in parts]
    in_specs.append(pl.BlockSpec((rows, width), lambda i, column: (i, 0)))
    return pl.pallas_call(
        prepare_kernel,
        out_shape=jax.ShapeDtypeStruct((count, matrix.shape[0], depth), BF),
        grid_spec=pltpu.PrefetchScalarGridSpec(
            num_scalar_prefetch=1,
            grid=(PREPARE_STEPS,),
            in_specs=in_specs,
            out_specs=pl.BlockSpec((count, rows, depth), lambda i, column: (0, i, 0)),
            scratch_shapes=[pltpu.VMEM((count * depth, width), BF)],
        ),
        compiler_params=pltpu.CompilerParams(vmem_limit_bytes=VMEM_BYTES),
        cost_estimate=pl.CostEstimate(
            flops=2 * count * depth * width * matrix.shape[0],
            bytes_accessed=2 * count * depth * (width + matrix.shape[0]),
            transcendentals=0,
        ),
    )(column, *parts, matrix)


def amp_kernel(matrix_ref, *refs):
    tile_refs, out_ref = refs[:-1], refs[-1]
    blocks_here, pairs = out_ref.shape[0] // len(tile_refs), out_ref.shape[2]
    for by, ref in enumerate(tile_refs):
        made = jnp.dot(matrix_ref[...], ref[...], preferred_element_type=F32).astype(BF)
        for m in range(blocks_here):
            out_ref[by * blocks_here + m] = made[:, m * pairs : (m + 1) * pairs]


def prepare_amps(parts, blocks_here, matrix):
    levels, size = len(parts), parts[0].size
    pairs = parts[0].shape[1] // blocks_here
    return pl.pallas_call(
        amp_kernel,
        out_shape=jax.ShapeDtypeStruct((levels * blocks_here, ROWS, pairs), BF),
        compiler_params=pltpu.CompilerParams(vmem_limit_bytes=VMEM_BYTES),
        cost_estimate=pl.CostEstimate(
            flops=2 * levels * size * ROWS, bytes_accessed=4 * levels * size, transcendentals=0
        ),
    )(matrix, *parts)


def turned(ref, groups, by):
    numbers = [min(A * GROUP + (p - by) % GROUP, TV - 1) for A in groups for p in range(GROUP)]
    return jnp.concatenate([ref[x * PAD : (x + 1) * PAD, :] for x in numbers], axis=0)


def ladder_kernel(find, made, sources, column_ref, owners_ref, local_ref, *refs):
    factor_refs, amp_refs, refs = refs[:sources], refs[sources : sources + 2], refs[sources + 2 :]
    back_ref, matrix_ref, refs = refs[0], None if made else refs[1], refs[1 if made else 2 :]
    out_ref, v_ref, u_ref, acc_ref, c_buf, r_buf, amp_buf, sems = refs[:8]
    column, columns = pl.program_id(0), pl.num_programs(0)
    step, steps = pl.program_id(1), pl.num_programs(1)
    at = column * steps + step
    slot = lax.rem(at, 2)

    def fetch(choices, source, index, part, buffer, to, sem):
        for n, ref in enumerate(choices):

            @pl.when(source == n)
            def _():
                tile = ref.at[index, pl.ds(part * ROWS, ROWS)] if part is not None else ref.at[index]
                pltpu.make_async_copy(tile, buffer.at[to], sem).start()

    def fetch_task(i, j, to):
        places = find(i, j, column_ref, owners_ref, local_ref)
        fetch(factor_refs, *places["col"], 0 if made else None, c_buf, to, sems.at[to, 0])
        fetch(factor_refs, *places["row"], 1 if made else None, r_buf, to, sems.at[to, 1])
        fetch(amp_refs, *places["amp"], None, amp_buf, to, sems.at[to, 2])

    @pl.when(at == 0)
    def _():
        fetch_task(0, 0, 0)

    @pl.when(at + 1 < columns * steps)
    def _():
        last = step == steps - 1
        fetch_task(jnp.where(last, column + 1, column), jnp.where(last, 0, step + 1), 1 - slot)

    @pl.when(step == 0)
    def _():
        acc_ref[...] = jnp.zeros_like(acc_ref)

    for n, buffer in enumerate((c_buf, r_buf, amp_buf)):
        pltpu.make_async_copy(buffer.at[slot], buffer.at[slot], sems.at[slot, n]).wait()
    c_form, r_form, amp_form = c_buf.at[slot], r_buf.at[slot], amp_buf.at[slot]
    if not made:
        forms = refs[8]
        for i, tile in enumerate((c_form, r_form)):
            forms[i] = lax.dot_general(
                matrix_ref[i * ROWS : (i + 1) * ROWS, :],
                tile[...],
                (((1,), (1,)), ((), ())),
                preferred_element_type=F32,
            ).astype(BF)
        c_form, r_form = forms.at[0], forms.at[1]

    spot = lax.broadcasted_iota(jnp.int32, (PAD, LANES), 1) // PAD
    at_spot = [spot == p for p in range(GROUP)]
    nothing = jnp.zeros((PAD, LANES), F32)
    for first in range(0, GROUPS, 2):
        groups = range(first, min(first + 2, GROUPS))
        lanes = slice(groups[0] * LANES, (groups[-1] + 1) * LANES)
        for g in range(GROUP):
            v_ref[START[g] : START[g + 1], lanes] = lax.dot_general(
                c_form[START[g] : START[g + 1], :],
                turned(r_form, groups, g),
                (((1,), (1,)), ((), ())),
                preferred_element_type=F32,
            )
        for A in groups:
            for D in range(GROUPS):
                blocks = [
                    v_ref[START[g] + D * PAD : START[g] + (D + 1) * PAD, A * LANES : (A + 1) * LANES]
                    if D * GROUP + g < TV
                    else nothing
                    for g in range(GROUP)
                ]
                for i in range(min(GROUP, TV - A * GROUP)):
                    block = blocks[-i % GROUP]
                    for p in range(1, GROUP):
                        block = jnp.where(at_spot[p], blocks[(p - i) % GROUP], block)
                    u_ref[START[i] + A * PAD : START[i] + (A + 1) * PAD, D * LANES : (D + 1) * LANES] = block.astype(BF)
    out = local_ref[find(column, step, column_ref, owners_ref, local_ref)["task"], 3]
    for i in range(GROUP):
        acc_ref[out, START[i] : START[i + 1], :] += jnp.dot(
            u_ref[START[i] : START[i + 1], :], turned(amp_form, range(GROUPS), i), preferred_element_type=F32
        )

    @pl.when(step == steps - 1)
    def _():
        blocks_here, pairs = out_ref.shape[1], out_ref.shape[3]
        sums = jnp.concatenate([acc_ref[m].astype(BF) for m in range(blocks_here)], axis=1)
        sums = jnp.dot(back_ref[...], sums, preferred_element_type=F32).astype(BF)
        for m in range(blocks_here):
            out_ref[0, m] = sums[:, m * pairs : (m + 1) * pairs]


def ladders(first, columns, levels, blocks_here, column, task_owners, task_local, tiles, amps, back, matrix):
    tasks = task_owners.shape[0] // (2 * levels)
    pairs = amps[0].shape[2]
    made = tiles[0].shape[1] == 2 * ROWS
    depth = tiles[0].shape[2] if made else tiles[0].shape[1]
    held = (ROWS, depth) if made else tiles[0].shape[1:]

    def find(i, j, column_ref, owners_ref, local_ref):
        level, core = column_ref[0] // 2, lax.rem(column_ref[0], 2)
        task = (2 * lax.rem(level + first + i, levels) + core) * tasks + j

        def place(kind):
            owner = owners_ref[task, kind]
            below = lax.rem(level - owner // 2 + levels, levels)
            far = jnp.where(lax.rem(owner, 2) != core, 1, 0)
            return below, far, local_ref[task, kind]

        def factor(kind):
            below, far, m = place(kind)
            if not made:
                return 0, (below * 2 + far) * blocks_here + m
            chunk = jnp.where(below == 3, 1, below)
            return chunk * 2 + far, m + jnp.where(below == 3, blocks_here, 0)

        below, far, m = place(2)
        return {"task": task, "row": factor(0), "col": factor(1), "amp": (far, below * blocks_here + m)}

    anywhere = pl.BlockSpec(memory_space=pl.ANY)
    fixed = lambda shape: pl.BlockSpec(shape, lambda i, j, *tables: (0,) * len(shape))
    operands = [*tiles, *amps, back]
    in_specs = [anywhere] * (len(tiles) + 2) + [fixed(back.shape)]
    scratch = [
        pltpu.VMEM((ROWS, WIDE), F32),
        pltpu.VMEM((ROWS, WIDE), BF),
        pltpu.VMEM((blocks_here, ROWS, pairs), F32),
        pltpu.VMEM((2, *held), BF),
        pltpu.VMEM((2, *held), BF),
        pltpu.VMEM((2, ROWS, pairs), BF),
        pltpu.SemaphoreType.DMA((2, 3)),
    ]
    if not made:
        in_specs.append(fixed(matrix.shape))
        scratch.append(pltpu.VMEM((2, ROWS, depth), BF))
        operands.append(matrix)
    return pl.pallas_call(
        functools.partial(ladder_kernel, find, made, len(tiles)),
        out_shape=jax.ShapeDtypeStruct((columns, blocks_here, TV * TV, pairs), BF),
        grid_spec=pltpu.PrefetchScalarGridSpec(
            num_scalar_prefetch=3,
            grid=(columns, tasks),
            in_specs=in_specs,
            out_specs=pl.BlockSpec((1, blocks_here, TV * TV, pairs), lambda i, j, *tables: (i, 0, 0, 0)),
            scratch_shapes=scratch,
        ),
        compiler_params=pltpu.CompilerParams(vmem_limit_bytes=VMEM_BYTES),
        cost_estimate=pl.CostEstimate(
            flops=2 * columns * tasks * ROWS * WIDE * (depth + pairs),
            bytes_accessed=2 * columns * tasks * ROWS * 2 * (depth + pairs),
            transcendentals=0,
        ),
    )(column, task_owners, task_local, *operands)


def after(values, done):
    return lax.optimization_barrier((values, done))[0]


def per_device(factor_blocks, amplitudes, residual_in, task_owners, task_local):
    pair_count = lax.axis_size("pair")
    task_count = lax.axis_size("task")
    column = lax.axis_index("task")
    blocks_here, depth_here, _ = factor_blocks.shape
    pairs = amplitudes.shape[1]
    levels = task_count // 2
    level = column // 2
    depth = depth_here // levels
    total = 2 * levels * blocks_here
    matrix = jnp.asarray(forms_matrix())
    back = jnp.asarray(back_matrix())
    other_core = lambda x: lax.ppermute(x, "task", [(c, c ^ 1) for c in range(task_count)])

    def around(x, by):
        return lax.ppermute(x, "task", [(c, (c + 2 * by) % task_count) for c in range(task_count)])

    same_core = [[2 * z + k for z in range(levels)] for k in range(2)]
    slices = factor_blocks.reshape(blocks_here, levels, depth, -1)
    mine = [lax.dynamic_index_in_dim(slices, (level + by) % levels, 1, keepdims=False) for by in range(levels)]
    if pair_count == 4 and levels == 4:
        sides = [
            [(p * task_count + c, (p ^ (1 if c % 2 == turn else 2)) * task_count + c) for p in range(4) for c in range(task_count)]
            for turn in range(2)
        ]
        first_side = lambda x: lax.ppermute(x, ("pair", "task"), sides[0])
        second_side = lambda x: lax.ppermute(x, ("pair", "task"), sides[1])
        made_forms = lambda *parts: prepare(parts, column[None], matrix)
        part0 = mine[0]
        a0, b0, part1, part3 = first_side(part0), second_side(part0), around(mine[1], 1), around(mine[3], 3)

        a0, b0, part0, part1, part3, to2 = after((a0, b0, part0, part1, part3, mine[2]), ())
        part13 = jnp.concatenate([part1, part3], axis=0)
        q0, a13, b13, part2 = second_side(a0), first_side(part13), second_side(part13), around(to2, 2)

        own = amplitudes.transpose(2, 0, 1).reshape(TV * TV, blocks_here * pairs)
        own, q0, a13, b13, part2, part13 = after((own, q0, a13, b13, part2, part13), ())
        q13, a2, b2, amp1 = second_side(a13), first_side(part2), second_side(part2), around(own, 1)
        forms0 = made_forms(part0, a0, b0, q0)
        far0 = other_core(forms0)

        q13, a2, b2, amp1 = after((q13, a2, b2, amp1), forms0)
        q2, amp2 = second_side(a2), around(amp1, 1)
        forms13 = made_forms(part13, a13, b13, q13)
        far13 = other_core(after(forms13, far0))

        q2, amp2 = after((q2, amp2), forms13)
        amp3 = around(amp2, 1)
        forms2 = made_forms(part2, a2, b2, q2)
        far2 = other_core(after(forms2, far13))
        amps = prepare_amps([own, amp1, amp2, after(amp3, forms2)], blocks_here, jnp.asarray(amp_matrix()))
        held = [forms0, far0, forms13, far13, forms2, far2]
    else:
        parts = [mine[0]] + [around(mine[by], by) for by in range(1, levels)]
        tiles = amplitudes.reshape(blocks_here, pairs, TV, TV).transpose(0, 3, 2, 1)
        tiles = jnp.pad(tiles, ((0, 0), (0, 0), (0, PAD - TV), (0, 0))).reshape(blocks_here, ROWS, pairs)
        amps = lax.all_gather(tiles, "task", axis=0, axis_index_groups=same_core)
        amps = amps[(level - jnp.arange(levels)) % levels].reshape(levels * blocks_here, ROWS, pairs)
        held = lax.all_gather(jnp.stack(parts), "pair", axis=2, tiled=True)
        held = [jnp.stack([held, other_core(held)], axis=1).reshape(total, depth * pair_count, -1)]
    amps = (amps, other_core(amps))

    ladder = None
    calls = min(levels, 4)
    width = levels // calls
    order = [2, 3, 1, 0] if calls == 4 else list(reversed(range(calls)))
    for call in order:
        first = call * width
        sums = ladders(
            first, width, levels, blocks_here, column[None], task_owners, task_local, held, amps, back, matrix
        )
        for i in range(width):
            term = (around(sums[i], first + i) if first + i else sums[i]).astype(F32)
            ladder = term if ladder is None else ladder + term
    return residual_in + ladder.transpose(0, 2, 1)


def solution(mesh):
    placed = (P("task", "pair", None), P("task", "pair", None), P("task", "pair", None), P(), P())
    return jax.shard_map(
        per_device, mesh=mesh, in_specs=placed, out_specs=P("task", "pair", None), check_vma=False
    )
```

```python
import functools

import jax
import jax.numpy as jnp
import numpy as np
from jax import lax
from jax.experimental import pallas as pl
from jax.experimental.pallas import tpu as pltpu
from jax.sharding import PartitionSpec as P

TV = 25
PAD = 32
GROUP = 4
LANES = PAD * GROUP
GROUPS = -(-TV // GROUP)
ROWS = TV * PAD
WIDE = GROUPS * LANES
ORDER = [x for g in range(GROUP) for x in range(g, TV, GROUP)]
START = [ORDER.index(g) * PAD for g in range(GROUP)] + [ROWS]
PLACE = np.argsort(ORDER)
PREPARE_STEPS = 2
BF = jnp.bfloat16
F32 = jnp.float32
VMEM_BYTES = 48 * 1024 * 1024


def spread(spots, rows):
    return (np.arange(rows)[:, None] == spots[None, :]).astype(jnp.bfloat16)


def forms_matrix():
    x, y = np.divmod(np.arange(TV * TV), TV)
    return np.concatenate([spread(PLACE[y] * PAD + x, ROWS), spread(x * PAD + y, ROWS)], axis=0)


def amp_matrix():
    c, d = np.divmod(np.arange(TV * TV), TV)
    return spread(d * PAD + c, ROWS)


def back_matrix():
    a, b = np.divmod(np.arange(TV * TV), TV)
    return spread(PLACE[a] * PAD + b, ROWS).T


def prepare_kernel(column_ref, *refs):
    tile_refs, matrix_ref, forms_ref, all_ref = refs[:4], refs[4], refs[5], refs[6]
    count, size, _ = tile_refs[0].shape
    depth = forms_ref.shape[2]

    @pl.when(pl.program_id(0) == 0)
    def _():
        core = lax.rem(column_ref[0], 2)
        for m in range(count):
            for place, ref in zip((0, 1 + core, 2 - core, 3), tile_refs):
                start = pl.multiple_of(m * depth + place * size, size)
                all_ref[pl.ds(start, size), :] = ref[m]

    wide = 2 if depth % LANES == 0 and count % 2 == 0 else 1
    for first in range(0, count, wide):
        made = lax.dot_general(
            matrix_ref[...],
            all_ref[first * depth : (first + wide) * depth, :],
            (((1,), (1,)), ((), ())),
            preferred_element_type=F32,
        ).astype(BF)
        for m in range(wide):
            forms_ref[first + m] = made[:, m * depth : (m + 1) * depth]


def prepare(parts, column, matrix):
    count, size, width = parts[0].shape
    depth = size * len(parts)
    rows = matrix.shape[0] // PREPARE_STEPS
    in_specs = [pl.BlockSpec(part.shape, lambda i, column: (0, 0, 0)) for part in parts]
    in_specs.append(pl.BlockSpec((rows, width), lambda i, column: (i, 0)))
    return pl.pallas_call(
        prepare_kernel,
        out_shape=jax.ShapeDtypeStruct((count, matrix.shape[0], depth), BF),
        grid_spec=pltpu.PrefetchScalarGridSpec(
            num_scalar_prefetch=1,
            grid=(PREPARE_STEPS,),
            in_specs=in_specs,
            out_specs=pl.BlockSpec((count, rows, depth), lambda i, column: (0, i, 0)),
            scratch_shapes=[pltpu.VMEM((count * depth, width), BF)],
        ),
        compiler_params=pltpu.CompilerParams(vmem_limit_bytes=VMEM_BYTES),
        cost_estimate=pl.CostEstimate(
            flops=2 * count * depth * width * matrix.shape[0],
            bytes_accessed=2 * count * depth * (width + matrix.shape[0]),
            transcendentals=0,
        ),
    )(column, *parts, matrix)


def amp_kernel(matrix_ref, *refs):
    tile_refs, out_ref = refs[:-1], refs[-1]
    blocks_here, pairs = out_ref.shape[0] // len(tile_refs), out_ref.shape[2]
    for by, ref in enumerate(tile_refs):
        made = jnp.dot(matrix_ref[...], ref[...], preferred_element_type=F32).astype(BF)
        for m in range(blocks_here):
            out_ref[by * blocks_here + m] = made[:, m * pairs : (m + 1) * pairs]


def prepare_amps(parts, blocks_here, matrix):
    levels, size = len(parts), parts[0].size
    pairs = parts[0].shape[1] // blocks_here
    return pl.pallas_call(
        amp_kernel,
        out_shape=jax.ShapeDtypeStruct((levels * blocks_here, ROWS, pairs), BF),
        compiler_params=pltpu.CompilerParams(vmem_limit_bytes=VMEM_BYTES),
        cost_estimate=pl.CostEstimate(
            flops=2 * levels * size * ROWS, bytes_accessed=4 * levels * size, transcendentals=0
        ),
    )(matrix, *parts)


def turned(ref, groups, by):
    numbers = [min(A * GROUP + (p - by) % GROUP, TV - 1) for A in groups for p in range(GROUP)]
    return jnp.concatenate([ref[x * PAD : (x + 1) * PAD, :] for x in numbers], axis=0)


def ladder_kernel(find, made, sources, column_ref, owners_ref, local_ref, *refs):
    factor_refs, amp_refs, refs = refs[:sources], refs[sources : sources + 2], refs[sources + 2 :]
    back_ref, matrix_ref, refs = refs[0], None if made else refs[1], refs[1 if made else 2 :]
    out_ref, v_ref, u_ref, acc_ref, c_buf, r_buf, amp_buf, sems = refs[:8]
    column, columns = pl.program_id(0), pl.num_programs(0)
    step, steps = pl.program_id(1), pl.num_programs(1)
    at = column * steps + step
    slot = lax.rem(at, 2)

    def fetch(choices, source, index, part, buffer, to, sem):
        for n, ref in enumerate(choices):

            @pl.when(source == n)
            def _():
                tile = ref.at[index, pl.ds(part * ROWS, ROWS)] if part is not None else ref.at[index]
                pltpu.make_async_copy(tile, buffer.at[to], sem).start()

    def fetch_task(i, j, to):
        places = find(i, j, column_ref, owners_ref, local_ref)
        fetch(factor_refs, *places["col"], 0 if made else None, c_buf, to, sems.at[to, 0])
        fetch(factor_refs, *places["row"], 1 if made else None, r_buf, to, sems.at[to, 1])
        fetch(amp_refs, *places["amp"], None, amp_buf, to, sems.at[to, 2])

    @pl.when(at == 0)
    def _():
        fetch_task(0, 0, 0)

    @pl.when(at + 1 < columns * steps)
    def _():
        last = step == steps - 1
        fetch_task(jnp.where(last, column + 1, column), jnp.where(last, 0, step + 1), 1 - slot)

    @pl.when(step == 0)
    def _():
        acc_ref[...] = jnp.zeros_like(acc_ref)

    for n, buffer in enumerate((c_buf, r_buf, amp_buf)):
        pltpu.make_async_copy(buffer.at[slot], buffer.at[slot], sems.at[slot, n]).wait()
    c_form, r_form, amp_form = c_buf.at[slot], r_buf.at[slot], amp_buf.at[slot]
    if not made:
        forms = refs[8]
        for i, tile in enumerate((c_form, r_form)):
            forms[i] = lax.dot_general(
                matrix_ref[i * ROWS : (i + 1) * ROWS, :],
                tile[...],
                (((1,), (1,)), ((), ())),
                preferred_element_type=F32,
            ).astype(BF)
        c_form, r_form = forms.at[0], forms.at[1]

    spot = lax.broadcasted_iota(jnp.int32, (PAD, LANES), 1) // PAD
    at_spot = [spot == p for p in range(GROUP)]
    nothing = jnp.zeros((PAD, LANES), F32)
    for first in range(0, GROUPS, 2):
        groups = range(first, min(first + 2, GROUPS))
        lanes = slice(groups[0] * LANES, (groups[-1] + 1) * LANES)
        for g in range(GROUP):
            v_ref[START[g] : START[g + 1], lanes] = lax.dot_general(
                c_form[START[g] : START[g + 1], :],
                turned(r_form, groups, g),
                (((1,), (1,)), ((), ())),
                preferred_element_type=F32,
            )
        for A in groups:
            for D in range(GROUPS):
                blocks = [
                    v_ref[START[g] + D * PAD : START[g] + (D + 1) * PAD, A * LANES : (A + 1) * LANES]
                    if D * GROUP + g < TV
                    else nothing
                    for g in range(GROUP)
                ]
                for i in range(min(GROUP, TV - A * GROUP)):
                    block = blocks[-i % GROUP]
                    for p in range(1, GROUP):
                        block = jnp.where(at_spot[p], blocks[(p - i) % GROUP], block)
                    u_ref[START[i] + A * PAD : START[i] + (A + 1) * PAD, D * LANES : (D + 1) * LANES] = block.astype(BF)
    out = local_ref[find(column, step, column_ref, owners_ref, local_ref)["task"], 3]
    for i in range(GROUP):
        acc_ref[out, START[i] : START[i + 1], :] += jnp.dot(
            u_ref[START[i] : START[i + 1], :], turned(amp_form, range(GROUPS), i), preferred_element_type=F32
        )

    @pl.when(step == steps - 1)
    def _():
        blocks_here, pairs = out_ref.shape[1], out_ref.shape[3]
        sums = jnp.concatenate([acc_ref[m].astype(BF) for m in range(blocks_here)], axis=1)
        sums = jnp.dot(back_ref[...], sums, preferred_element_type=F32).astype(BF)
        for m in range(blocks_here):
            out_ref[0, m] = sums[:, m * pairs : (m + 1) * pairs]


def ladders(first, columns, levels, blocks_here, column, task_owners, task_local, tiles, amps, back, matrix):
    tasks = task_owners.shape[0] // (2 * levels)
    pairs = amps[0].shape[2]
    made = tiles[0].shape[1] == 2 * ROWS
    depth = tiles[0].shape[2] if made else tiles[0].shape[1]
    held = (ROWS, depth) if made else tiles[0].shape[1:]

    def find(i, j, column_ref, owners_ref, local_ref):
        level, core = column_ref[0] // 2, lax.rem(column_ref[0], 2)
        task = (2 * lax.rem(level + first + i, levels) + core) * tasks + j

        def place(kind):
            owner = owners_ref[task, kind]
            below = lax.rem(level - owner // 2 + levels, levels)
            far = jnp.where(lax.rem(owner, 2) != core, 1, 0)
            return below, far, local_ref[task, kind]

        def factor(kind):
            below, far, m = place(kind)
            if not made:
                return 0, (below * 2 + far) * blocks_here + m
            chunk = jnp.where(below == 3, 1, below)
            return chunk * 2 + far, m + jnp.where(below == 3, blocks_here, 0)

        below, far, m = place(2)
        return {"task": task, "row": factor(0), "col": factor(1), "amp": (far, below * blocks_here + m)}

    anywhere = pl.BlockSpec(memory_space=pl.ANY)
    fixed = lambda shape: pl.BlockSpec(shape, lambda i, j, *tables: (0,) * len(shape))
    operands = [*tiles, *amps, back]
    in_specs = [anywhere] * (len(tiles) + 2) + [fixed(back.shape)]
    scratch = [
        pltpu.VMEM((ROWS, WIDE), F32),
        pltpu.VMEM((ROWS, WIDE), BF),
        pltpu.VMEM((blocks_here, ROWS, pairs), F32),
        pltpu.VMEM((2, *held), BF),
        pltpu.VMEM((2, *held), BF),
        pltpu.VMEM((2, ROWS, pairs), BF),
        pltpu.SemaphoreType.DMA((2, 3)),
    ]
    if not made:
        in_specs.append(fixed(matrix.shape))
        scratch.append(pltpu.VMEM((2, ROWS, depth), BF))
        operands.append(matrix)
    return pl.pallas_call(
        functools.partial(ladder_kernel, find, made, len(tiles)),
        out_shape=jax.ShapeDtypeStruct((columns, blocks_here, TV * TV, pairs), BF),
        grid_spec=pltpu.PrefetchScalarGridSpec(
            num_scalar_prefetch=3,
            grid=(columns, tasks),
            in_specs=in_specs,
            out_specs=pl.BlockSpec((1, blocks_here, TV * TV, pairs), lambda i, j, *tables: (i, 0, 0, 0)),
            scratch_shapes=scratch,
        ),
        compiler_params=pltpu.CompilerParams(vmem_limit_bytes=VMEM_BYTES),
        cost_estimate=pl.CostEstimate(
            flops=2 * columns * tasks * ROWS * WIDE * (depth + pairs),
            bytes_accessed=2 * columns * tasks * ROWS * 2 * (depth + pairs),
            transcendentals=0,
        ),
    )(column, task_owners, task_local, *operands)


def after(values, done):
    return lax.optimization_barrier((values, done))[0]


def per_device(factor_blocks, amplitudes, residual_in, task_owners, task_local):
    pair_count = lax.axis_size("pair")
    task_count = lax.axis_size("task")
    column = lax.axis_index("task")
    blocks_here, depth_here, _ = factor_blocks.shape
    pairs = amplitudes.shape[1]
    levels = task_count // 2
    level = column // 2
    depth = depth_here // levels
    total = 2 * levels * blocks_here
    matrix = jnp.asarray(forms_matrix())
    back = jnp.asarray(back_matrix())
    other_core = lambda x: lax.ppermute(x, "task", [(c, c ^ 1) for c in range(task_count)])

    def around(x, by):
        return lax.ppermute(x, "task", [(c, (c + 2 * by) % task_count) for c in range(task_count)])

    same_core = [[2 * z + k for z in range(levels)] for k in range(2)]
    slices = factor_blocks.reshape(blocks_here, levels, depth, -1)
    mine = [lax.dynamic_index_in_dim(slices, (level + by) % levels, 1, keepdims=False) for by in range(levels)]
    if pair_count == 4 and levels == 4:
        sides = [
            [(p * task_count + c, (p ^ (1 if c % 2 == turn else 2)) * task_count + c) for p in range(4) for c in range(task_count)]
            for turn in range(2)
        ]
        first_side = lambda x: lax.ppermute(x, ("pair", "task"), sides[0])
        second_side = lambda x: lax.ppermute(x, ("pair", "task"), sides[1])
        made_forms = lambda *parts: prepare(parts, column[None], matrix)
        own = amplitudes.transpose(2, 0, 1).reshape(TV * TV, blocks_here * pairs)
        amp1 = around(own, 1)
        part0 = mine[0]
        a0, b0, part1, part3 = first_side(part0), second_side(part0), around(mine[1], 1), around(mine[3], 3)

        a0, b0, part0, part1, part3, amp1, to2 = after((a0, b0, part0, part1, part3, amp1, mine[2]), ())
        part13 = jnp.concatenate([part1, part3], axis=0)
        q0, a13, b13, part2 = second_side(a0), first_side(part13), second_side(part13), around(to2, 2)

        own, q0, a13, b13, part2, part13 = after((own, q0, a13, b13, part2, part13), ())
        q13, a2, b2, amp2 = second_side(a13), first_side(part2), second_side(part2), around(own, 2)
        forms0 = made_forms(part0, a0, b0, q0)
        far0 = other_core(forms0)

        q13, a2, b2, own, amp2 = after((q13, a2, b2, own, amp2), forms0)
        q2, amp3 = second_side(a2), around(own, 3)
        forms13 = made_forms(part13, a13, b13, q13)
        far13 = other_core(after(forms13, far0))

        q2 = after(q2, forms13)
        forms2 = made_forms(part2, a2, b2, q2)
        far2 = other_core(after(forms2, far13))
        amps = prepare_amps([own, amp1, amp2, after(amp3, forms2)], blocks_here, jnp.asarray(amp_matrix()))
        held = [forms0, far0, forms13, far13, forms2, far2]
    else:
        parts = [mine[0]] + [around(mine[by], by) for by in range(1, levels)]
        tiles = amplitudes.reshape(blocks_here, pairs, TV, TV).transpose(0, 3, 2, 1)
        tiles = jnp.pad(tiles, ((0, 0), (0, 0), (0, PAD - TV), (0, 0))).reshape(blocks_here, ROWS, pairs)
        amps = lax.all_gather(tiles, "task", axis=0, axis_index_groups=same_core)
        amps = amps[(level - jnp.arange(levels)) % levels].reshape(levels * blocks_here, ROWS, pairs)
        held = lax.all_gather(jnp.stack(parts), "pair", axis=2, tiled=True)
        held = [jnp.stack([held, other_core(held)], axis=1).reshape(total, depth * pair_count, -1)]
    amps = (amps, other_core(amps))

    ladder = None
    calls = min(levels, 4)
    width = levels // calls
    order = [2, 3, 1, 0] if calls == 4 else list(reversed(range(calls)))
    for call in order:
        first = call * width
        sums = ladders(
            first, width, levels, blocks_here, column[None], task_owners, task_local, held, amps, back, matrix
        )
        for i in range(width):
            term = (around(sums[i], first + i) if first + i else sums[i]).astype(F32)
            ladder = term if ladder is None else ladder + term
    return residual_in + ladder.transpose(0, 2, 1)


def solution(mesh):
    placed = (P("task", "pair", None), P("task", "pair", None), P("task", "pair", None), P(), P())
    return jax.shard_map(
        per_device, mesh=mesh, in_specs=placed, out_specs=P("task", "pair", None), check_vma=False
    )
```

```python
import functools

import jax
import jax.numpy as jnp
import numpy as np
from jax import lax
from jax.experimental import pallas as pl
from jax.experimental.pallas import tpu as pltpu
from jax.sharding import PartitionSpec as P

TV = 25
PAD = 32
GROUP = 4
LANES = PAD * GROUP
GROUPS = -(-TV // GROUP)
ROWS = TV * PAD
WIDE = GROUPS * LANES
ORDER = [x for g in range(GROUP) for x in range(g, TV, GROUP)]
START = [ORDER.index(g) * PAD for g in range(GROUP)] + [ROWS]
PLACE = np.argsort(ORDER)
PREPARE_STEPS = 2
BF = jnp.bfloat16
F32 = jnp.float32
VMEM_BYTES = 48 * 1024 * 1024


def spread(spots, rows):
    return (np.arange(rows)[:, None] == spots[None, :]).astype(jnp.bfloat16)


def forms_matrix():
    x, y = np.divmod(np.arange(TV * TV), TV)
    return np.concatenate([spread(PLACE[y] * PAD + x, ROWS), spread(x * PAD + y, ROWS)], axis=0)


def amp_matrix():
    c, d = np.divmod(np.arange(TV * TV), TV)
    return spread(d * PAD + c, ROWS)


def back_matrix():
    a, b = np.divmod(np.arange(TV * TV), TV)
    return spread(PLACE[a] * PAD + b, ROWS).T


def prepare_kernel(column_ref, *refs):
    tile_refs, matrix_ref, forms_ref, all_ref = refs[:4], refs[4], refs[5], refs[6]
    count, size, _ = tile_refs[0].shape
    depth = forms_ref.shape[2]

    @pl.when(pl.program_id(0) == 0)
    def _():
        core = lax.rem(column_ref[0], 2)
        for m in range(count):
            for place, ref in zip((0, 1 + core, 2 - core, 3), tile_refs):
                start = pl.multiple_of(m * depth + place * size, size)
                all_ref[pl.ds(start, size), :] = ref[m]

    wide = 2 if depth % LANES == 0 and count % 2 == 0 else 1
    for first in range(0, count, wide):
        made = lax.dot_general(
            matrix_ref[...],
            all_ref[first * depth : (first + wide) * depth, :],
            (((1,), (1,)), ((), ())),
            preferred_element_type=F32,
        ).astype(BF)
        for m in range(wide):
            forms_ref[first + m] = made[:, m * depth : (m + 1) * depth]


def prepare(parts, column, matrix):
    count, size, width = parts[0].shape
    depth = size * len(parts)
    rows = matrix.shape[0] // PREPARE_STEPS
    in_specs = [pl.BlockSpec(part.shape, lambda i, column: (0, 0, 0)) for part in parts]
    in_specs.append(pl.BlockSpec((rows, width), lambda i, column: (i, 0)))
    return pl.pallas_call(
        prepare_kernel,
        out_shape=jax.ShapeDtypeStruct((count, matrix.shape[0], depth), BF),
        grid_spec=pltpu.PrefetchScalarGridSpec(
            num_scalar_prefetch=1,
            grid=(PREPARE_STEPS,),
            in_specs=in_specs,
            out_specs=pl.BlockSpec((count, rows, depth), lambda i, column: (0, i, 0)),
            scratch_shapes=[pltpu.VMEM((count * depth, width), BF)],
        ),
        compiler_params=pltpu.CompilerParams(vmem_limit_bytes=VMEM_BYTES),
        cost_estimate=pl.CostEstimate(
            flops=2 * count * depth * width * matrix.shape[0],
            bytes_accessed=2 * count * depth * (width + matrix.shape[0]),
            transcendentals=0,
        ),
    )(column, *parts, matrix)


def amp_kernel(matrix_ref, *refs):
    tile_refs, out_ref = refs[:-1], refs[-1]
    blocks_here, pairs = out_ref.shape[0] // len(tile_refs), out_ref.shape[2]
    for by, ref in enumerate(tile_refs):
        made = jnp.dot(matrix_ref[...], ref[...], preferred_element_type=F32).astype(BF)
        for m in range(blocks_here):
            out_ref[by * blocks_here + m] = made[:, m * pairs : (m + 1) * pairs]


def prepare_amps(parts, blocks_here, matrix):
    levels, size = len(parts), parts[0].size
    pairs = parts[0].shape[1] // blocks_here
    return pl.pallas_call(
        amp_kernel,
        out_shape=jax.ShapeDtypeStruct((levels * blocks_here, ROWS, pairs), BF),
        compiler_params=pltpu.CompilerParams(vmem_limit_bytes=VMEM_BYTES),
        cost_estimate=pl.CostEstimate(
            flops=2 * levels * size * ROWS, bytes_accessed=4 * levels * size, transcendentals=0
        ),
    )(matrix, *parts)


def turned(ref, groups, by):
    numbers = [min(A * GROUP + (p - by) % GROUP, TV - 1) for A in groups for p in range(GROUP)]
    return jnp.concatenate([ref[x * PAD : (x + 1) * PAD, :] for x in numbers], axis=0)


def ladder_kernel(find, made, sources, column_ref, owners_ref, local_ref, *refs):
    factor_refs, amp_refs, refs = refs[:sources], refs[sources : sources + 2], refs[sources + 2 :]
    back_ref, matrix_ref, refs = refs[0], None if made else refs[1], refs[1 if made else 2 :]
    out_ref, v_ref, u_ref, acc_ref, c_buf, r_buf, amp_buf, sems = refs[:8]
    column, columns = pl.program_id(0), pl.num_programs(0)
    step, steps = pl.program_id(1), pl.num_programs(1)
    at = column * steps + step
    slot = lax.rem(at, 2)

    def fetch(choices, source, index, part, buffer, to, sem):
        for n, ref in enumerate(choices):

            @pl.when(source == n)
            def _():
                tile = ref.at[index, pl.ds(part * ROWS, ROWS)] if part is not None else ref.at[index]
                pltpu.make_async_copy(tile, buffer.at[to], sem).start()

    def fetch_task(i, j, to):
        places = find(i, j, column_ref, owners_ref, local_ref)
        fetch(factor_refs, *places["col"], 0 if made else None, c_buf, to, sems.at[to, 0])
        fetch(factor_refs, *places["row"], 1 if made else None, r_buf, to, sems.at[to, 1])
        fetch(amp_refs, *places["amp"], None, amp_buf, to, sems.at[to, 2])

    @pl.when(at == 0)
    def _():
        fetch_task(0, 0, 0)

    @pl.when(at + 1 < columns * steps)
    def _():
        last = step == steps - 1
        fetch_task(jnp.where(last, column + 1, column), jnp.where(last, 0, step + 1), 1 - slot)

    @pl.when(step == 0)
    def _():
        acc_ref[...] = jnp.zeros_like(acc_ref)

    for n, buffer in enumerate((c_buf, r_buf, amp_buf)):
        pltpu.make_async_copy(buffer.at[slot], buffer.at[slot], sems.at[slot, n]).wait()
    c_form, r_form, amp_form = c_buf.at[slot], r_buf.at[slot], amp_buf.at[slot]
    if not made:
        forms = refs[8]
        for i, tile in enumerate((c_form, r_form)):
            forms[i] = lax.dot_general(
                matrix_ref[i * ROWS : (i + 1) * ROWS, :],
                tile[...],
                (((1,), (1,)), ((), ())),
                preferred_element_type=F32,
            ).astype(BF)
        c_form, r_form = forms.at[0], forms.at[1]

    spot = lax.broadcasted_iota(jnp.int32, (PAD, LANES), 1) // PAD
    at_spot = [spot == p for p in range(GROUP)]
    nothing = jnp.zeros((PAD, LANES), F32)
    for first in range(0, GROUPS, 2):
        groups = range(first, min(first + 2, GROUPS))
        lanes = slice(groups[0] * LANES, (groups[-1] + 1) * LANES)
        for g in range(GROUP):
            v_ref[START[g] : START[g + 1], lanes] = lax.dot_general(
                c_form[START[g] : START[g + 1], :],
                turned(r_form, groups, g),
                (((1,), (1,)), ((), ())),
                preferred_element_type=F32,
            )
        for A in groups:
            for D in range(GROUPS):
                blocks = [
                    v_ref[START[g] + D * PAD : START[g] + (D + 1) * PAD, A * LANES : (A + 1) * LANES]
                    if D * GROUP + g < TV
                    else nothing
                    for g in range(GROUP)
                ]
                for i in range(min(GROUP, TV - A * GROUP)):
                    block = blocks[-i % GROUP]
                    for p in range(1, GROUP):
                        block = jnp.where(at_spot[p], blocks[(p - i) % GROUP], block)
                    u_ref[START[i] + A * PAD : START[i] + (A + 1) * PAD, D * LANES : (D + 1) * LANES] = block.astype(BF)
    out = local_ref[find(column, step, column_ref, owners_ref, local_ref)["task"], 3]
    for i in range(GROUP):
        acc_ref[out, START[i] : START[i + 1], :] += jnp.dot(
            u_ref[START[i] : START[i + 1], :], turned(amp_form, range(GROUPS), i), preferred_element_type=F32
        )

    @pl.when(step == steps - 1)
    def _():
        blocks_here, pairs = out_ref.shape[1], out_ref.shape[3]
        sums = jnp.concatenate([acc_ref[m].astype(BF) for m in range(blocks_here)], axis=1)
        sums = jnp.dot(back_ref[...], sums, preferred_element_type=F32).astype(BF)
        for m in range(blocks_here):
            out_ref[0, m] = sums[:, m * pairs : (m + 1) * pairs]


def ladders(first, columns, levels, blocks_here, column, task_owners, task_local, tiles, amps, back, matrix):
    tasks = task_owners.shape[0] // (2 * levels)
    pairs = amps[0].shape[2]
    made = tiles[0].shape[1] == 2 * ROWS
    depth = tiles[0].shape[2] if made else tiles[0].shape[1]
    held = (ROWS, depth) if made else tiles[0].shape[1:]

    def find(i, j, column_ref, owners_ref, local_ref):
        level, core = column_ref[0] // 2, lax.rem(column_ref[0], 2)
        task = (2 * lax.rem(level + first + i, levels) + core) * tasks + j

        def place(kind):
            owner = owners_ref[task, kind]
            below = lax.rem(level - owner // 2 + levels, levels)
            far = jnp.where(lax.rem(owner, 2) != core, 1, 0)
            return below, far, local_ref[task, kind]

        def factor(kind):
            below, far, m = place(kind)
            if not made:
                return 0, (below * 2 + far) * blocks_here + m
            chunk = jnp.where(below == 3, 1, below)
            return chunk * 2 + far, m + jnp.where(below == 3, blocks_here, 0)

        below, far, m = place(2)
        return {"task": task, "row": factor(0), "col": factor(1), "amp": (far, below * blocks_here + m)}

    anywhere = pl.BlockSpec(memory_space=pl.ANY)
    fixed = lambda shape: pl.BlockSpec(shape, lambda i, j, *tables: (0,) * len(shape))
    operands = [*tiles, *amps, back]
    in_specs = [anywhere] * (len(tiles) + 2) + [fixed(back.shape)]
    scratch = [
        pltpu.VMEM((ROWS, WIDE), F32),
        pltpu.VMEM((ROWS, WIDE), BF),
        pltpu.VMEM((blocks_here, ROWS, pairs), F32),
        pltpu.VMEM((2, *held), BF),
        pltpu.VMEM((2, *held), BF),
        pltpu.VMEM((2, ROWS, pairs), BF),
        pltpu.SemaphoreType.DMA((2, 3)),
    ]
    if not made:
        in_specs.append(fixed(matrix.shape))
        scratch.append(pltpu.VMEM((2, ROWS, depth), BF))
        operands.append(matrix)
    return pl.pallas_call(
        functools.partial(ladder_kernel, find, made, len(tiles)),
        out_shape=jax.ShapeDtypeStruct((columns, blocks_here, TV * TV, pairs), BF),
        grid_spec=pltpu.PrefetchScalarGridSpec(
            num_scalar_prefetch=3,
            grid=(columns, tasks),
            in_specs=in_specs,
            out_specs=pl.BlockSpec((1, blocks_here, TV * TV, pairs), lambda i, j, *tables: (i, 0, 0, 0)),
            scratch_shapes=scratch,
        ),
        compiler_params=pltpu.CompilerParams(vmem_limit_bytes=VMEM_BYTES),
        cost_estimate=pl.CostEstimate(
            flops=2 * columns * tasks * ROWS * WIDE * (depth + pairs),
            bytes_accessed=2 * columns * tasks * ROWS * 2 * (depth + pairs),
            transcendentals=0,
        ),
    )(column, task_owners, task_local, *operands)


def after(values, done):
    return lax.optimization_barrier((values, done))[0]


def per_device(factor_blocks, amplitudes, residual_in, task_owners, task_local):
    pair_count = lax.axis_size("pair")
    task_count = lax.axis_size("task")
    column = lax.axis_index("task")
    blocks_here, depth_here, _ = factor_blocks.shape
    pairs = amplitudes.shape[1]
    levels = task_count // 2
    level = column // 2
    depth = depth_here // levels
    total = 2 * levels * blocks_here
    matrix = jnp.asarray(forms_matrix())
    back = jnp.asarray(back_matrix())
    other_core = lambda x: lax.ppermute(x, "task", [(c, c ^ 1) for c in range(task_count)])

    def around(x, by):
        return lax.ppermute(x, "task", [(c, (c + 2 * by) % task_count) for c in range(task_count)])

    same_core = [[2 * z + k for z in range(levels)] for k in range(2)]
    slices = factor_blocks.reshape(blocks_here, levels, depth, -1)
    mine = [lax.dynamic_index_in_dim(slices, (level + by) % levels, 1, keepdims=False) for by in range(levels)]
    if pair_count == 4 and levels == 4:
        sides = [
            [(p * task_count + c, (p ^ (1 if c % 2 == turn else 2)) * task_count + c) for p in range(4) for c in range(task_count)]
            for turn in range(2)
        ]
        first_side = lambda x: lax.ppermute(x, ("pair", "task"), sides[0])
        second_side = lambda x: lax.ppermute(x, ("pair", "task"), sides[1])
        made_forms = lambda *parts: prepare(parts, column[None], matrix)
        own = amplitudes.transpose(2, 0, 1).reshape(TV * TV, blocks_here * pairs)
        amp1 = around(own, 1)
        part0 = mine[0]
        a0, b0, part1, part3 = first_side(part0), second_side(part0), around(mine[1], 1), around(mine[3], 3)

        a0, b0, part0, part1, part3, amp1, to2 = after((a0, b0, part0, part1, part3, amp1, mine[2]), ())
        part13 = jnp.concatenate([part1, part3], axis=0)
        q0, a13, b13, part2 = second_side(a0), first_side(part13), second_side(part13), around(to2, 2)
        forms0 = made_forms(part0, a0, b0, q0)

        own, forms0, a13, b13, part2, part13 = after((own, forms0, a13, b13, part2, part13), ())
        q13, a2, b2, amp2 = second_side(a13), first_side(part2), second_side(part2), around(own, 2)
        far0 = other_core(forms0)
        forms13 = made_forms(part13, a13, b13, q13)

        forms13, part2, a2, b2, own, amp2 = after((forms13, part2, a2, b2, own, amp2), ())
        q2, amp3 = second_side(a2), around(own, 3)
        far13 = other_core(after(forms13, far0))
        amps = prepare_amps([own, amp1, amp2, amp3], blocks_here, jnp.asarray(amp_matrix()))
        forms2 = made_forms(part2, a2, b2, after(q2, amps))
        far2 = other_core(after(forms2, far13))
        held = [forms0, far0, forms13, far13, forms2, far2]
    else:
        parts = [mine[0]] + [around(mine[by], by) for by in range(1, levels)]
        tiles = amplitudes.reshape(blocks_here, pairs, TV, TV).transpose(0, 3, 2, 1)
        tiles = jnp.pad(tiles, ((0, 0), (0, 0), (0, PAD - TV), (0, 0))).reshape(blocks_here, ROWS, pairs)
        amps = lax.all_gather(tiles, "task", axis=0, axis_index_groups=same_core)
        amps = amps[(level - jnp.arange(levels)) % levels].reshape(levels * blocks_here, ROWS, pairs)
        held = lax.all_gather(jnp.stack(parts), "pair", axis=2, tiled=True)
        held = [jnp.stack([held, other_core(held)], axis=1).reshape(total, depth * pair_count, -1)]
    amps = (amps, other_core(amps))

    ladder = None
    calls = min(levels, 4)
    width = levels // calls
    order = [2, 3, 1, 0] if calls == 4 else list(reversed(range(calls)))
    for call in order:
        first = call * width
        sums = ladders(
            first, width, levels, blocks_here, column[None], task_owners, task_local, held, amps, back, matrix
        )
        for i in range(width):
            term = (around(sums[i], first + i) if first + i else sums[i]).astype(F32)
            ladder = term if ladder is None else ladder + term
    return residual_in + ladder.transpose(0, 2, 1)


def solution(mesh):
    placed = (P("task", "pair", None), P("task", "pair", None), P("task", "pair", None), P(), P())
    return jax.shard_map(
        per_device, mesh=mesh, in_specs=placed, out_specs=P("task", "pair", None), check_vma=False
    )
```

```python
import functools

import jax
import jax.numpy as jnp
import numpy as np
from jax import lax
from jax.experimental import pallas as pl
from jax.experimental.pallas import tpu as pltpu
from jax.sharding import PartitionSpec as P

TV = 25
PAD = 32
GROUP = 4
LANES = PAD * GROUP
GROUPS = -(-TV // GROUP)
ROWS = TV * PAD
WIDE = GROUPS * LANES
ORDER = [x for g in range(GROUP) for x in range(g, TV, GROUP)]
START = [ORDER.index(g) * PAD for g in range(GROUP)] + [ROWS]
PLACE = np.argsort(ORDER)
PREPARE_STEPS = 2
BF = jnp.bfloat16
F32 = jnp.float32
VMEM_BYTES = 48 * 1024 * 1024


def spread(spots, rows):
    return (np.arange(rows)[:, None] == spots[None, :]).astype(jnp.bfloat16)


def forms_matrix():
    x, y = np.divmod(np.arange(TV * TV), TV)
    return np.concatenate([spread(PLACE[y] * PAD + x, ROWS), spread(x * PAD + y, ROWS)], axis=0)


def amp_matrix():
    c, d = np.divmod(np.arange(TV * TV), TV)
    return spread(d * PAD + c, ROWS)


def back_matrix():
    a, b = np.divmod(np.arange(TV * TV), TV)
    return spread(PLACE[a] * PAD + b, ROWS).T


def prepare_kernel(column_ref, *refs):
    tile_refs, matrix_ref, forms_ref, all_ref = refs[:4], refs[4], refs[5], refs[6]
    count, size, _ = tile_refs[0].shape
    depth = forms_ref.shape[2]

    @pl.when(pl.program_id(0) == 0)
    def _():
        core = lax.rem(column_ref[0], 2)
        for m in range(count):
            for place, ref in zip((0, 1 + core, 2 - core, 3), tile_refs):
                start = pl.multiple_of(m * depth + place * size, size)
                all_ref[pl.ds(start, size), :] = ref[m]

    wide = 2 if depth % LANES == 0 and count % 2 == 0 else 1
    for first in range(0, count, wide):
        made = lax.dot_general(
            matrix_ref[...],
            all_ref[first * depth : (first + wide) * depth, :],
            (((1,), (1,)), ((), ())),
            preferred_element_type=F32,
        ).astype(BF)
        for m in range(wide):
            forms_ref[first + m] = made[:, m * depth : (m + 1) * depth]


def prepare(parts, column, matrix):
    count, size, width = parts[0].shape
    depth = size * len(parts)
    rows = matrix.shape[0] // PREPARE_STEPS
    in_specs = [pl.BlockSpec(part.shape, lambda i, column: (0, 0, 0)) for part in parts]
    in_specs.append(pl.BlockSpec((rows, width), lambda i, column: (i, 0)))
    return pl.pallas_call(
        prepare_kernel,
        out_shape=jax.ShapeDtypeStruct((count, matrix.shape[0], depth), BF),
        grid_spec=pltpu.PrefetchScalarGridSpec(
            num_scalar_prefetch=1,
            grid=(PREPARE_STEPS,),
            in_specs=in_specs,
            out_specs=pl.BlockSpec((count, rows, depth), lambda i, column: (0, i, 0)),
            scratch_shapes=[pltpu.VMEM((count * depth, width), BF)],
        ),
        compiler_params=pltpu.CompilerParams(vmem_limit_bytes=VMEM_BYTES),
        cost_estimate=pl.CostEstimate(
            flops=2 * count * depth * width * matrix.shape[0],
            bytes_accessed=2 * count * depth * (width + matrix.shape[0]),
            transcendentals=0,
        ),
    )(column, *parts, matrix)


def amp_kernel(matrix_ref, *refs):
    tile_refs, out_ref = refs[:-1], refs[-1]
    blocks_here, pairs = out_ref.shape[0] // len(tile_refs), out_ref.shape[2]
    for by, ref in enumerate(tile_refs):
        made = jnp.dot(matrix_ref[...], ref[...], preferred_element_type=F32).astype(BF)
        for m in range(blocks_here):
            out_ref[by * blocks_here + m] = made[:, m * pairs : (m + 1) * pairs]


def prepare_amps(parts, blocks_here, matrix):
    levels, size = len(parts), parts[0].size
    pairs = parts[0].shape[1] // blocks_here
    return pl.pallas_call(
        amp_kernel,
        out_shape=jax.ShapeDtypeStruct((levels * blocks_here, ROWS, pairs), BF),
        compiler_params=pltpu.CompilerParams(vmem_limit_bytes=VMEM_BYTES),
        cost_estimate=pl.CostEstimate(
            flops=2 * levels * size * ROWS, bytes_accessed=4 * levels * size, transcendentals=0
        ),
    )(matrix, *parts)


def turned(ref, groups, by):
    numbers = [min(A * GROUP + (p - by) % GROUP, TV - 1) for A in groups for p in range(GROUP)]
    return jnp.concatenate([ref[x * PAD : (x + 1) * PAD, :] for x in numbers], axis=0)


def ladder_kernel(find, made, sources, column_ref, owners_ref, local_ref, *refs):
    factor_refs, amp_refs, refs = refs[:sources], refs[sources : sources + 2], refs[sources + 2 :]
    back_ref, matrix_ref, refs = refs[0], None if made else refs[1], refs[1 if made else 2 :]
    out_ref, v_ref, u_ref, acc_ref, c_buf, r_buf, amp_buf, sems = refs[:8]
    column, columns = pl.program_id(0), pl.num_programs(0)
    step, steps = pl.program_id(1), pl.num_programs(1)
    at = column * steps + step
    slot = lax.rem(at, 2)

    def fetch(choices, source, index, part, buffer, to, sem):
        for n, ref in enumerate(choices):

            @pl.when(source == n)
            def _():
                tile = ref.at[index, pl.ds(part * ROWS, ROWS)] if part is not None else ref.at[index]
                pltpu.make_async_copy(tile, buffer.at[to], sem).start()

    def fetch_task(i, j, to):
        places = find(i, j, column_ref, owners_ref, local_ref)
        fetch(factor_refs, *places["col"], 0 if made else None, c_buf, to, sems.at[to, 0])
        fetch(factor_refs, *places["row"], 1 if made else None, r_buf, to, sems.at[to, 1])
        fetch(amp_refs, *places["amp"], None, amp_buf, to, sems.at[to, 2])

    @pl.when(at == 0)
    def _():
        fetch_task(0, 0, 0)

    @pl.when(at + 1 < columns * steps)
    def _():
        last = step == steps - 1
        fetch_task(jnp.where(last, column + 1, column), jnp.where(last, 0, step + 1), 1 - slot)

    @pl.when(step == 0)
    def _():
        acc_ref[...] = jnp.zeros_like(acc_ref)

    for n, buffer in enumerate((c_buf, r_buf, amp_buf)):
        pltpu.make_async_copy(buffer.at[slot], buffer.at[slot], sems.at[slot, n]).wait()
    c_form, r_form, amp_form = c_buf.at[slot], r_buf.at[slot], amp_buf.at[slot]
    if not made:
        forms = refs[8]
        for i, tile in enumerate((c_form, r_form)):
            forms[i] = lax.dot_general(
                matrix_ref[i * ROWS : (i + 1) * ROWS, :],
                tile[...],
                (((1,), (1,)), ((), ())),
                preferred_element_type=F32,
            ).astype(BF)
        c_form, r_form = forms.at[0], forms.at[1]

    spot = lax.broadcasted_iota(jnp.int32, (PAD, LANES), 1) // PAD
    at_spot = [spot == p for p in range(GROUP)]
    nothing = jnp.zeros((PAD, LANES), F32)
    for first in range(0, GROUPS, 2):
        groups = range(first, min(first + 2, GROUPS))
        lanes = slice(groups[0] * LANES, (groups[-1] + 1) * LANES)
        for g in range(GROUP):
            v_ref[START[g] : START[g + 1], lanes] = lax.dot_general(
                c_form[START[g] : START[g + 1], :],
                turned(r_form, groups, g),
                (((1,), (1,)), ((), ())),
                preferred_element_type=F32,
            )
        for A in groups:
            for D in range(GROUPS):
                blocks = [
                    v_ref[START[g] + D * PAD : START[g] + (D + 1) * PAD, A * LANES : (A + 1) * LANES]
                    if D * GROUP + g < TV
                    else nothing
                    for g in range(GROUP)
                ]
                for i in range(min(GROUP, TV - A * GROUP)):
                    block = blocks[-i % GROUP]
                    for p in range(1, GROUP):
                        block = jnp.where(at_spot[p], blocks[(p - i) % GROUP], block)
                    u_ref[START[i] + A * PAD : START[i] + (A + 1) * PAD, D * LANES : (D + 1) * LANES] = block.astype(BF)
    out = local_ref[find(column, step, column_ref, owners_ref, local_ref)["task"], 3]
    for i in range(GROUP):
        acc_ref[out, START[i] : START[i + 1], :] += jnp.dot(
            u_ref[START[i] : START[i + 1], :], turned(amp_form, range(GROUPS), i), preferred_element_type=F32
        )

    @pl.when(step == steps - 1)
    def _():
        blocks_here, pairs = out_ref.shape[1], out_ref.shape[3]
        sums = jnp.concatenate([acc_ref[m].astype(BF) for m in range(blocks_here)], axis=1)
        sums = jnp.dot(back_ref[...], sums, preferred_element_type=F32).astype(BF)
        for m in range(blocks_here):
            out_ref[0, m] = sums[:, m * pairs : (m + 1) * pairs]


def ladders(first, columns, levels, blocks_here, column, task_owners, task_local, tiles, amps, back, matrix):
    tasks = task_owners.shape[0] // (2 * levels)
    pairs = amps[0].shape[2]
    made = tiles[0].shape[1] == 2 * ROWS
    depth = tiles[0].shape[2] if made else tiles[0].shape[1]
    held = (ROWS, depth) if made else tiles[0].shape[1:]

    def find(i, j, column_ref, owners_ref, local_ref):
        level, core = column_ref[0] // 2, lax.rem(column_ref[0], 2)
        task = (2 * lax.rem(level + first + i, levels) + core) * tasks + j

        def place(kind):
            owner = owners_ref[task, kind]
            below = lax.rem(level - owner // 2 + levels, levels)
            far = jnp.where(lax.rem(owner, 2) != core, 1, 0)
            return below, far, local_ref[task, kind]

        def factor(kind):
            below, far, m = place(kind)
            if not made:
                return 0, (below * 2 + far) * blocks_here + m
            return below * 2 + far, m

        below, far, m = place(2)
        return {"task": task, "row": factor(0), "col": factor(1), "amp": (far, below * blocks_here + m)}

    anywhere = pl.BlockSpec(memory_space=pl.ANY)
    fixed = lambda shape: pl.BlockSpec(shape, lambda i, j, *tables: (0,) * len(shape))
    operands = [*tiles, *amps, back]
    in_specs = [anywhere] * (len(tiles) + 2) + [fixed(back.shape)]
    scratch = [
        pltpu.VMEM((ROWS, WIDE), F32),
        pltpu.VMEM((ROWS, WIDE), BF),
        pltpu.VMEM((blocks_here, ROWS, pairs), F32),
        pltpu.VMEM((2, *held), BF),
        pltpu.VMEM((2, *held), BF),
        pltpu.VMEM((2, ROWS, pairs), BF),
        pltpu.SemaphoreType.DMA((2, 3)),
    ]
    if not made:
        in_specs.append(fixed(matrix.shape))
        scratch.append(pltpu.VMEM((2, ROWS, depth), BF))
        operands.append(matrix)
    return pl.pallas_call(
        functools.partial(ladder_kernel, find, made, len(tiles)),
        out_shape=jax.ShapeDtypeStruct((columns, blocks_here, TV * TV, pairs), BF),
        grid_spec=pltpu.PrefetchScalarGridSpec(
            num_scalar_prefetch=3,
            grid=(columns, tasks),
            in_specs=in_specs,
            out_specs=pl.BlockSpec((1, blocks_here, TV * TV, pairs), lambda i, j, *tables: (i, 0, 0, 0)),
            scratch_shapes=scratch,
        ),
        compiler_params=pltpu.CompilerParams(vmem_limit_bytes=VMEM_BYTES),
        cost_estimate=pl.CostEstimate(
            flops=2 * columns * tasks * ROWS * WIDE * (depth + pairs),
            bytes_accessed=2 * columns * tasks * ROWS * 2 * (depth + pairs),
            transcendentals=0,
        ),
    )(column, task_owners, task_local, *operands)


def after(values, done):
    return lax.optimization_barrier((values, done))[0]


def per_device(factor_blocks, amplitudes, residual_in, task_owners, task_local):
    pair_count = lax.axis_size("pair")
    task_count = lax.axis_size("task")
    column = lax.axis_index("task")
    blocks_here, depth_here, _ = factor_blocks.shape
    pairs = amplitudes.shape[1]
    levels = task_count // 2
    level = column // 2
    depth = depth_here // levels
    total = 2 * levels * blocks_here
    matrix = jnp.asarray(forms_matrix())
    back = jnp.asarray(back_matrix())
    other_core = lambda x: lax.ppermute(x, "task", [(c, c ^ 1) for c in range(task_count)])

    def around(x, by):
        return lax.ppermute(x, "task", [(c, (c + 2 * by) % task_count) for c in range(task_count)])

    same_core = [[2 * z + k for z in range(levels)] for k in range(2)]
    slices = factor_blocks.reshape(blocks_here, levels, depth, -1)
    mine = [lax.dynamic_index_in_dim(slices, (level + by) % levels, 1, keepdims=False) for by in range(levels)]
    if pair_count == 4 and levels == 4:
        sides = [
            [(p * task_count + c, (p ^ (1 if c % 2 == turn else 2)) * task_count + c) for p in range(4) for c in range(task_count)]
            for turn in range(2)
        ]
        first_side = lambda x: lax.ppermute(x, ("pair", "task"), sides[0])
        second_side = lambda x: lax.ppermute(x, ("pair", "task"), sides[1])
        made_forms = lambda *parts: prepare(parts, column[None], matrix)
        own = amplitudes.transpose(2, 0, 1).reshape(TV * TV, blocks_here * pairs)
        amp1 = around(own, 1)
        part0 = mine[0]
        a0, b0, part1, part3 = first_side(part0), second_side(part0), around(mine[1], 1), around(mine[3], 3)

        a0, b0, part0, part1, part3, amp1, to2 = after((a0, b0, part0, part1, part3, amp1, mine[2]), ())
        q0, a1, b1, part2 = second_side(a0), first_side(part1), second_side(part1), around(to2, 2)
        forms0 = made_forms(part0, a0, b0, q0)

        forms0, part1, a1, b1, part2, part3, amp1 = after((forms0, part1, a1, b1, part2, part3, amp1), ())
        q1, a3, b3, amp2 = second_side(a1), first_side(part3), second_side(part3), around(amp1, 1)
        far0 = other_core(forms0)
        forms1 = made_forms(part1, a1, b1, q1)

        forms1, part3, a3, b3, part2, amp2, far0 = after((forms1, part3, a3, b3, part2, amp2, far0), ())
        q3, a2, b2, amp3 = second_side(a3), first_side(part2), second_side(part2), around(amp2, 1)
        far1 = other_core(forms1)
        forms3 = made_forms(part3, a3, b3, q3)

        forms3, part2, a2, b2, amp3, far1 = after((forms3, part2, a2, b2, amp3, far1), ())
        q2 = second_side(a2)
        far3 = other_core(forms3)
        amps = prepare_amps([own, amp1, amp2, amp3], blocks_here, jnp.asarray(amp_matrix()))
        forms2 = made_forms(part2, a2, b2, after(q2, amps))
        far2 = other_core(after(forms2, far3))
        held = [forms0, far0, forms1, far1, forms2, far2, forms3, far3]
    else:
        parts = [mine[0]] + [around(mine[by], by) for by in range(1, levels)]
        tiles = amplitudes.reshape(blocks_here, pairs, TV, TV).transpose(0, 3, 2, 1)
        tiles = jnp.pad(tiles, ((0, 0), (0, 0), (0, PAD - TV), (0, 0))).reshape(blocks_here, ROWS, pairs)
        amps = lax.all_gather(tiles, "task", axis=0, axis_index_groups=same_core)
        amps = amps[(level - jnp.arange(levels)) % levels].reshape(levels * blocks_here, ROWS, pairs)
        held = lax.all_gather(jnp.stack(parts), "pair", axis=2, tiled=True)
        held = [jnp.stack([held, other_core(held)], axis=1).reshape(total, depth * pair_count, -1)]
    amps = (amps, other_core(amps))

    ladder = None
    calls = min(levels, 4)
    width = levels // calls
    order = [2, 3, 1, 0] if calls == 4 else list(reversed(range(calls)))
    for call in order:
        first = call * width
        sums = ladders(
            first, width, levels, blocks_here, column[None], task_owners, task_local, held, amps, back, matrix
        )
        for i in range(width):
            term = (around(sums[i], first + i) if first + i else sums[i]).astype(F32)
            ladder = term if ladder is None else ladder + term
    return residual_in + ladder.transpose(0, 2, 1)


def solution(mesh):
    placed = (P("task", "pair", None), P("task", "pair", None), P("task", "pair", None), P(), P())
    return jax.shard_map(
        per_device, mesh=mesh, in_specs=placed, out_specs=P("task", "pair", None), check_vma=False
    )
```

```python
import functools

import jax
import jax.numpy as jnp
import numpy as np
from jax import lax
from jax.experimental import pallas as pl
from jax.experimental.pallas import tpu as pltpu
from jax.sharding import PartitionSpec as P

TV = 25
PAD = 32
GROUP = 4
LANES = PAD * GROUP
GROUPS = -(-TV // GROUP)
ROWS = TV * PAD
WIDE = GROUPS * LANES
ORDER = [x for g in range(GROUP) for x in range(g, TV, GROUP)]
START = [ORDER.index(g) * PAD for g in range(GROUP)] + [ROWS]
PLACE = np.argsort(ORDER)
PREPARE_STEPS = 2
BF = jnp.bfloat16
F32 = jnp.float32
VMEM_BYTES = 48 * 1024 * 1024


def spread(spots, rows):
    return (np.arange(rows)[:, None] == spots[None, :]).astype(jnp.bfloat16)


def forms_matrix():
    x, y = np.divmod(np.arange(TV * TV), TV)
    return np.concatenate([spread(PLACE[y] * PAD + x, ROWS), spread(x * PAD + y, ROWS)], axis=0)


def amp_matrix():
    c, d = np.divmod(np.arange(TV * TV), TV)
    return spread(d * PAD + c, ROWS)


def back_matrix():
    a, b = np.divmod(np.arange(TV * TV), TV)
    return spread(PLACE[a] * PAD + b, ROWS).T


def prepare_kernel(column_ref, *refs):
    tile_refs, matrix_ref, forms_ref, all_ref = refs[:4], refs[4], refs[5], refs[6]
    count, size, _ = tile_refs[0].shape
    depth = forms_ref.shape[2]

    @pl.when(pl.program_id(0) == 0)
    def _():
        core = lax.rem(column_ref[0], 2)
        for m in range(count):
            for place, ref in zip((0, 1 + core, 2 - core, 3), tile_refs):
                start = pl.multiple_of(m * depth + place * size, size)
                all_ref[pl.ds(start, size), :] = ref[m]

    wide = 2 if depth % LANES == 0 and count % 2 == 0 else 1
    for first in range(0, count, wide):
        made = lax.dot_general(
            matrix_ref[...],
            all_ref[first * depth : (first + wide) * depth, :],
            (((1,), (1,)), ((), ())),
            preferred_element_type=F32,
        ).astype(BF)
        for m in range(wide):
            forms_ref[first + m] = made[:, m * depth : (m + 1) * depth]


def prepare(parts, column, matrix):
    count, size, width = parts[0].shape
    depth = size * len(parts)
    rows = matrix.shape[0] // PREPARE_STEPS
    in_specs = [pl.BlockSpec(part.shape, lambda i, column: (0, 0, 0)) for part in parts]
    in_specs.append(pl.BlockSpec((rows, width), lambda i, column: (i, 0)))
    return pl.pallas_call(
        prepare_kernel,
        out_shape=jax.ShapeDtypeStruct((count, matrix.shape[0], depth), BF),
        grid_spec=pltpu.PrefetchScalarGridSpec(
            num_scalar_prefetch=1,
            grid=(PREPARE_STEPS,),
            in_specs=in_specs,
            out_specs=pl.BlockSpec((count, rows, depth), lambda i, column: (0, i, 0)),
            scratch_shapes=[pltpu.VMEM((count * depth, width), BF)],
        ),
        compiler_params=pltpu.CompilerParams(vmem_limit_bytes=VMEM_BYTES),
        cost_estimate=pl.CostEstimate(
            flops=2 * count * depth * width * matrix.shape[0],
            bytes_accessed=2 * count * depth * (width + matrix.shape[0]),
            transcendentals=0,
        ),
    )(column, *parts, matrix)


def amp_kernel(matrix_ref, *refs):
    tile_refs, out_ref = refs[:-1], refs[-1]
    blocks_here, pairs = out_ref.shape[0] // len(tile_refs), out_ref.shape[2]
    for by, ref in enumerate(tile_refs):
        made = jnp.dot(matrix_ref[...], ref[...], preferred_element_type=F32).astype(BF)
        for m in range(blocks_here):
            out_ref[by * blocks_here + m] = made[:, m * pairs : (m + 1) * pairs]


def prepare_amps(parts, blocks_here, matrix):
    levels, size = len(parts), parts[0].size
    pairs = parts[0].shape[1] // blocks_here
    return pl.pallas_call(
        amp_kernel,
        out_shape=jax.ShapeDtypeStruct((levels * blocks_here, ROWS, pairs), BF),
        compiler_params=pltpu.CompilerParams(vmem_limit_bytes=VMEM_BYTES),
        cost_estimate=pl.CostEstimate(
            flops=2 * levels * size * ROWS, bytes_accessed=4 * levels * size, transcendentals=0
        ),
    )(matrix, *parts)


def turned(ref, groups, by):
    numbers = [min(A * GROUP + (p - by) % GROUP, TV - 1) for A in groups for p in range(GROUP)]
    return jnp.concatenate([ref[x * PAD : (x + 1) * PAD, :] for x in numbers], axis=0)


def ladder_kernel(find, made, sources, column_ref, owners_ref, local_ref, *refs):
    factor_refs, amp_refs, refs = refs[:sources], refs[sources : sources + 2], refs[sources + 2 :]
    back_ref, matrix_ref, refs = refs[0], None if made else refs[1], refs[1 if made else 2 :]
    out_ref, v_ref, u_ref, acc_ref, c_buf, r_buf, amp_buf, sems = refs[:8]
    column, columns = pl.program_id(0), pl.num_programs(0)
    step, steps = pl.program_id(1), pl.num_programs(1)
    at = column * steps + step
    slot = lax.rem(at, 2)

    def fetch(choices, source, index, part, buffer, to, sem):
        for n, ref in enumerate(choices):

            @pl.when(source == n)
            def _():
                tile = ref.at[index, pl.ds(part * ROWS, ROWS)] if part is not None else ref.at[index]
                pltpu.make_async_copy(tile, buffer.at[to], sem).start()

    def fetch_task(i, j, to):
        places = find(i, j, column_ref, owners_ref, local_ref)
        fetch(factor_refs, *places["col"], 0 if made else None, c_buf, to, sems.at[to, 0])
        fetch(factor_refs, *places["row"], 1 if made else None, r_buf, to, sems.at[to, 1])
        fetch(amp_refs, *places["amp"], None, amp_buf, to, sems.at[to, 2])

    @pl.when(at == 0)
    def _():
        fetch_task(0, 0, 0)

    @pl.when(at + 1 < columns * steps)
    def _():
        last = step == steps - 1
        fetch_task(jnp.where(last, column + 1, column), jnp.where(last, 0, step + 1), 1 - slot)

    @pl.when(step == 0)
    def _():
        acc_ref[...] = jnp.zeros_like(acc_ref)

    for n, buffer in enumerate((c_buf, r_buf, amp_buf)):
        pltpu.make_async_copy(buffer.at[slot], buffer.at[slot], sems.at[slot, n]).wait()
    c_form, r_form, amp_form = c_buf.at[slot], r_buf.at[slot], amp_buf.at[slot]
    if not made:
        forms = refs[8]
        for i, tile in enumerate((c_form, r_form)):
            forms[i] = lax.dot_general(
                matrix_ref[i * ROWS : (i + 1) * ROWS, :],
                tile[...],
                (((1,), (1,)), ((), ())),
                preferred_element_type=F32,
            ).astype(BF)
        c_form, r_form = forms.at[0], forms.at[1]

    spot = lax.broadcasted_iota(jnp.int32, (PAD, LANES), 1) // PAD
    at_spot = [spot == p for p in range(GROUP)]
    nothing = jnp.zeros((PAD, LANES), F32)
    for first in range(0, GROUPS, 2):
        groups = range(first, min(first + 2, GROUPS))
        lanes = slice(groups[0] * LANES, (groups[-1] + 1) * LANES)
        for g in range(GROUP):
            v_ref[START[g] : START[g + 1], lanes] = lax.dot_general(
                c_form[START[g] : START[g + 1], :],
                turned(r_form, groups, g),
                (((1,), (1,)), ((), ())),
                preferred_element_type=F32,
            )
        for A in groups:
            for D in range(GROUPS):
                blocks = [
                    v_ref[START[g] + D * PAD : START[g] + (D + 1) * PAD, A * LANES : (A + 1) * LANES]
                    if D * GROUP + g < TV
                    else nothing
                    for g in range(GROUP)
                ]
                for i in range(min(GROUP, TV - A * GROUP)):
                    block = blocks[-i % GROUP]
                    for p in range(1, GROUP):
                        block = jnp.where(at_spot[p], blocks[(p - i) % GROUP], block)
                    u_ref[START[i] + A * PAD : START[i] + (A + 1) * PAD, D * LANES : (D + 1) * LANES] = block.astype(BF)
    out = local_ref[find(column, step, column_ref, owners_ref, local_ref)["task"], 3]
    for i in range(GROUP):
        acc_ref[out, START[i] : START[i + 1], :] += jnp.dot(
            u_ref[START[i] : START[i + 1], :], turned(amp_form, range(GROUPS), i), preferred_element_type=F32
        )

    @pl.when(step == steps - 1)
    def _():
        blocks_here, pairs = out_ref.shape[1], out_ref.shape[3]
        sums = jnp.concatenate([acc_ref[m].astype(BF) for m in range(blocks_here)], axis=1)
        sums = jnp.dot(back_ref[...], sums, preferred_element_type=F32).astype(BF)
        for m in range(blocks_here):
            out_ref[0, m] = sums[:, m * pairs : (m + 1) * pairs]


def ladders(first, columns, levels, blocks_here, column, task_owners, task_local, tiles, amps, back, matrix):
    tasks = task_owners.shape[0] // (2 * levels)
    pairs = amps[0].shape[2]
    made = tiles[0].shape[1] == 2 * ROWS
    depth = tiles[0].shape[2] if made else tiles[0].shape[1]
    held = (ROWS, depth) if made else tiles[0].shape[1:]

    def find(i, j, column_ref, owners_ref, local_ref):
        level, core = column_ref[0] // 2, lax.rem(column_ref[0], 2)
        task = (2 * lax.rem(level + first + i, levels) + core) * tasks + j

        def place(kind):
            owner = owners_ref[task, kind]
            below = lax.rem(level - owner // 2 + levels, levels)
            far = jnp.where(lax.rem(owner, 2) != core, 1, 0)
            return below, far, local_ref[task, kind]

        def factor(kind):
            below, far, m = place(kind)
            if not made:
                return 0, (below * 2 + far) * blocks_here + m
            return below * 2 + far, m

        below, far, m = place(2)
        return {"task": task, "row": factor(0), "col": factor(1), "amp": (far, below * blocks_here + m)}

    anywhere = pl.BlockSpec(memory_space=pl.ANY)
    fixed = lambda shape: pl.BlockSpec(shape, lambda i, j, *tables: (0,) * len(shape))
    operands = [*tiles, *amps, back]
    in_specs = [anywhere] * (len(tiles) + 2) + [fixed(back.shape)]
    scratch = [
        pltpu.VMEM((ROWS, WIDE), F32),
        pltpu.VMEM((ROWS, WIDE), BF),
        pltpu.VMEM((blocks_here, ROWS, pairs), F32),
        pltpu.VMEM((2, *held), BF),
        pltpu.VMEM((2, *held), BF),
        pltpu.VMEM((2, ROWS, pairs), BF),
        pltpu.SemaphoreType.DMA((2, 3)),
    ]
    if not made:
        in_specs.append(fixed(matrix.shape))
        scratch.append(pltpu.VMEM((2, ROWS, depth), BF))
        operands.append(matrix)
    return pl.pallas_call(
        functools.partial(ladder_kernel, find, made, len(tiles)),
        out_shape=jax.ShapeDtypeStruct((columns, blocks_here, TV * TV, pairs), BF),
        grid_spec=pltpu.PrefetchScalarGridSpec(
            num_scalar_prefetch=3,
            grid=(columns, tasks),
            in_specs=in_specs,
            out_specs=pl.BlockSpec((1, blocks_here, TV * TV, pairs), lambda i, j, *tables: (i, 0, 0, 0)),
            scratch_shapes=scratch,
        ),
        compiler_params=pltpu.CompilerParams(vmem_limit_bytes=VMEM_BYTES),
        cost_estimate=pl.CostEstimate(
            flops=2 * columns * tasks * ROWS * WIDE * (depth + pairs),
            bytes_accessed=2 * columns * tasks * ROWS * 2 * (depth + pairs),
            transcendentals=0,
        ),
    )(column, task_owners, task_local, *operands)


def after(values, done):
    return lax.optimization_barrier((values, done))[0]


def per_device(factor_blocks, amplitudes, residual_in, task_owners, task_local):
    pair_count = lax.axis_size("pair")
    task_count = lax.axis_size("task")
    column = lax.axis_index("task")
    blocks_here, depth_here, _ = factor_blocks.shape
    pairs = amplitudes.shape[1]
    levels = task_count // 2
    level = column // 2
    depth = depth_here // levels
    total = 2 * levels * blocks_here
    matrix = jnp.asarray(forms_matrix())
    back = jnp.asarray(back_matrix())
    other_core = lambda x: lax.ppermute(x, "task", [(c, c ^ 1) for c in range(task_count)])

    def around(x, by):
        return lax.ppermute(x, "task", [(c, (c + 2 * by) % task_count) for c in range(task_count)])

    same_core = [[2 * z + k for z in range(levels)] for k in range(2)]
    slices = factor_blocks.reshape(blocks_here, levels, depth, -1)
    mine = [lax.dynamic_index_in_dim(slices, (level + by) % levels, 1, keepdims=False) for by in range(levels)]
    if pair_count == 4 and levels == 4:
        sides = [
            [(p * task_count + c, (p ^ (1 if c % 2 == turn else 2)) * task_count + c) for p in range(4) for c in range(task_count)]
            for turn in range(2)
        ]
        first_side = lambda x: lax.ppermute(x, ("pair", "task"), sides[0])
        second_side = lambda x: lax.ppermute(x, ("pair", "task"), sides[1])
        made_forms = lambda *parts: prepare(parts, column[None], matrix)
        own = amplitudes.transpose(2, 0, 1).reshape(TV * TV, blocks_here * pairs)
        amp1 = around(own, 1)
        part0 = mine[0]
        a0, b0, part1 = first_side(part0), second_side(part0), around(mine[1], 1)

        a0, b0, part0, part1, amp1, to3 = after((a0, b0, part0, part1, amp1, mine[3]), ())
        q0, a1, b1, part3 = second_side(a0), first_side(part1), second_side(part1), around(to3, 3)
        forms0 = made_forms(part0, a0, b0, q0)

        forms0, part1, a1, b1, part3, to2 = after((forms0, part1, a1, b1, part3, mine[2]), ())
        q1, a3, b3, part2 = second_side(a1), first_side(part3), second_side(part3), around(to2, 2)
        far0 = other_core(forms0)
        forms1 = made_forms(part1, a1, b1, q1)

        forms1, part3, a3, b3, part2, amp1, far0 = after((forms1, part3, a3, b3, part2, amp1, far0), ())
        q3, a2, b2, amp2 = second_side(a3), first_side(part2), second_side(part2), around(amp1, 1)
        far1 = other_core(forms1)
        forms3 = made_forms(part3, a3, b3, q3)

        forms3, part2, a2, b2, amp2, far1 = after((forms3, part2, a2, b2, amp2, far1), ())
        q2, amp3 = second_side(a2), around(amp2, 1)
        far3 = other_core(forms3)
        forms2 = made_forms(part2, a2, b2, q2)

        forms2, amp3, far3 = after((forms2, amp3, far3), ())
        far2 = other_core(forms2)
        amps = prepare_amps([own, amp1, amp2, amp3], blocks_here, jnp.asarray(amp_matrix()))
        held = [forms0, far0, forms1, far1, forms2, far2, forms3, far3]
    else:
        parts = [mine[0]] + [around(mine[by], by) for by in range(1, levels)]
        tiles = amplitudes.reshape(blocks_here, pairs, TV, TV).transpose(0, 3, 2, 1)
        tiles = jnp.pad(tiles, ((0, 0), (0, 0), (0, PAD - TV), (0, 0))).reshape(blocks_here, ROWS, pairs)
        amps = lax.all_gather(tiles, "task", axis=0, axis_index_groups=same_core)
        amps = amps[(level - jnp.arange(levels)) % levels].reshape(levels * blocks_here, ROWS, pairs)
        held = lax.all_gather(jnp.stack(parts), "pair", axis=2, tiled=True)
        held = [jnp.stack([held, other_core(held)], axis=1).reshape(total, depth * pair_count, -1)]
    amps = (amps, other_core(amps))

    ladder = None
    calls = min(levels, 4)
    width = levels // calls
    order = [2, 3, 1, 0] if calls == 4 else list(reversed(range(calls)))
    for call in order:
        first = call * width
        sums = ladders(
            first, width, levels, blocks_here, column[None], task_owners, task_local, held, amps, back, matrix
        )
        for i in range(width):
            term = (around(sums[i], first + i) if first + i else sums[i]).astype(F32)
            ladder = term if ladder is None else ladder + term
    return residual_in + ladder.transpose(0, 2, 1)


def solution(mesh):
    placed = (P("task", "pair", None), P("task", "pair", None), P("task", "pair", None), P(), P())
    return jax.shard_map(
        per_device, mesh=mesh, in_specs=placed, out_specs=P("task", "pair", None), check_vma=False
    )
```

```python
import functools

import jax
import jax.numpy as jnp
import numpy as np
from jax import lax
from jax.experimental import pallas as pl
from jax.experimental.pallas import tpu as pltpu
from jax.sharding import PartitionSpec as P

TV = 25
PAD = 32
GROUP = 4
LANES = PAD * GROUP
GROUPS = -(-TV // GROUP)
ROWS = TV * PAD
WIDE = GROUPS * LANES
ORDER = [x for g in range(GROUP) for x in range(g, TV, GROUP)]
START = [ORDER.index(g) * PAD for g in range(GROUP)] + [ROWS]
PLACE = np.argsort(ORDER)
PREPARE_STEPS = 2
BF = jnp.bfloat16
F32 = jnp.float32
VMEM_BYTES = 48 * 1024 * 1024
LADDER_VMEM_BYTES = 60 * 1024 * 1024


def spread(spots, rows):
    return (np.arange(rows)[:, None] == spots[None, :]).astype(jnp.bfloat16)


def forms_matrix():
    x, y = np.divmod(np.arange(TV * TV), TV)
    return np.concatenate([spread(PLACE[y] * PAD + x, ROWS), spread(x * PAD + y, ROWS)], axis=0)


def amp_matrix():
    c, d = np.divmod(np.arange(TV * TV), TV)
    return spread(d * PAD + c, ROWS)


def prepare_kernel(column_ref, *refs):
    tile_refs, matrix_ref, forms_ref, all_ref = refs[:4], refs[4], refs[5], refs[6]
    count, size, _ = tile_refs[0].shape
    depth = forms_ref.shape[2]

    @pl.when(pl.program_id(0) == 0)
    def _():
        core = lax.rem(column_ref[0], 2)
        for m in range(count):
            for place, ref in zip((0, 1 + core, 2 - core, 3), tile_refs):
                start = pl.multiple_of(m * depth + place * size, size)
                all_ref[pl.ds(start, size), :] = ref[m]

    wide = 2 if depth % LANES == 0 and count % 2 == 0 else 1
    for first in range(0, count, wide):
        made = lax.dot_general(
            matrix_ref[...],
            all_ref[first * depth : (first + wide) * depth, :],
            (((1,), (1,)), ((), ())),
            preferred_element_type=F32,
        ).astype(BF)
        for m in range(wide):
            forms_ref[first + m] = made[:, m * depth : (m + 1) * depth]


def prepare(parts, column, matrix):
    count, size, width = parts[0].shape
    depth = size * len(parts)
    rows = matrix.shape[0] // PREPARE_STEPS
    in_specs = [pl.BlockSpec(part.shape, lambda i, column: (0, 0, 0)) for part in parts]
    in_specs.append(pl.BlockSpec((rows, width), lambda i, column: (i, 0)))
    return pl.pallas_call(
        prepare_kernel,
        out_shape=jax.ShapeDtypeStruct((count, matrix.shape[0], depth), BF),
        grid_spec=pltpu.PrefetchScalarGridSpec(
            num_scalar_prefetch=1,
            grid=(PREPARE_STEPS,),
            in_specs=in_specs,
            out_specs=pl.BlockSpec((count, rows, depth), lambda i, column: (0, i, 0)),
            scratch_shapes=[pltpu.VMEM((count * depth, width), BF)],
        ),
        compiler_params=pltpu.CompilerParams(vmem_limit_bytes=VMEM_BYTES),
        cost_estimate=pl.CostEstimate(
            flops=2 * count * depth * width * matrix.shape[0],
            bytes_accessed=2 * count * depth * (width + matrix.shape[0]),
            transcendentals=0,
        ),
    )(column, *parts, matrix)


def amp_kernel(matrix_ref, *refs):
    tile_refs, out_ref = refs[:-1], refs[-1]
    blocks_here, pairs = out_ref.shape[0] // len(tile_refs), out_ref.shape[2]
    for by, ref in enumerate(tile_refs):
        made = jnp.dot(matrix_ref[...], ref[...], preferred_element_type=F32).astype(BF)
        for m in range(blocks_here):
            out_ref[by * blocks_here + m] = made[:, m * pairs : (m + 1) * pairs]


def prepare_amps(parts, blocks_here, matrix):
    levels, size = len(parts), parts[0].size
    pairs = parts[0].shape[1] // blocks_here
    return pl.pallas_call(
        amp_kernel,
        out_shape=jax.ShapeDtypeStruct((levels * blocks_here, ROWS, pairs), BF),
        compiler_params=pltpu.CompilerParams(vmem_limit_bytes=VMEM_BYTES),
        cost_estimate=pl.CostEstimate(
            flops=2 * levels * size * ROWS, bytes_accessed=4 * levels * size, transcendentals=0
        ),
    )(matrix, *parts)


def turned(ref, groups, by):
    numbers = [min(A * GROUP + (p - by) % GROUP, TV - 1) for A in groups for p in range(GROUP)]
    return jnp.concatenate([ref[x * PAD : (x + 1) * PAD, :] for x in numbers], axis=0)


def ladder_kernel(find, made, sources, column_ref, owners_ref, local_ref, *refs):
    factor_refs, amp_refs, refs = refs[:sources], refs[sources : sources + 2], refs[sources + 2 :]
    matrix_ref, refs = None if made else refs[0], refs[0 if made else 1 :]
    out_ref, v_ref, u_ref, acc_ref, c_buf, r_buf, amp_buf, sems = refs[:8]
    column, columns = pl.program_id(0), pl.num_programs(0)
    step, steps = pl.program_id(1), pl.num_programs(1)
    at = column * steps + step
    slot = at & 1

    def fetch(choices, source, index, part, buffer, to, sem):
        for n, ref in enumerate(choices):

            @pl.when(source == n)
            def _():
                tile = ref.at[index, pl.ds(part * ROWS, ROWS)] if part is not None else ref.at[index]
                pltpu.make_async_copy(tile, buffer.at[to], sem).start()

    def fetch_task(i, j, to):
        places = find(i, j, column_ref, owners_ref, local_ref)
        fetch(factor_refs, *places["col"], 0 if made else None, c_buf, to, sems.at[to, 0])
        fetch(factor_refs, *places["row"], 1 if made else None, r_buf, to, sems.at[to, 1])
        fetch(amp_refs, *places["amp"], None, amp_buf, to, sems.at[to, 2])

    @pl.when(at == 0)
    def _():
        fetch_task(0, 0, 0)

    @pl.when(at + 1 < columns * steps)
    def _():
        last = step == steps - 1
        fetch_task(jnp.where(last, column + 1, column), jnp.where(last, 0, step + 1), 1 - slot)

    @pl.when(step == 0)
    def _():
        acc_ref[...] = jnp.zeros_like(acc_ref)

    for n, buffer in enumerate((c_buf, r_buf, amp_buf)):
        pltpu.make_async_copy(buffer.at[slot], buffer.at[slot], sems.at[slot, n]).wait()
    c_form, r_form, amp_form = c_buf.at[slot], r_buf.at[slot], amp_buf.at[slot]
    if not made:
        forms = refs[8]
        for i, tile in enumerate((c_form, r_form)):
            forms[i] = lax.dot_general(
                matrix_ref[i * ROWS : (i + 1) * ROWS, :],
                tile[...],
                (((1,), (1,)), ((), ())),
                preferred_element_type=F32,
            ).astype(BF)
        c_form, r_form = forms.at[0], forms.at[1]

    spot = lax.broadcasted_iota(jnp.int32, (PAD, LANES), 1) // PAD
    at_spot = [spot == p for p in range(GROUP)]
    nothing = jnp.zeros((PAD, LANES), F32)
    for first in range(0, GROUPS, 2):
        groups = range(first, min(first + 2, GROUPS))
        lanes = slice(groups[0] * LANES, (groups[-1] + 1) * LANES)
        for g in range(GROUP):
            v_ref[START[g] : START[g + 1], lanes] = lax.dot_general(
                c_form[START[g] : START[g + 1], :],
                turned(r_form, groups, g),
                (((1,), (1,)), ((), ())),
                preferred_element_type=F32,
            )
        for A in groups:
            for D in range(GROUPS):
                blocks = [
                    v_ref[START[g] + D * PAD : START[g] + (D + 1) * PAD, A * LANES : (A + 1) * LANES]
                    if D * GROUP + g < TV
                    else nothing
                    for g in range(GROUP)
                ]
                for i in range(min(GROUP, TV - A * GROUP)):
                    block = blocks[-i % GROUP]
                    for p in range(1, GROUP):
                        block = jnp.where(at_spot[p], blocks[(p - i) % GROUP], block)
                    u_ref[START[i] + A * PAD : START[i] + (A + 1) * PAD, D * LANES : (D + 1) * LANES] = block.astype(BF)
    out = local_ref[find(column, step, column_ref, owners_ref, local_ref)["task"], 3]
    for i in range(GROUP):
        acc_ref[out, START[i] : START[i + 1], :] += jnp.dot(
            u_ref[START[i] : START[i + 1], :], turned(amp_form, range(GROUPS), i), preferred_element_type=F32
        )

    @pl.when(step == steps - 1)
    def _():
        for m in range(out_ref.shape[1]):
            rows = [acc_ref[m, PLACE[a] * PAD : PLACE[a] * PAD + TV, :] for a in range(TV)]
            out_ref[0, m] = jnp.concatenate(rows, axis=0).astype(BF)


def ladders(first, columns, levels, blocks_here, column, task_owners, task_local, tiles, amps, matrix):
    tasks = task_owners.shape[0] // (2 * levels)
    pairs = amps[0].shape[2]
    made = tiles[0].shape[1] == 2 * ROWS
    depth = tiles[0].shape[2] if made else tiles[0].shape[1]
    held = (ROWS, depth) if made else tiles[0].shape[1:]

    def find(i, j, column_ref, owners_ref, local_ref):
        level, core = column_ref[0] >> 1, column_ref[0] & 1
        above = level + first + i
        task = (2 * jnp.where(above >= levels, above - levels, above) + core) * tasks + j

        def place(kind):
            owner = owners_ref[task, kind]
            below = level - (owner >> 1)
            below = jnp.where(below < 0, below + levels, below)
            far = (owner & 1) ^ core
            return below, far, local_ref[task, kind]

        def factor(kind):
            below, far, m = place(kind)
            if not made:
                return 0, (below * 2 + far) * blocks_here + m
            return below * 2 + far, m

        below, far, m = place(2)
        return {"task": task, "row": factor(0), "col": factor(1), "amp": (far, below * blocks_here + m)}

    anywhere = pl.BlockSpec(memory_space=pl.ANY)
    operands = [*tiles, *amps]
    in_specs = [anywhere] * (len(tiles) + 2)
    scratch = [
        pltpu.VMEM((ROWS, WIDE), F32),
        pltpu.VMEM((ROWS, WIDE), BF),
        pltpu.VMEM((blocks_here, ROWS, pairs), F32),
        pltpu.VMEM((2, *held), BF),
        pltpu.VMEM((2, *held), BF),
        pltpu.VMEM((2, ROWS, pairs), BF),
        pltpu.SemaphoreType.DMA((2, 3)),
    ]
    if not made:
        in_specs.append(pl.BlockSpec(matrix.shape, lambda i, j, *tables: (0, 0)))
        scratch.append(pltpu.VMEM((2, ROWS, depth), BF))
        operands.append(matrix)
    return pl.pallas_call(
        functools.partial(ladder_kernel, find, made, len(tiles)),
        out_shape=jax.ShapeDtypeStruct((columns, blocks_here, TV * TV, pairs), BF),
        grid_spec=pltpu.PrefetchScalarGridSpec(
            num_scalar_prefetch=3,
            grid=(columns, tasks),
            in_specs=in_specs,
            out_specs=pl.BlockSpec((1, blocks_here, TV * TV, pairs), lambda i, j, *tables: (i, 0, 0, 0)),
            scratch_shapes=scratch,
        ),
        compiler_params=pltpu.CompilerParams(vmem_limit_bytes=LADDER_VMEM_BYTES),
        cost_estimate=pl.CostEstimate(
            flops=2 * columns * tasks * ROWS * WIDE * (depth + pairs),
            bytes_accessed=2 * columns * tasks * ROWS * 2 * (depth + pairs),
            transcendentals=0,
        ),
    )(column, task_owners, task_local, *operands)


def after(values, done):
    return lax.optimization_barrier((values, done))[0]


def per_device(factor_blocks, amplitudes, residual_in, task_owners, task_local):
    pair_count = lax.axis_size("pair")
    task_count = lax.axis_size("task")
    column = lax.axis_index("task")
    blocks_here, depth_here, _ = factor_blocks.shape
    pairs = amplitudes.shape[1]
    levels = task_count // 2
    level = column // 2
    depth = depth_here // levels
    total = 2 * levels * blocks_here
    matrix = jnp.asarray(forms_matrix())
    other_core = lambda x: lax.ppermute(x, "task", [(c, c ^ 1) for c in range(task_count)])

    def around(x, by):
        return lax.ppermute(x, "task", [(c, (c + 2 * by) % task_count) for c in range(task_count)])

    same_core = [[2 * z + k for z in range(levels)] for k in range(2)]
    slices = factor_blocks.reshape(blocks_here, levels, depth, -1)
    mine = [lax.dynamic_index_in_dim(slices, (level + by) % levels, 1, keepdims=False) for by in range(levels)]
    if pair_count == 4 and levels == 4:
        sides = [
            [(p * task_count + c, (p ^ (1 if c % 2 == turn else 2)) * task_count + c) for p in range(4) for c in range(task_count)]
            for turn in range(2)
        ]
        first_side = lambda x: lax.ppermute(x, ("pair", "task"), sides[0])
        second_side = lambda x: lax.ppermute(x, ("pair", "task"), sides[1])
        made_forms = lambda *parts: prepare(parts, column[None], matrix)
        own = amplitudes.transpose(2, 0, 1).reshape(TV * TV, blocks_here * pairs)
        amp1 = around(own, 1)
        part0 = mine[0]
        a0, b0, part1 = first_side(part0), second_side(part0), around(mine[1], 1)

        a0, b0, part0, part1, amp1, to3 = after((a0, b0, part0, part1, amp1, mine[3]), ())
        q0, a1, b1, part3, amp2 = second_side(a0), first_side(part1), second_side(part1), around(to3, 3), around(amp1, 1)
        forms0 = made_forms(part0, a0, b0, q0)

        forms0, part1, a1, b1, part3, to2, amp2 = after((forms0, part1, a1, b1, part3, mine[2], amp2), ())
        q1, a3, b3, part2 = second_side(a1), first_side(part3), second_side(part3), around(to2, 2)
        far0 = other_core(forms0)
        forms1 = made_forms(part1, a1, b1, q1)

        forms1, part3, a3, b3, part2, far0, amp2 = after((forms1, part3, a3, b3, part2, far0, amp2), ())
        q3, a2, b2, amp3 = second_side(a3), first_side(part2), second_side(part2), around(amp2, 1)
        far1 = other_core(forms1)
        forms3 = made_forms(part3, a3, b3, q3)

        forms3, part2, a2, b2, amp3, far1 = after((forms3, part2, a2, b2, amp3, far1), ())
        q2, far3 = second_side(a2), other_core(forms3)
        amps = prepare_amps([own, amp1, amp2, amp3], blocks_here, jnp.asarray(amp_matrix()))
        forms2 = made_forms(part2, a2, b2, q2)
        far2 = other_core(after(forms2, far3))
        held = [forms0, far0, forms1, far1, forms2, far2, forms3, far3]
    else:
        parts = [mine[0]] + [around(mine[by], by) for by in range(1, levels)]
        tiles = amplitudes.reshape(blocks_here, pairs, TV, TV).transpose(0, 3, 2, 1)
        tiles = jnp.pad(tiles, ((0, 0), (0, 0), (0, PAD - TV), (0, 0))).reshape(blocks_here, ROWS, pairs)
        amps = lax.all_gather(tiles, "task", axis=0, axis_index_groups=same_core)
        amps = amps[(level - jnp.arange(levels)) % levels].reshape(levels * blocks_here, ROWS, pairs)
        held = lax.all_gather(jnp.stack(parts), "pair", axis=2, tiled=True)
        held = [jnp.stack([held, other_core(held)], axis=1).reshape(total, depth * pair_count, -1)]
    amps = (amps, other_core(amps))

    ladder = None
    calls = min(levels, 4)
    width = levels // calls
    order = [2, 3, 1, 0] if calls == 4 else list(reversed(range(calls)))
    for call in order:
        first = call * width
        sums = ladders(first, width, levels, blocks_here, column[None], task_owners, task_local, held, amps, matrix)
        for i in range(width):
            term = (around(sums[i], first + i) if first + i else sums[i]).astype(F32)
            ladder = term if ladder is None else ladder + term
    return residual_in + ladder.transpose(0, 2, 1)


def solution(mesh):
    placed = (P("task", "pair", None), P("task", "pair", None), P("task", "pair", None), P(), P())
    return jax.shard_map(
        per_device, mesh=mesh, in_specs=placed, out_specs=P("task", "pair", None), check_vma=False
    )
```

```python
import functools

import jax
import jax.numpy as jnp
import numpy as np
from jax import lax
from jax.experimental import pallas as pl
from jax.experimental.pallas import tpu as pltpu
from jax.sharding import PartitionSpec as P

TV = 25
PAD = 32
GROUP = 4
LANES = PAD * GROUP
GROUPS = -(-TV // GROUP)
ROWS = TV * PAD
WIDE = GROUPS * LANES
ORDER = [x for g in range(GROUP) for x in range(g, TV, GROUP)]
START = [ORDER.index(g) * PAD for g in range(GROUP)] + [ROWS]
PLACE = np.argsort(ORDER)
PREPARE_STEPS = 2
BF = jnp.bfloat16
F32 = jnp.float32
VMEM_BYTES = 48 * 1024 * 1024


def spread(spots, rows):
    return (np.arange(rows)[:, None] == spots[None, :]).astype(jnp.bfloat16)


def forms_matrix():
    x, y = np.divmod(np.arange(TV * TV), TV)
    return np.concatenate([spread(PLACE[y] * PAD + x, ROWS), spread(x * PAD + y, ROWS)], axis=0)


def amp_matrix():
    c, d = np.divmod(np.arange(TV * TV), TV)
    return spread(d * PAD + c, ROWS)


def prepare_kernel(column_ref, *refs):
    tile_refs, matrix_ref, forms_ref, all_ref = refs[:4], refs[4], refs[5], refs[6]
    count, size, _ = tile_refs[0].shape
    depth = forms_ref.shape[2]

    @pl.when(pl.program_id(0) == 0)
    def _():
        core = lax.rem(column_ref[0], 2)
        for m in range(count):
            for place, ref in zip((0, 1 + core, 2 - core, 3), tile_refs):
                start = pl.multiple_of(m * depth + place * size, size)
                all_ref[pl.ds(start, size), :] = ref[m]

    wide = 2 if depth % LANES == 0 and count % 2 == 0 else 1
    for first in range(0, count, wide):
        made = lax.dot_general(
            matrix_ref[...],
            all_ref[first * depth : (first + wide) * depth, :],
            (((1,), (1,)), ((), ())),
            preferred_element_type=F32,
        ).astype(BF)
        for m in range(wide):
            forms_ref[first + m] = made[:, m * depth : (m + 1) * depth]


def prepare(parts, column, matrix):
    count, size, width = parts[0].shape
    depth = size * len(parts)
    rows = matrix.shape[0] // PREPARE_STEPS
    in_specs = [pl.BlockSpec(part.shape, lambda i, column: (0, 0, 0)) for part in parts]
    in_specs.append(pl.BlockSpec((rows, width), lambda i, column: (i, 0)))
    return pl.pallas_call(
        prepare_kernel,
        out_shape=jax.ShapeDtypeStruct((count, matrix.shape[0], depth), BF),
        grid_spec=pltpu.PrefetchScalarGridSpec(
            num_scalar_prefetch=1,
            grid=(PREPARE_STEPS,),
            in_specs=in_specs,
            out_specs=pl.BlockSpec((count, rows, depth), lambda i, column: (0, i, 0)),
            scratch_shapes=[pltpu.VMEM((count * depth, width), BF)],
        ),
        compiler_params=pltpu.CompilerParams(vmem_limit_bytes=VMEM_BYTES),
        cost_estimate=pl.CostEstimate(
            flops=2 * count * depth * width * matrix.shape[0],
            bytes_accessed=2 * count * depth * (width + matrix.shape[0]),
            transcendentals=0,
        ),
    )(column, *parts, matrix)


def amp_kernel(matrix_ref, *refs):
    tile_refs, out_ref = refs[:-1], refs[-1]
    blocks_here, pairs = out_ref.shape[0] // len(tile_refs), out_ref.shape[2]
    for by, ref in enumerate(tile_refs):
        made = jnp.dot(matrix_ref[...], ref[...], preferred_element_type=F32).astype(BF)
        for m in range(blocks_here):
            out_ref[by * blocks_here + m] = made[:, m * pairs : (m + 1) * pairs]


def prepare_amps(parts, blocks_here, matrix):
    levels, size = len(parts), parts[0].size
    pairs = parts[0].shape[1] // blocks_here
    return pl.pallas_call(
        amp_kernel,
        out_shape=jax.ShapeDtypeStruct((levels * blocks_here, ROWS, pairs), BF),
        compiler_params=pltpu.CompilerParams(vmem_limit_bytes=VMEM_BYTES),
        cost_estimate=pl.CostEstimate(
            flops=2 * levels * size * ROWS, bytes_accessed=4 * levels * size, transcendentals=0
        ),
    )(matrix, *parts)


def turned(ref, groups, by):
    numbers = [min(A * GROUP + (p - by) % GROUP, TV - 1) for A in groups for p in range(GROUP)]
    return jnp.concatenate([ref[x * PAD : (x + 1) * PAD, :] for x in numbers], axis=0)


def ladder_kernel(find, made, sources, column_ref, owners_ref, local_ref, *refs):
    factor_refs, amp_refs, refs = refs[:sources], refs[sources : sources + 2], refs[sources + 2 :]
    matrix_ref, refs = None if made else refs[0], refs[0 if made else 1 :]
    out_ref, v_ref, u_ref, acc_ref, c_buf, r_buf, amp_buf, sems = refs[:8]
    column, columns = pl.program_id(0), pl.num_programs(0)
    step, steps = pl.program_id(1), pl.num_programs(1)
    at = column * steps + step
    slot = at & 1

    def fetch(choices, source, index, part, buffer, to, sem):
        for n, ref in enumerate(choices):

            @pl.when(source == n)
            def _():
                tile = ref.at[index, pl.ds(part * ROWS, ROWS)] if part is not None else ref.at[index]
                pltpu.make_async_copy(tile, buffer.at[to], sem).start()

    def fetch_task(i, j, to):
        places = find(i, j, column_ref, owners_ref, local_ref)
        fetch(factor_refs, *places["col"], 0 if made else None, c_buf, to, sems.at[to, 0])
        fetch(factor_refs, *places["row"], 1 if made else None, r_buf, to, sems.at[to, 1])

    @pl.when(at == 0)
    def _():
        fetch_task(0, 0, 0)

    @pl.when(at + 1 < columns * steps)
    def _():
        last = step == steps - 1
        fetch_task(jnp.where(last, column + 1, column), jnp.where(last, 0, step + 1), 1 - slot)

    @pl.when(step == 0)
    def _():
        acc_ref[...] = jnp.zeros_like(acc_ref)

    here = find(column, step, column_ref, owners_ref, local_ref)
    for core in range(2):

        @pl.when(here["amp"][0] == core)
        def _():
            amp_buf[...] = amp_refs[core][here["amp"][1]]

    for n, buffer in enumerate((c_buf, r_buf)):
        pltpu.make_async_copy(buffer.at[slot], buffer.at[slot], sems.at[slot, n]).wait()
    c_form, r_form, amp_form = c_buf.at[slot], r_buf.at[slot], amp_buf
    if not made:
        forms = refs[8]
        for i, tile in enumerate((c_form, r_form)):
            forms[i] = lax.dot_general(
                matrix_ref[i * ROWS : (i + 1) * ROWS, :],
                tile[...],
                (((1,), (1,)), ((), ())),
                preferred_element_type=F32,
            ).astype(BF)
        c_form, r_form = forms.at[0], forms.at[1]

    spot = lax.broadcasted_iota(jnp.int32, (PAD, LANES), 1) // PAD
    at_spot = [spot == p for p in range(GROUP)]
    nothing = jnp.zeros((PAD, LANES), F32)
    for first in range(0, GROUPS, 2):
        groups = range(first, min(first + 2, GROUPS))
        lanes = slice(groups[0] * LANES, (groups[-1] + 1) * LANES)
        for g in range(GROUP):
            v_ref[START[g] : START[g + 1], lanes] = lax.dot_general(
                c_form[START[g] : START[g + 1], :],
                turned(r_form, groups, g),
                (((1,), (1,)), ((), ())),
                preferred_element_type=F32,
            )
        for A in groups:
            for D in range(GROUPS):
                blocks = [
                    v_ref[START[g] + D * PAD : START[g] + (D + 1) * PAD, A * LANES : (A + 1) * LANES]
                    if D * GROUP + g < TV
                    else nothing
                    for g in range(GROUP)
                ]
                for i in range(min(GROUP, TV - A * GROUP)):
                    block = blocks[-i % GROUP]
                    for p in range(1, GROUP):
                        block = jnp.where(at_spot[p], blocks[(p - i) % GROUP], block)
                    u_ref[START[i] + A * PAD : START[i] + (A + 1) * PAD, D * LANES : (D + 1) * LANES] = block.astype(BF)
    out = local_ref[here["task"], 3]
    for i in range(GROUP):
        acc_ref[out, START[i] : START[i + 1], :] += jnp.dot(
            u_ref[START[i] : START[i + 1], :], turned(amp_form, range(GROUPS), i), preferred_element_type=F32
        )

    @pl.when(step == steps - 1)
    def _():
        for m in range(out_ref.shape[1]):
            rows = [acc_ref[m, PLACE[a] * PAD : PLACE[a] * PAD + TV, :] for a in range(TV)]
            out_ref[0, m] = jnp.concatenate(rows, axis=0).astype(BF)


def ladders(first, columns, levels, blocks_here, column, task_owners, task_local, tiles, amps, matrix):
    tasks = task_owners.shape[0] // (2 * levels)
    pairs = amps[0].shape[2]
    made = tiles[0].shape[1] == 2 * ROWS
    depth = tiles[0].shape[2] if made else tiles[0].shape[1]
    held = (ROWS, depth) if made else tiles[0].shape[1:]

    def find(i, j, column_ref, owners_ref, local_ref):
        level, core = column_ref[0] >> 1, column_ref[0] & 1
        above = level + first + i
        task = (2 * jnp.where(above >= levels, above - levels, above) + core) * tasks + j

        def place(kind):
            owner = owners_ref[task, kind]
            below = level - (owner >> 1)
            below = jnp.where(below < 0, below + levels, below)
            far = (owner & 1) ^ core
            return below, far, local_ref[task, kind]

        def factor(kind):
            below, far, m = place(kind)
            if not made:
                return 0, (below * 2 + far) * blocks_here + m
            return below * 2 + far, m

        below, far, m = place(2)
        return {"task": task, "row": factor(0), "col": factor(1), "amp": (far, below * blocks_here + m)}

    anywhere = pl.BlockSpec(memory_space=pl.ANY)
    operands = [*tiles, *amps]
    in_specs = [anywhere] * len(tiles) + [pl.BlockSpec(memory_space=pltpu.VMEM)] * 2
    scratch = [
        pltpu.VMEM((ROWS, WIDE), F32),
        pltpu.VMEM((ROWS, WIDE), BF),
        pltpu.VMEM((blocks_here, ROWS, pairs), F32),
        pltpu.VMEM((2, *held), BF),
        pltpu.VMEM((2, *held), BF),
        pltpu.VMEM((ROWS, pairs), BF),
        pltpu.SemaphoreType.DMA((2, 2)),
    ]
    if not made:
        in_specs.append(pl.BlockSpec(matrix.shape, lambda i, j, *tables: (0, 0)))
        scratch.append(pltpu.VMEM((2, ROWS, depth), BF))
        operands.append(matrix)
    return pl.pallas_call(
        functools.partial(ladder_kernel, find, made, len(tiles)),
        out_shape=jax.ShapeDtypeStruct((columns, blocks_here, TV * TV, pairs), BF),
        grid_spec=pltpu.PrefetchScalarGridSpec(
            num_scalar_prefetch=3,
            grid=(columns, tasks),
            in_specs=in_specs,
            out_specs=pl.BlockSpec((1, blocks_here, TV * TV, pairs), lambda i, j, *tables: (i, 0, 0, 0)),
            scratch_shapes=scratch,
        ),
        compiler_params=pltpu.CompilerParams(vmem_limit_bytes=VMEM_BYTES),
        cost_estimate=pl.CostEstimate(
            flops=2 * columns * tasks * ROWS * WIDE * (depth + pairs),
            bytes_accessed=2 * columns * tasks * ROWS * 2 * (depth + pairs),
            transcendentals=0,
        ),
    )(column, task_owners, task_local, *operands)


def after(values, done):
    return lax.optimization_barrier((values, done))[0]


def per_device(factor_blocks, amplitudes, residual_in, task_owners, task_local):
    pair_count = lax.axis_size("pair")
    task_count = lax.axis_size("task")
    column = lax.axis_index("task")
    blocks_here, depth_here, _ = factor_blocks.shape
    pairs = amplitudes.shape[1]
    levels = task_count // 2
    level = column // 2
    depth = depth_here // levels
    total = 2 * levels * blocks_here
    matrix = jnp.asarray(forms_matrix())
    other_core = lambda x: lax.ppermute(x, "task", [(c, c ^ 1) for c in range(task_count)])

    def around(x, by):
        return lax.ppermute(x, "task", [(c, (c + 2 * by) % task_count) for c in range(task_count)])

    same_core = [[2 * z + k for z in range(levels)] for k in range(2)]
    slices = factor_blocks.reshape(blocks_here, levels, depth, -1)
    mine = [lax.dynamic_index_in_dim(slices, (level + by) % levels, 1, keepdims=False) for by in range(levels)]
    if pair_count == 4 and levels == 4:
        sides = [
            [(p * task_count + c, (p ^ (1 if c % 2 == turn else 2)) * task_count + c) for p in range(4) for c in range(task_count)]
            for turn in range(2)
        ]
        first_side = lambda x: lax.ppermute(x, ("pair", "task"), sides[0])
        second_side = lambda x: lax.ppermute(x, ("pair", "task"), sides[1])
        made_forms = lambda *parts: prepare(parts, column[None], matrix)
        own = amplitudes.transpose(2, 0, 1).reshape(TV * TV, blocks_here * pairs)
        part0 = mine[0]
        a0, b0, part1 = first_side(part0), second_side(part0), around(mine[1], 1)

        a0, b0, part0, part1, own, to3 = after((a0, b0, part0, part1, own, mine[3]), ())
        q0, a1, b1, part3, amp1 = second_side(a0), first_side(part1), second_side(part1), around(to3, 3), around(own, 1)
        forms0 = made_forms(part0, a0, b0, q0)

        forms0, part1, a1, b1, part3, to2, amp1 = after((forms0, part1, a1, b1, part3, mine[2], amp1), ())
        q1, a3, b3, part2 = second_side(a1), first_side(part3), second_side(part3), around(to2, 2)
        far0 = other_core(forms0)
        forms1 = made_forms(part1, a1, b1, q1)

        forms1, part3, a3, b3, part2, amp1, far0 = after((forms1, part3, a3, b3, part2, amp1, far0), ())
        q3, a2, b2, amp2 = second_side(a3), first_side(part2), second_side(part2), around(amp1, 1)
        far1 = other_core(forms1)
        forms3 = made_forms(part3, a3, b3, q3)

        forms3, part2, a2, b2, amp2, far1 = after((forms3, part2, a2, b2, amp2, far1), ())
        q2, amp3 = second_side(a2), around(amp2, 1)
        far3 = other_core(forms3)
        forms2 = made_forms(part2, a2, b2, q2)

        forms2, amp3, far3 = after((forms2, amp3, far3), ())
        far2 = other_core(forms2)
        amps = prepare_amps([own, amp1, amp2, amp3], blocks_here, jnp.asarray(amp_matrix()))
        held = [forms0, far0, forms1, far1, forms2, far2, forms3, far3]
    else:
        parts = [mine[0]] + [around(mine[by], by) for by in range(1, levels)]
        tiles = amplitudes.reshape(blocks_here, pairs, TV, TV).transpose(0, 3, 2, 1)
        tiles = jnp.pad(tiles, ((0, 0), (0, 0), (0, PAD - TV), (0, 0))).reshape(blocks_here, ROWS, pairs)
        amps = lax.all_gather(tiles, "task", axis=0, axis_index_groups=same_core)
        amps = amps[(level - jnp.arange(levels)) % levels].reshape(levels * blocks_here, ROWS, pairs)
        held = lax.all_gather(jnp.stack(parts), "pair", axis=2, tiled=True)
        held = [jnp.stack([held, other_core(held)], axis=1).reshape(total, depth * pair_count, -1)]
    amps = (amps, other_core(amps))

    ladder = None
    calls = min(levels, 4)
    width = levels // calls
    order = [2, 3, 1, 0] if calls == 4 else list(reversed(range(calls)))
    for call in order:
        first = call * width
        sums = ladders(first, width, levels, blocks_here, column[None], task_owners, task_local, held, amps, matrix)
        for i in range(width):
            term = (around(sums[i], first + i) if first + i else sums[i]).astype(F32)
            ladder = term if ladder is None else ladder + term
    return residual_in + ladder.transpose(0, 2, 1)


def solution(mesh):
    placed = (P("task", "pair", None), P("task", "pair", None), P("task", "pair", None), P(), P())
    return jax.shard_map(
        per_device, mesh=mesh, in_specs=placed, out_specs=P("task", "pair", None), check_vma=False
    )
```

```python
import functools

import jax
import jax.numpy as jnp
import numpy as np
from jax import lax
from jax.experimental import pallas as pl
from jax.experimental.pallas import tpu as pltpu
from jax.sharding import PartitionSpec as P

TV = 25
PAD = 32
GROUP = 4
LANES = PAD * GROUP
GROUPS = -(-TV // GROUP)
ROWS = TV * PAD
WIDE = GROUPS * LANES
ORDER = [x for g in range(GROUP) for x in range(g, TV, GROUP)]
START = [ORDER.index(g) * PAD for g in range(GROUP)] + [ROWS]
PLACE = np.argsort(ORDER)
PREPARE_STEPS = 2
BF = jnp.bfloat16
F32 = jnp.float32
VMEM_BYTES = 48 * 1024 * 1024
LADDER_VMEM_BYTES = 56 * 1024 * 1024


def spread(spots, rows):
    return (np.arange(rows)[:, None] == spots[None, :]).astype(jnp.bfloat16)


def forms_matrix():
    x, y = np.divmod(np.arange(TV * TV), TV)
    return np.concatenate([spread(PLACE[y] * PAD + x, ROWS), spread(x * PAD + y, ROWS)], axis=0)


def amp_matrix():
    c, d = np.divmod(np.arange(TV * TV), TV)
    return spread(d * PAD + c, ROWS)


def prepare_kernel(column_ref, *refs):
    tile_refs, matrix_ref, forms_ref, all_ref = refs[:4], refs[4], refs[5], refs[6]
    count, size, _ = tile_refs[0].shape
    depth = forms_ref.shape[2]

    @pl.when(pl.program_id(0) == 0)
    def _():
        core = lax.rem(column_ref[0], 2)
        for m in range(count):
            for place, ref in zip((0, 1 + core, 2 - core, 3), tile_refs):
                start = pl.multiple_of(m * depth + place * size, size)
                all_ref[pl.ds(start, size), :] = ref[m]

    wide = 2 if depth % LANES == 0 and count % 2 == 0 else 1
    for first in range(0, count, wide):
        made = lax.dot_general(
            matrix_ref[...],
            all_ref[first * depth : (first + wide) * depth, :],
            (((1,), (1,)), ((), ())),
            preferred_element_type=F32,
        ).astype(BF)
        for m in range(wide):
            forms_ref[first + m] = made[:, m * depth : (m + 1) * depth]


def prepare(parts, column, matrix):
    count, size, width = parts[0].shape
    depth = size * len(parts)
    rows = matrix.shape[0] // PREPARE_STEPS
    in_specs = [pl.BlockSpec(part.shape, lambda i, column: (0, 0, 0)) for part in parts]
    in_specs.append(pl.BlockSpec((rows, width), lambda i, column: (i, 0)))
    return pl.pallas_call(
        prepare_kernel,
        out_shape=jax.ShapeDtypeStruct((count, matrix.shape[0], depth), BF),
        grid_spec=pltpu.PrefetchScalarGridSpec(
            num_scalar_prefetch=1,
            grid=(PREPARE_STEPS,),
            in_specs=in_specs,
            out_specs=pl.BlockSpec((count, rows, depth), lambda i, column: (0, i, 0)),
            scratch_shapes=[pltpu.VMEM((count * depth, width), BF)],
        ),
        compiler_params=pltpu.CompilerParams(vmem_limit_bytes=VMEM_BYTES),
        cost_estimate=pl.CostEstimate(
            flops=2 * count * depth * width * matrix.shape[0],
            bytes_accessed=2 * count * depth * (width + matrix.shape[0]),
            transcendentals=0,
        ),
    )(column, *parts, matrix)


def amp_kernel(matrix_ref, *refs):
    tile_refs, out_ref = refs[:-1], refs[-1]
    blocks_here, pairs = out_ref.shape[0] // len(tile_refs), out_ref.shape[2]
    for by, ref in enumerate(tile_refs):
        made = jnp.dot(matrix_ref[...], ref[...], preferred_element_type=F32).astype(BF)
        for m in range(blocks_here):
            out_ref[by * blocks_here + m] = made[:, m * pairs : (m + 1) * pairs]


def prepare_amps(parts, blocks_here, matrix):
    levels, size = len(parts), parts[0].size
    pairs = parts[0].shape[1] // blocks_here
    return pl.pallas_call(
        amp_kernel,
        out_shape=jax.ShapeDtypeStruct((levels * blocks_here, ROWS, pairs), BF),
        compiler_params=pltpu.CompilerParams(vmem_limit_bytes=VMEM_BYTES),
        cost_estimate=pl.CostEstimate(
            flops=2 * levels * size * ROWS, bytes_accessed=4 * levels * size, transcendentals=0
        ),
    )(matrix, *parts)


def turned(ref, groups, by):
    numbers = [min(A * GROUP + (p - by) % GROUP, TV - 1) for A in groups for p in range(GROUP)]
    return jnp.concatenate([ref[x * PAD : (x + 1) * PAD, :] for x in numbers], axis=0)


def ladder_kernel(find, made, sources, column_ref, owners_ref, local_ref, *refs):
    factor_refs, amp_refs, refs = refs[:sources], refs[sources : sources + 2], refs[sources + 2 :]
    matrix_ref, refs = None if made else refs[0], refs[0 if made else 1 :]
    out_ref, v_ref, u_ref, acc_ref, c_buf, r_buf, amp_buf, sems = refs[:8]
    column, columns = pl.program_id(0), pl.num_programs(0)
    step, steps = pl.program_id(1), pl.num_programs(1)
    at = column * steps + step
    slot = at & 1

    def fetch(choices, source, index, part, buffer, to, sem):
        for n, ref in enumerate(choices):

            @pl.when(source == n)
            def _():
                tile = ref.at[index, pl.ds(part * ROWS, ROWS)] if part is not None else ref.at[index]
                pltpu.make_async_copy(tile, buffer.at[to], sem).start()

    def fetch_task(i, j, to):
        places = find(i, j, column_ref, owners_ref, local_ref)
        fetch(factor_refs, *places["col"], 0 if made else None, c_buf, to, sems.at[to, 0])
        fetch(factor_refs, *places["row"], 1 if made else None, r_buf, to, sems.at[to, 1])

    @pl.when(at == 0)
    def _():
        fetch_task(0, 0, 0)

    @pl.when(at + 1 < columns * steps)
    def _():
        last = step == steps - 1
        fetch_task(jnp.where(last, column + 1, column), jnp.where(last, 0, step + 1), 1 - slot)

    @pl.when(step == 0)
    def _():
        acc_ref[...] = jnp.zeros_like(acc_ref)

    here = find(column, step, column_ref, owners_ref, local_ref)
    for core in range(2):

        @pl.when(here["amp"][0] == core)
        def _():
            amp_buf[...] = amp_refs[core][here["amp"][1]]

    for n, buffer in enumerate((c_buf, r_buf)):
        pltpu.make_async_copy(buffer.at[slot], buffer.at[slot], sems.at[slot, n]).wait()
    c_form, r_form, amp_form = c_buf.at[slot], r_buf.at[slot], amp_buf
    if not made:
        forms = refs[8]
        for i, tile in enumerate((c_form, r_form)):
            forms[i] = lax.dot_general(
                matrix_ref[i * ROWS : (i + 1) * ROWS, :],
                tile[...],
                (((1,), (1,)), ((), ())),
                preferred_element_type=F32,
            ).astype(BF)
        c_form, r_form = forms.at[0], forms.at[1]

    spot = lax.broadcasted_iota(jnp.int32, (PAD, LANES), 1) // PAD
    at_spot = [spot == p for p in range(GROUP)]
    nothing = jnp.zeros((PAD, LANES), F32)
    for first in range(0, GROUPS, 2):
        groups = range(first, min(first + 2, GROUPS))
        lanes = slice(groups[0] * LANES, (groups[-1] + 1) * LANES)
        for g in range(GROUP):
            v_ref[START[g] : START[g + 1], lanes] = lax.dot_general(
                c_form[START[g] : START[g + 1], :],
                turned(r_form, groups, g),
                (((1,), (1,)), ((), ())),
                preferred_element_type=F32,
            )
        for A in groups:
            for D in range(GROUPS):
                blocks = [
                    v_ref[START[g] + D * PAD : START[g] + (D + 1) * PAD, A * LANES : (A + 1) * LANES]
                    if D * GROUP + g < TV
                    else nothing
                    for g in range(GROUP)
                ]
                for i in range(min(GROUP, TV - A * GROUP)):
                    block = blocks[-i % GROUP]
                    for p in range(1, GROUP):
                        block = jnp.where(at_spot[p], blocks[(p - i) % GROUP], block)
                    u_ref[START[i] + A * PAD : START[i] + (A + 1) * PAD, D * LANES : (D + 1) * LANES] = block.astype(BF)
    out = local_ref[here["task"], 3]
    for i in range(GROUP):
        acc_ref[out, START[i] : START[i + 1], :] += jnp.dot(
            u_ref[START[i] : START[i + 1], :], turned(amp_form, range(GROUPS), i), preferred_element_type=F32
        )

    @pl.when(step == steps - 1)
    def _():
        for m in range(out_ref.shape[1]):
            rows = [acc_ref[m, PLACE[a] * PAD : PLACE[a] * PAD + TV, :] for a in range(TV)]
            out_ref[0, m] = jnp.concatenate(rows, axis=0).astype(BF)


def ladders(first, columns, levels, blocks_here, column, task_owners, task_local, tiles, amps, matrix):
    tasks = task_owners.shape[0] // (2 * levels)
    pairs = amps[0].shape[2]
    made = tiles[0].shape[1] == 2 * ROWS
    depth = tiles[0].shape[2] if made else tiles[0].shape[1]
    held = (ROWS, depth) if made else tiles[0].shape[1:]

    def find(i, j, column_ref, owners_ref, local_ref):
        level, core = column_ref[0] >> 1, column_ref[0] & 1
        above = level + first + i
        task = (2 * jnp.where(above >= levels, above - levels, above) + core) * tasks + j

        def place(kind):
            owner = owners_ref[task, kind]
            below = level - (owner >> 1)
            below = jnp.where(below < 0, below + levels, below)
            far = (owner & 1) ^ core
            return below, far, local_ref[task, kind]

        def factor(kind):
            below, far, m = place(kind)
            if not made:
                return 0, (below * 2 + far) * blocks_here + m
            return below * 2 + far, m

        below, far, m = place(2)
        return {"task": task, "row": factor(0), "col": factor(1), "amp": (far, below * blocks_here + m)}

    anywhere = pl.BlockSpec(memory_space=pl.ANY)
    operands = [*tiles, *amps]
    in_specs = [anywhere] * len(tiles) + [pl.BlockSpec(memory_space=pltpu.VMEM)] * 2
    scratch = [
        pltpu.VMEM((ROWS, WIDE), F32),
        pltpu.VMEM((ROWS, WIDE), BF),
        pltpu.VMEM((blocks_here, ROWS, pairs), F32),
        pltpu.VMEM((2, *held), BF),
        pltpu.VMEM((2, *held), BF),
        pltpu.VMEM((ROWS, pairs), BF),
        pltpu.SemaphoreType.DMA((2, 2)),
    ]
    if not made:
        in_specs.append(pl.BlockSpec(matrix.shape, lambda i, j, *tables: (0, 0)))
        scratch.append(pltpu.VMEM((2, ROWS, depth), BF))
        operands.append(matrix)
    return pl.pallas_call(
        functools.partial(ladder_kernel, find, made, len(tiles)),
        out_shape=jax.ShapeDtypeStruct((columns, blocks_here, TV * TV, pairs), BF),
        grid_spec=pltpu.PrefetchScalarGridSpec(
            num_scalar_prefetch=3,
            grid=(columns, tasks),
            in_specs=in_specs,
            out_specs=pl.BlockSpec((1, blocks_here, TV * TV, pairs), lambda i, j, *tables: (i, 0, 0, 0)),
            scratch_shapes=scratch,
        ),
        compiler_params=pltpu.CompilerParams(vmem_limit_bytes=LADDER_VMEM_BYTES),
        cost_estimate=pl.CostEstimate(
            flops=2 * columns * tasks * ROWS * WIDE * (depth + pairs),
            bytes_accessed=2 * columns * tasks * ROWS * 2 * (depth + pairs),
            transcendentals=0,
        ),
    )(column, task_owners, task_local, *operands)


def after(values, done):
    return lax.optimization_barrier((values, done))[0]


def per_device(factor_blocks, amplitudes, residual_in, task_owners, task_local):
    pair_count = lax.axis_size("pair")
    task_count = lax.axis_size("task")
    column = lax.axis_index("task")
    blocks_here, depth_here, _ = factor_blocks.shape
    pairs = amplitudes.shape[1]
    levels = task_count // 2
    level = column // 2
    depth = depth_here // levels
    total = 2 * levels * blocks_here
    matrix = jnp.asarray(forms_matrix())
    other_core = lambda x: lax.ppermute(x, "task", [(c, c ^ 1) for c in range(task_count)])

    def around(x, by):
        return lax.ppermute(x, "task", [(c, (c + 2 * by) % task_count) for c in range(task_count)])

    same_core = [[2 * z + k for z in range(levels)] for k in range(2)]
    slices = factor_blocks.reshape(blocks_here, levels, depth, -1)
    mine = [lax.dynamic_index_in_dim(slices, (level + by) % levels, 1, keepdims=False) for by in range(levels)]
    if pair_count == 4 and levels == 4:
        sides = [
            [(p * task_count + c, (p ^ (1 if c % 2 == turn else 2)) * task_count + c) for p in range(4) for c in range(task_count)]
            for turn in range(2)
        ]
        first_side = lambda x: lax.ppermute(x, ("pair", "task"), sides[0])
        second_side = lambda x: lax.ppermute(x, ("pair", "task"), sides[1])
        made_forms = lambda *parts: prepare(parts, column[None], matrix)
        own = amplitudes.transpose(2, 0, 1).reshape(TV * TV, blocks_here * pairs)
        amp1 = around(own, 1)
        part0 = mine[0]
        a0, b0, part1 = first_side(part0), second_side(part0), around(mine[1], 1)

        a0, b0, part0, part1, amp1, own, to3 = after((a0, b0, part0, part1, amp1, own, mine[3]), ())
        q0, a1, b1, part3 = second_side(a0), first_side(part1), second_side(part1), around(to3, 3)
        far_own = other_core(own)
        forms0 = made_forms(part0, a0, b0, q0)

        forms0, part1, a1, b1, part3, to2, far_own = after((forms0, part1, a1, b1, part3, mine[2], far_own), ())
        q1, a3, b3, part2 = second_side(a1), first_side(part3), second_side(part3), around(to2, 2)
        far0 = other_core(forms0)
        forms1 = made_forms(part1, a1, b1, q1)

        forms1, part3, a3, b3, part2, amp1, far0 = after((forms1, part3, a3, b3, part2, amp1, far0), ())
        q3, a2, b2, amp2 = second_side(a3), first_side(part2), second_side(part2), around(amp1, 1)
        far1 = other_core(forms1)
        forms3 = made_forms(part3, a3, b3, q3)

        forms3, part2, a2, b2, amp1, amp2, far1 = after((forms3, part2, a2, b2, amp1, amp2, far1), ())
        q2, amp3 = second_side(a2), around(amp2, 1)
        far3, far_amp1, far_amp2 = other_core(forms3), other_core(amp1), other_core(amp2)
        forms2 = made_forms(part2, a2, b2, q2)

        forms2, amp3, far3, far_amp1, far_amp2 = after((forms2, amp3, far3, far_amp1, far_amp2), ())
        far2, far_amp3 = other_core(forms2), other_core(amp3)
        amps = [[own, amp1, amp2, amp3], [far_own, far_amp1, far_amp2, far_amp3]]
        amps = [prepare_amps(tiles, blocks_here, jnp.asarray(amp_matrix())) for tiles in amps]
        held = [forms0, far0, forms1, far1, forms2, far2, forms3, far3]
    else:
        parts = [mine[0]] + [around(mine[by], by) for by in range(1, levels)]
        tiles = amplitudes.reshape(blocks_here, pairs, TV, TV).transpose(0, 3, 2, 1)
        tiles = jnp.pad(tiles, ((0, 0), (0, 0), (0, PAD - TV), (0, 0))).reshape(blocks_here, ROWS, pairs)
        amps = lax.all_gather(tiles, "task", axis=0, axis_index_groups=same_core)
        amps = amps[(level - jnp.arange(levels)) % levels].reshape(levels * blocks_here, ROWS, pairs)
        held = lax.all_gather(jnp.stack(parts), "pair", axis=2, tiled=True)
        amps = [amps, other_core(amps)]
        held = [jnp.stack([held, other_core(held)], axis=1).reshape(total, depth * pair_count, -1)]
    ladder, here = None, column[None]
    calls = min(levels, 4)
    width = levels // calls
    order = [2, 3, 1, 0] if calls == 4 else list(reversed(range(calls)))
    for call in order:
        first = call * width
        sums = ladders(first, width, levels, blocks_here, here, task_owners, task_local, held, amps, matrix)
        here = after(here, sums)
        for i in range(width):
            term = (around(sums[i], first + i) if first + i else sums[i]).astype(F32)
            ladder = term if ladder is None else ladder + term
    return residual_in + ladder.transpose(0, 2, 1)


def solution(mesh):
    placed = (P("task", "pair", None), P("task", "pair", None), P("task", "pair", None), P(), P())
    return jax.shard_map(
        per_device, mesh=mesh, in_specs=placed, out_specs=P("task", "pair", None), check_vma=False
    )
```

```python
import functools

import jax
import jax.numpy as jnp
import numpy as np
from jax import lax
from jax.experimental import pallas as pl
from jax.experimental.pallas import tpu as pltpu
from jax.sharding import PartitionSpec as P

TV = 25
PAD = 32
GROUP = 4
LANES = PAD * GROUP
GROUPS = -(-TV // GROUP)
ROWS = TV * PAD
WIDE = GROUPS * LANES
ORDER = [x for g in range(GROUP) for x in range(g, TV, GROUP)]
START = [ORDER.index(g) * PAD for g in range(GROUP)] + [ROWS]
PLACE = np.argsort(ORDER)
PREPARE_STEPS = 2
BF = jnp.bfloat16
F32 = jnp.float32
VMEM_BYTES = 48 * 1024 * 1024


def spread(spots, rows):
    return (np.arange(rows)[:, None] == spots[None, :]).astype(jnp.bfloat16)


def forms_matrix():
    x, y = np.divmod(np.arange(TV * TV), TV)
    return np.concatenate([spread(PLACE[y] * PAD + x, ROWS), spread(x * PAD + y, ROWS)], axis=0)


def amp_matrix():
    c, d = np.divmod(np.arange(TV * TV), TV)
    return spread(d * PAD + c, ROWS)


def prepare_kernel(column_ref, *refs):
    tile_refs, matrix_ref, forms_ref, all_ref = refs[:4], refs[4], refs[5], refs[6]
    count, size, _ = tile_refs[0].shape
    depth = forms_ref.shape[2]

    @pl.when(pl.program_id(0) == 0)
    def _():
        core = lax.rem(column_ref[0], 2)
        for m in range(count):
            for place, ref in zip((0, 1 + core, 2 - core, 3), tile_refs):
                start = pl.multiple_of(m * depth + place * size, size)
                all_ref[pl.ds(start, size), :] = ref[m]

    wide = 2 if depth % LANES == 0 and count % 2 == 0 else 1
    for first in range(0, count, wide):
        made = lax.dot_general(
            matrix_ref[...],
            all_ref[first * depth : (first + wide) * depth, :],
            (((1,), (1,)), ((), ())),
            preferred_element_type=F32,
        ).astype(BF)
        for m in range(wide):
            forms_ref[first + m] = made[:, m * depth : (m + 1) * depth]


def prepare(parts, column, matrix):
    count, size, width = parts[0].shape
    depth = size * len(parts)
    rows = matrix.shape[0] // PREPARE_STEPS
    in_specs = [pl.BlockSpec(part.shape, lambda i, column: (0, 0, 0)) for part in parts]
    in_specs.append(pl.BlockSpec((rows, width), lambda i, column: (i, 0)))
    return pl.pallas_call(
        prepare_kernel,
        out_shape=jax.ShapeDtypeStruct((count, matrix.shape[0], depth), BF),
        grid_spec=pltpu.PrefetchScalarGridSpec(
            num_scalar_prefetch=1,
            grid=(PREPARE_STEPS,),
            in_specs=in_specs,
            out_specs=pl.BlockSpec((count, rows, depth), lambda i, column: (0, i, 0)),
            scratch_shapes=[pltpu.VMEM((count * depth, width), BF)],
        ),
        compiler_params=pltpu.CompilerParams(vmem_limit_bytes=VMEM_BYTES),
        cost_estimate=pl.CostEstimate(
            flops=2 * count * depth * width * matrix.shape[0],
            bytes_accessed=2 * count * depth * (width + matrix.shape[0]),
            transcendentals=0,
        ),
    )(column, *parts, matrix)


def amp_kernel(matrix_ref, *refs):
    tile_refs, out_ref = refs[:-1], refs[-1]
    blocks_here, pairs = out_ref.shape[0] // len(tile_refs), out_ref.shape[2]
    for by, ref in enumerate(tile_refs):
        made = jnp.dot(matrix_ref[...], ref[...], preferred_element_type=F32).astype(BF)
        for m in range(blocks_here):
            out_ref[by * blocks_here + m] = made[:, m * pairs : (m + 1) * pairs]


def prepare_amps(parts, blocks_here, matrix):
    levels, size = len(parts), parts[0].size
    pairs = parts[0].shape[1] // blocks_here
    return pl.pallas_call(
        amp_kernel,
        out_shape=jax.ShapeDtypeStruct((levels * blocks_here, ROWS, pairs), BF),
        compiler_params=pltpu.CompilerParams(vmem_limit_bytes=VMEM_BYTES),
        cost_estimate=pl.CostEstimate(
            flops=2 * levels * size * ROWS, bytes_accessed=4 * levels * size, transcendentals=0
        ),
    )(matrix, *parts)


def turned(ref, groups, by):
    numbers = [min(A * GROUP + (p - by) % GROUP, TV - 1) for A in groups for p in range(GROUP)]
    return jnp.concatenate([ref[x * PAD : (x + 1) * PAD, :] for x in numbers], axis=0)


def ladder_kernel(find, made, sources, column_ref, owners_ref, local_ref, *refs):
    factor_refs, amp_refs, refs = refs[:sources], refs[sources : sources + 2], refs[sources + 2 :]
    matrix_ref, refs = None if made else refs[0], refs[0 if made else 1 :]
    out_ref, v_ref, u_ref, acc_ref, c_buf, r_buf, amp_buf, sems = refs[:8]
    column, columns = pl.program_id(0), pl.num_programs(0)
    step, steps = pl.program_id(1), pl.num_programs(1)
    at = column * steps + step
    slot = at & 1

    def fetch(choices, source, index, part, buffer, to, sem):
        for n, ref in enumerate(choices):

            @pl.when(source == n)
            def _():
                tile = ref.at[index, pl.ds(part * ROWS, ROWS)] if part is not None else ref.at[index]
                pltpu.make_async_copy(tile, buffer.at[to], sem).start()

    def fetch_task(i, j, to):
        places = find(i, j, column_ref, owners_ref, local_ref)
        fetch(factor_refs, *places["col"], 0 if made else None, c_buf, to, sems.at[to, 0])
        fetch(factor_refs, *places["row"], 1 if made else None, r_buf, to, sems.at[to, 1])

    @pl.when(at == 0)
    def _():
        fetch_task(0, 0, 0)

    @pl.when(at + 1 < columns * steps)
    def _():
        last = step == steps - 1
        fetch_task(jnp.where(last, column + 1, column), jnp.where(last, 0, step + 1), 1 - slot)

    @pl.when(step == 0)
    def _():
        acc_ref[...] = jnp.zeros_like(acc_ref)

    here = find(column, step, column_ref, owners_ref, local_ref)
    for core in range(2):

        @pl.when(here["amp"][0] == core)
        def _():
            amp_buf[...] = amp_refs[core][here["amp"][1]]

    for n, buffer in enumerate((c_buf, r_buf)):
        pltpu.make_async_copy(buffer.at[slot], buffer.at[slot], sems.at[slot, n]).wait()
    c_form, r_form, amp_form = c_buf.at[slot], r_buf.at[slot], amp_buf
    if not made:
        forms = refs[8]
        for i, tile in enumerate((c_form, r_form)):
            forms[i] = lax.dot_general(
                matrix_ref[i * ROWS : (i + 1) * ROWS, :],
                tile[...],
                (((1,), (1,)), ((), ())),
                preferred_element_type=F32,
            ).astype(BF)
        c_form, r_form = forms.at[0], forms.at[1]

    spot = lax.broadcasted_iota(jnp.int32, (PAD, LANES), 1) // PAD
    at_spot = [spot == p for p in range(GROUP)]
    nothing = jnp.zeros((PAD, LANES), F32)
    for first in range(0, GROUPS, 2):
        groups = range(first, min(first + 2, GROUPS))
        lanes = slice(groups[0] * LANES, (groups[-1] + 1) * LANES)
        for g in range(GROUP):
            v_ref[START[g] : START[g + 1], lanes] = lax.dot_general(
                c_form[START[g] : START[g + 1], :],
                turned(r_form, groups, g),
                (((1,), (1,)), ((), ())),
                preferred_element_type=F32,
            )
        for A in groups:
            for D in range(GROUPS):
                blocks = [
                    v_ref[START[g] + D * PAD : START[g] + (D + 1) * PAD, A * LANES : (A + 1) * LANES]
                    if D * GROUP + g < TV
                    else nothing
                    for g in range(GROUP)
                ]
                for i in range(min(GROUP, TV - A * GROUP)):
                    block = blocks[-i % GROUP]
                    for p in range(1, GROUP):
                        block = jnp.where(at_spot[p], blocks[(p - i) % GROUP], block)
                    u_ref[START[i] + A * PAD : START[i] + (A + 1) * PAD, D * LANES : (D + 1) * LANES] = block.astype(BF)
    out = local_ref[here["task"], 3]
    for i in range(GROUP):
        acc_ref[out, START[i] : START[i + 1], :] += jnp.dot(
            u_ref[START[i] : START[i + 1], :], turned(amp_form, range(GROUPS), i), preferred_element_type=F32
        )

    @pl.when(step == steps - 1)
    def _():
        for m in range(out_ref.shape[1]):
            rows = [acc_ref[m, PLACE[a] * PAD : PLACE[a] * PAD + TV, :] for a in range(TV)]
            out_ref[0, m] = jnp.concatenate(rows, axis=0).astype(BF)


def ladders(first, columns, levels, blocks_here, column, task_owners, task_local, tiles, amps, matrix):
    tasks = task_owners.shape[0] // (2 * levels)
    pairs = amps[0].shape[2]
    made = tiles[0].shape[1] == 2 * ROWS
    depth = tiles[0].shape[2] if made else tiles[0].shape[1]
    held = (ROWS, depth) if made else tiles[0].shape[1:]

    def find(i, j, column_ref, owners_ref, local_ref):
        level, core = column_ref[0] >> 1, column_ref[0] & 1
        above = level + first + i
        task = (2 * jnp.where(above >= levels, above - levels, above) + core) * tasks + j

        def place(kind):
            owner = owners_ref[task, kind]
            below = level - (owner >> 1)
            below = jnp.where(below < 0, below + levels, below)
            far = (owner & 1) ^ core
            return below, far, local_ref[task, kind]

        def factor(kind):
            below, far, m = place(kind)
            if not made:
                return 0, (below * 2 + far) * blocks_here + m
            return below * 2 + far, m

        below, far, m = place(2)
        return {"task": task, "row": factor(0), "col": factor(1), "amp": (far, below * blocks_here + m)}

    anywhere = pl.BlockSpec(memory_space=pl.ANY)
    operands = [*tiles, *amps]
    in_specs = [anywhere] * len(tiles) + [pl.BlockSpec(memory_space=pltpu.VMEM)] * 2
    scratch = [
        pltpu.VMEM((ROWS, WIDE), F32),
        pltpu.VMEM((ROWS, WIDE), BF),
        pltpu.VMEM((blocks_here, ROWS, pairs), F32),
        pltpu.VMEM((2, *held), BF),
        pltpu.VMEM((2, *held), BF),
        pltpu.VMEM((ROWS, pairs), BF),
        pltpu.SemaphoreType.DMA((2, 2)),
    ]
    if not made:
        in_specs.append(pl.BlockSpec(matrix.shape, lambda i, j, *tables: (0, 0)))
        scratch.append(pltpu.VMEM((2, ROWS, depth), BF))
        operands.append(matrix)
    return pl.pallas_call(
        functools.partial(ladder_kernel, find, made, len(tiles)),
        out_shape=jax.ShapeDtypeStruct((columns, blocks_here, TV * TV, pairs), BF),
        grid_spec=pltpu.PrefetchScalarGridSpec(
            num_scalar_prefetch=3,
            grid=(columns, tasks),
            in_specs=in_specs,
            out_specs=pl.BlockSpec((1, blocks_here, TV * TV, pairs), lambda i, j, *tables: (i, 0, 0, 0)),
            scratch_shapes=scratch,
        ),
        compiler_params=pltpu.CompilerParams(vmem_limit_bytes=VMEM_BYTES),
        cost_estimate=pl.CostEstimate(
            flops=2 * columns * tasks * ROWS * WIDE * (depth + pairs),
            bytes_accessed=2 * columns * tasks * ROWS * 2 * (depth + pairs),
            transcendentals=0,
        ),
    )(column, task_owners, task_local, *operands)


def after(values, done):
    return lax.optimization_barrier((values, done))[0]


def per_device(factor_blocks, amplitudes, residual_in, task_owners, task_local):
    pair_count = lax.axis_size("pair")
    task_count = lax.axis_size("task")
    column = lax.axis_index("task")
    blocks_here, depth_here, _ = factor_blocks.shape
    pairs = amplitudes.shape[1]
    levels = task_count // 2
    level = column // 2
    depth = depth_here // levels
    total = 2 * levels * blocks_here
    matrix = jnp.asarray(forms_matrix())
    other_core = lambda x: lax.ppermute(x, "task", [(c, c ^ 1) for c in range(task_count)])

    def around(x, by):
        return lax.ppermute(x, "task", [(c, (c + 2 * by) % task_count) for c in range(task_count)])

    same_core = [[2 * z + k for z in range(levels)] for k in range(2)]
    slices = factor_blocks.reshape(blocks_here, levels, depth, -1)
    mine = [lax.dynamic_index_in_dim(slices, (level + by) % levels, 1, keepdims=False) for by in range(levels)]
    if pair_count == 4 and levels == 4:
        sides = [
            [(p * task_count + c, (p ^ (1 if c % 2 == turn else 2)) * task_count + c) for p in range(4) for c in range(task_count)]
            for turn in range(2)
        ]
        first_side = lambda x: lax.ppermute(x, ("pair", "task"), sides[0])
        second_side = lambda x: lax.ppermute(x, ("pair", "task"), sides[1])
        made_forms = lambda *parts: prepare(parts, column[None], matrix)
        own = amplitudes.transpose(2, 0, 1).reshape(TV * TV, blocks_here * pairs)
        amp1 = around(own, 1)
        part0 = mine[0]
        a0, b0, part1 = first_side(part0), second_side(part0), around(mine[1], 1)

        a0, b0, part0, part1, amp1, to3 = after((a0, b0, part0, part1, amp1, mine[3]), ())
        q0, a1, b1, part3 = second_side(a0), first_side(part1), second_side(part1), around(to3, 3)
        forms0 = made_forms(part0, a0, b0, q0)

        forms0, part1, a1, b1, part3, to2 = after((forms0, part1, a1, b1, part3, mine[2]), ())
        q1, a3, b3, part2 = second_side(a1), first_side(part3), second_side(part3), around(to2, 2)
        far0 = other_core(forms0)
        forms1 = made_forms(part1, a1, b1, q1)

        forms1, part3, a3, b3, part2, amp1, far0 = after((forms1, part3, a3, b3, part2, amp1, far0), ())
        q3, a2, b2, amp2 = second_side(a3), first_side(part2), second_side(part2), around(amp1, 1)
        far1 = other_core(forms1)
        forms3 = made_forms(part3, a3, b3, q3)

        forms3, part2, a2, b2, amp2, far1 = after((forms3, part2, a2, b2, amp2, far1), ())
        q2, amp3 = second_side(a2), around(amp2, 1)
        far3 = other_core(forms3)
        forms2 = made_forms(part2, a2, b2, q2)

        forms2, amp3, far3 = after((forms2, amp3, far3), ())
        far2 = other_core(forms2)
        amps = prepare_amps([own, amp1, amp2, amp3], blocks_here, jnp.asarray(amp_matrix()))
        held = [forms0, far0, forms1, far1, forms2, far2, forms3, far3]
    else:
        parts = [mine[0]] + [around(mine[by], by) for by in range(1, levels)]
        tiles = amplitudes.reshape(blocks_here, pairs, TV, TV).transpose(0, 3, 2, 1)
        tiles = jnp.pad(tiles, ((0, 0), (0, 0), (0, PAD - TV), (0, 0))).reshape(blocks_here, ROWS, pairs)
        amps = lax.all_gather(tiles, "task", axis=0, axis_index_groups=same_core)
        amps = amps[(level - jnp.arange(levels)) % levels].reshape(levels * blocks_here, ROWS, pairs)
        held = lax.all_gather(jnp.stack(parts), "pair", axis=2, tiled=True)
        held = [jnp.stack([held, other_core(held)], axis=1).reshape(total, depth * pair_count, -1)]
    amps = (amps, other_core(amps))

    ladder = None
    calls = min(levels, 4)
    width = levels // calls
    order = list(reversed(range(calls)))
    for call in order:
        first = call * width
        sums = ladders(first, width, levels, blocks_here, column[None], task_owners, task_local, held, amps, matrix)
        for i in range(width):
            term = (around(sums[i], first + i) if first + i else sums[i]).astype(F32)
            ladder = term if ladder is None else ladder + term
    return residual_in + ladder.transpose(0, 2, 1)


def solution(mesh):
    placed = (P("task", "pair", None), P("task", "pair", None), P("task", "pair", None), P(), P())
    return jax.shard_map(
        per_device, mesh=mesh, in_specs=placed, out_specs=P("task", "pair", None), check_vma=False
    )
```

```python
import functools

import jax
import jax.numpy as jnp
import numpy as np
from jax import lax
from jax.experimental import pallas as pl
from jax.experimental.pallas import tpu as pltpu
from jax.sharding import PartitionSpec as P

TV = 25
PAD = 32
GROUP = 4
LANES = PAD * GROUP
GROUPS = -(-TV // GROUP)
ROWS = TV * PAD
WIDE = GROUPS * LANES
ORDER = [x for g in range(GROUP) for x in range(g, TV, GROUP)]
START = [ORDER.index(g) * PAD for g in range(GROUP)] + [ROWS]
PLACE = np.argsort(ORDER)
PREPARE_STEPS = 2
BF = jnp.bfloat16
F32 = jnp.float32
VMEM_BYTES = 48 * 1024 * 1024


def spread(spots, rows):
    return (np.arange(rows)[:, None] == spots[None, :]).astype(jnp.bfloat16)


def forms_matrix():
    x, y = np.divmod(np.arange(TV * TV), TV)
    return np.concatenate([spread(PLACE[y] * PAD + x, ROWS), spread(x * PAD + y, ROWS)], axis=0)


def amp_matrix():
    c, d = np.divmod(np.arange(TV * TV), TV)
    return spread(d * PAD + c, ROWS)


def prepare_kernel(column_ref, *refs):
    tile_refs, matrix_ref, forms_ref, all_ref = refs[:4], refs[4], refs[5], refs[6]
    count, size, _ = tile_refs[0].shape
    depth = forms_ref.shape[2]

    @pl.when(pl.program_id(0) == 0)
    def _():
        core = lax.rem(column_ref[0], 2)
        for m in range(count):
            for place, ref in zip((0, 1 + core, 2 - core, 3), tile_refs):
                start = pl.multiple_of(m * depth + place * size, size)
                all_ref[pl.ds(start, size), :] = ref[m]

    wide = 2 if depth % LANES == 0 and count % 2 == 0 else 1
    for first in range(0, count, wide):
        made = lax.dot_general(
            matrix_ref[...],
            all_ref[first * depth : (first + wide) * depth, :],
            (((1,), (1,)), ((), ())),
            preferred_element_type=F32,
        ).astype(BF)
        for m in range(wide):
            forms_ref[first + m] = made[:, m * depth : (m + 1) * depth]


def prepare(parts, column, matrix):
    count, size, width = parts[0].shape
    depth = size * len(parts)
    rows = matrix.shape[0] // PREPARE_STEPS
    in_specs = [pl.BlockSpec(part.shape, lambda i, column: (0, 0, 0)) for part in parts]
    in_specs.append(pl.BlockSpec((rows, width), lambda i, column: (i, 0)))
    return pl.pallas_call(
        prepare_kernel,
        out_shape=jax.ShapeDtypeStruct((count, matrix.shape[0], depth), BF),
        grid_spec=pltpu.PrefetchScalarGridSpec(
            num_scalar_prefetch=1,
            grid=(PREPARE_STEPS,),
            in_specs=in_specs,
            out_specs=pl.BlockSpec((count, rows, depth), lambda i, column: (0, i, 0)),
            scratch_shapes=[pltpu.VMEM((count * depth, width), BF)],
        ),
        compiler_params=pltpu.CompilerParams(vmem_limit_bytes=VMEM_BYTES),
        cost_estimate=pl.CostEstimate(
            flops=2 * count * depth * width * matrix.shape[0],
            bytes_accessed=2 * count * depth * (width + matrix.shape[0]),
            transcendentals=0,
        ),
    )(column, *parts, matrix)


def amp_kernel(matrix_ref, *refs):
    tile_refs, out_ref = refs[:-1], refs[-1]
    blocks_here, pairs = out_ref.shape[0] // len(tile_refs), out_ref.shape[2]
    for by, ref in enumerate(tile_refs):
        made = jnp.dot(matrix_ref[...], ref[...], preferred_element_type=F32).astype(BF)
        for m in range(blocks_here):
            out_ref[by * blocks_here + m] = made[:, m * pairs : (m + 1) * pairs]


def prepare_amps(parts, blocks_here, matrix):
    levels, size = len(parts), parts[0].size
    pairs = parts[0].shape[1] // blocks_here
    return pl.pallas_call(
        amp_kernel,
        out_shape=jax.ShapeDtypeStruct((levels * blocks_here, ROWS, pairs), BF),
        compiler_params=pltpu.CompilerParams(vmem_limit_bytes=VMEM_BYTES),
        cost_estimate=pl.CostEstimate(
            flops=2 * levels * size * ROWS, bytes_accessed=4 * levels * size, transcendentals=0
        ),
    )(matrix, *parts)


def turned(ref, groups, by):
    numbers = [min(A * GROUP + (p - by) % GROUP, TV - 1) for A in groups for p in range(GROUP)]
    return jnp.concatenate([ref[x * PAD : (x + 1) * PAD, :] for x in numbers], axis=0)


def ladder_kernel(find, made, sources, column_ref, owners_ref, local_ref, *refs):
    factor_refs, amp_refs, refs = refs[:sources], refs[sources : sources + 2], refs[sources + 2 :]
    matrix_ref, refs = None if made else refs[0], refs[0 if made else 1 :]
    out_ref, v_ref, u_ref, acc_ref, c_buf, r_buf, amp_buf, sems = refs[:8]
    column, columns = pl.program_id(0), pl.num_programs(0)
    step, steps = pl.program_id(1), pl.num_programs(1)
    at = column * steps + step
    slot = at & 1

    def fetch(choices, source, index, part, buffer, to, sem):
        for n, ref in enumerate(choices):

            @pl.when(source == n)
            def _():
                tile = ref.at[index, pl.ds(part * ROWS, ROWS)] if part is not None else ref.at[index]
                pltpu.make_async_copy(tile, buffer.at[to], sem).start()

    def fetch_task(i, j, to):
        places = find(i, j, column_ref, owners_ref, local_ref)
        fetch(factor_refs, *places["col"], 0 if made else None, c_buf, to, sems.at[to, 0])
        fetch(factor_refs, *places["row"], 1 if made else None, r_buf, to, sems.at[to, 1])

    @pl.when(at == 0)
    def _():
        fetch_task(0, 0, 0)

    @pl.when(at + 1 < columns * steps)
    def _():
        last = step == steps - 1
        fetch_task(jnp.where(last, column + 1, column), jnp.where(last, 0, step + 1), 1 - slot)

    @pl.when(step == 0)
    def _():
        acc_ref[...] = jnp.zeros_like(acc_ref)

    here = find(column, step, column_ref, owners_ref, local_ref)
    for core in range(2):

        @pl.when(here["amp"][0] == core)
        def _():
            amp_buf[...] = amp_refs[core][here["amp"][1]]

    for n, buffer in enumerate((c_buf, r_buf)):
        pltpu.make_async_copy(buffer.at[slot], buffer.at[slot], sems.at[slot, n]).wait()
    c_form, r_form, amp_form = c_buf.at[slot], r_buf.at[slot], amp_buf
    if not made:
        forms = refs[8]
        for i, tile in enumerate((c_form, r_form)):
            forms[i] = lax.dot_general(
                matrix_ref[i * ROWS : (i + 1) * ROWS, :],
                tile[...],
                (((1,), (1,)), ((), ())),
                preferred_element_type=F32,
            ).astype(BF)
        c_form, r_form = forms.at[0], forms.at[1]

    spot = lax.broadcasted_iota(jnp.int32, (PAD, LANES), 1) // PAD
    at_spot = [spot == p for p in range(GROUP)]
    nothing = jnp.zeros((PAD, LANES), F32)
    for first in range(0, GROUPS, 2):
        groups = range(first, min(first + 2, GROUPS))
        lanes = slice(groups[0] * LANES, (groups[-1] + 1) * LANES)
        for g in range(GROUP):
            v_ref[START[g] : START[g + 1], lanes] = lax.dot_general(
                c_form[START[g] : START[g + 1], :],
                turned(r_form, groups, g),
                (((1,), (1,)), ((), ())),
                preferred_element_type=F32,
            )
        for A in groups:
            for D in range(GROUPS):
                blocks = [
                    v_ref[START[g] + D * PAD : START[g] + (D + 1) * PAD, A * LANES : (A + 1) * LANES]
                    if D * GROUP + g < TV
                    else nothing
                    for g in range(GROUP)
                ]
                for i in range(min(GROUP, TV - A * GROUP)):
                    block = blocks[-i % GROUP]
                    for p in range(1, GROUP):
                        block = jnp.where(at_spot[p], blocks[(p - i) % GROUP], block)
                    u_ref[START[i] + A * PAD : START[i] + (A + 1) * PAD, D * LANES : (D + 1) * LANES] = block.astype(BF)
    out = local_ref[here["task"], 3]
    for i in range(GROUP):
        acc_ref[out, START[i] : START[i + 1], :] += jnp.dot(
            u_ref[START[i] : START[i + 1], :], turned(amp_form, range(GROUPS), i), preferred_element_type=F32
        )

    @pl.when(step == steps - 1)
    def _():
        for m in range(out_ref.shape[1]):
            rows = [acc_ref[m, PLACE[a] * PAD : PLACE[a] * PAD + TV, :] for a in range(TV)]
            out_ref[0, m] = jnp.concatenate(rows, axis=0).astype(BF)


def ladders(first, columns, levels, blocks_here, column, task_owners, task_local, tiles, amps, matrix):
    tasks = task_owners.shape[0] // (2 * levels)
    pairs = amps[0].shape[2]
    made = tiles[0].shape[1] == 2 * ROWS
    depth = tiles[0].shape[2] if made else tiles[0].shape[1]
    held = (ROWS, depth) if made else tiles[0].shape[1:]

    def find(i, j, column_ref, owners_ref, local_ref):
        level, core = column_ref[0] >> 1, column_ref[0] & 1
        above = level + first + i
        task = (2 * jnp.where(above >= levels, above - levels, above) + core) * tasks + j

        def place(kind):
            owner = owners_ref[task, kind]
            below = level - (owner >> 1)
            below = jnp.where(below < 0, below + levels, below)
            far = (owner & 1) ^ core
            return below, far, local_ref[task, kind]

        def factor(kind):
            below, far, m = place(kind)
            if not made:
                return 0, (below * 2 + far) * blocks_here + m
            return below * 2 + far, m

        below, far, m = place(2)
        return {"task": task, "row": factor(0), "col": factor(1), "amp": (far, below * blocks_here + m)}

    anywhere = pl.BlockSpec(memory_space=pl.ANY)
    operands = [*tiles, *amps]
    in_specs = [anywhere] * len(tiles) + [pl.BlockSpec(memory_space=pltpu.VMEM)] * 2
    scratch = [
        pltpu.VMEM((ROWS, WIDE), F32),
        pltpu.VMEM((ROWS, WIDE), BF),
        pltpu.VMEM((blocks_here, ROWS, pairs), F32),
        pltpu.VMEM((2, *held), BF),
        pltpu.VMEM((2, *held), BF),
        pltpu.VMEM((ROWS, pairs), BF),
        pltpu.SemaphoreType.DMA((2, 2)),
    ]
    if not made:
        in_specs.append(pl.BlockSpec(matrix.shape, lambda i, j, *tables: (0, 0)))
        scratch.append(pltpu.VMEM((2, ROWS, depth), BF))
        operands.append(matrix)
    return pl.pallas_call(
        functools.partial(ladder_kernel, find, made, len(tiles)),
        out_shape=jax.ShapeDtypeStruct((columns, blocks_here, TV * TV, pairs), BF),
        grid_spec=pltpu.PrefetchScalarGridSpec(
            num_scalar_prefetch=3,
            grid=(columns, tasks),
            in_specs=in_specs,
            out_specs=pl.BlockSpec((1, blocks_here, TV * TV, pairs), lambda i, j, *tables: (i, 0, 0, 0)),
            scratch_shapes=scratch,
        ),
        compiler_params=pltpu.CompilerParams(vmem_limit_bytes=VMEM_BYTES),
        cost_estimate=pl.CostEstimate(
            flops=2 * columns * tasks * ROWS * WIDE * (depth + pairs),
            bytes_accessed=2 * columns * tasks * ROWS * 2 * (depth + pairs),
            transcendentals=0,
        ),
    )(column, task_owners, task_local, *operands)


def after(values, done):
    return lax.optimization_barrier((values, done))[0]


def per_device(factor_blocks, amplitudes, residual_in, task_owners, task_local):
    pair_count = lax.axis_size("pair")
    task_count = lax.axis_size("task")
    column = lax.axis_index("task")
    blocks_here, depth_here, _ = factor_blocks.shape
    pairs = amplitudes.shape[1]
    levels = task_count // 2
    level = column // 2
    depth = depth_here // levels
    total = 2 * levels * blocks_here
    matrix = jnp.asarray(forms_matrix())
    other_core = lambda x: lax.ppermute(x, "task", [(c, c ^ 1) for c in range(task_count)])

    def around(x, by):
        return lax.ppermute(x, "task", [(c, (c + 2 * by) % task_count) for c in range(task_count)])

    same_core = [[2 * z + k for z in range(levels)] for k in range(2)]
    slices = factor_blocks.reshape(blocks_here, levels, depth, -1)
    mine = [lax.dynamic_index_in_dim(slices, (level + by) % levels, 1, keepdims=False) for by in range(levels)]
    if pair_count == 4 and levels == 4:
        sides = [
            [(p * task_count + c, (p ^ (1 if c % 2 == turn else 2)) * task_count + c) for p in range(4) for c in range(task_count)]
            for turn in range(2)
        ]
        first_side = lambda x: lax.ppermute(x, ("pair", "task"), sides[0])
        second_side = lambda x: lax.ppermute(x, ("pair", "task"), sides[1])
        made_forms = lambda *parts: prepare(parts, column[None], matrix)
        own = amplitudes.transpose(2, 0, 1).reshape(TV * TV, blocks_here * pairs)
        amp1 = around(own, 1)
        part0 = mine[0]
        a0, b0, part1 = first_side(part0), second_side(part0), around(mine[1], 1)

        a0, b0, part0, part1, amp1, to2 = after((a0, b0, part0, part1, amp1, mine[2]), ())
        q0, a1, b1, part2 = second_side(a0), first_side(part1), second_side(part1), around(to2, 2)
        forms0 = made_forms(part0, a0, b0, q0)

        forms0, part1, a1, b1, part2, to3 = after((forms0, part1, a1, b1, part2, mine[3]), ())
        q1, a2, b2, part3 = second_side(a1), first_side(part2), second_side(part2), around(to3, 3)
        far0 = other_core(forms0)
        forms1 = made_forms(part1, a1, b1, q1)

        forms1, part2, a2, b2, part3, amp1, far0 = after((forms1, part2, a2, b2, part3, amp1, far0), ())
        q2, a3, b3, amp2 = second_side(a2), first_side(part3), second_side(part3), around(amp1, 1)
        far1 = other_core(forms1)
        forms2 = made_forms(part2, a2, b2, q2)

        forms2, part3, a3, b3, amp2, far1 = after((forms2, part3, a3, b3, amp2, far1), ())
        q3, amp3 = second_side(a3), around(amp2, 1)
        far2 = other_core(forms2)
        forms3 = made_forms(part3, a3, b3, q3)

        forms3, amp3, far2 = after((forms3, amp3, far2), ())
        far3 = other_core(forms3)
        amps = prepare_amps([own, amp1, amp2, amp3], blocks_here, jnp.asarray(amp_matrix()))
        held = [forms0, far0, forms1, far1, forms2, far2, forms3, far3]
    else:
        parts = [mine[0]] + [around(mine[by], by) for by in range(1, levels)]
        tiles = amplitudes.reshape(blocks_here, pairs, TV, TV).transpose(0, 3, 2, 1)
        tiles = jnp.pad(tiles, ((0, 0), (0, 0), (0, PAD - TV), (0, 0))).reshape(blocks_here, ROWS, pairs)
        amps = lax.all_gather(tiles, "task", axis=0, axis_index_groups=same_core)
        amps = amps[(level - jnp.arange(levels)) % levels].reshape(levels * blocks_here, ROWS, pairs)
        held = lax.all_gather(jnp.stack(parts), "pair", axis=2, tiled=True)
        held = [jnp.stack([held, other_core(held)], axis=1).reshape(total, depth * pair_count, -1)]
    amps = (amps, other_core(amps))

    ladder = None
    calls = min(levels, 4)
    width = levels // calls
    order = list(reversed(range(calls)))
    for call in order:
        first = call * width
        sums = ladders(first, width, levels, blocks_here, column[None], task_owners, task_local, held, amps, matrix)
        for i in range(width):
            term = (around(sums[i], first + i) if first + i else sums[i]).astype(F32)
            ladder = term if ladder is None else ladder + term
    return residual_in + ladder.transpose(0, 2, 1)


def solution(mesh):
    placed = (P("task", "pair", None), P("task", "pair", None), P("task", "pair", None), P(), P())
    return jax.shard_map(
        per_device, mesh=mesh, in_specs=placed, out_specs=P("task", "pair", None), check_vma=False
    )
```

```python
import functools

import jax
import jax.numpy as jnp
import numpy as np
from jax import lax
from jax.experimental import pallas as pl
from jax.experimental.pallas import tpu as pltpu
from jax.sharding import PartitionSpec as P

TV = 25
PAD = 32
GROUP = 4
LANES = PAD * GROUP
GROUPS = -(-TV // GROUP)
ROWS = TV * PAD
WIDE = GROUPS * LANES
ORDER = [x for g in range(GROUP) for x in range(g, TV, GROUP)]
START = [ORDER.index(g) * PAD for g in range(GROUP)] + [ROWS]
PLACE = np.argsort(ORDER)
PREPARE_STEPS = 2
BF = jnp.bfloat16
F32 = jnp.float32
VMEM_BYTES = 48 * 1024 * 1024


def spread(spots, rows):
    return (np.arange(rows)[:, None] == spots[None, :]).astype(jnp.bfloat16)


def forms_matrix():
    x, y = np.divmod(np.arange(TV * TV), TV)
    return np.concatenate([spread(PLACE[y] * PAD + x, ROWS), spread(x * PAD + y, ROWS)], axis=0)


def amp_matrix():
    c, d = np.divmod(np.arange(TV * TV), TV)
    return spread(d * PAD + c, ROWS)


def prepare_kernel(column_ref, *refs):
    tile_refs, matrix_ref, forms_ref, all_ref = refs[:4], refs[4], refs[5], refs[6]
    count, size, _ = tile_refs[0].shape
    depth = forms_ref.shape[2]

    @pl.when(pl.program_id(0) == 0)
    def _():
        core = lax.rem(column_ref[0], 2)
        for m in range(count):
            for place, ref in zip((0, 1 + core, 2 - core, 3), tile_refs):
                start = pl.multiple_of(m * depth + place * size, size)
                all_ref[pl.ds(start, size), :] = ref[m]

    wide = 2 if depth % LANES == 0 and count % 2 == 0 else 1
    for first in range(0, count, wide):
        made = lax.dot_general(
            matrix_ref[...],
            all_ref[first * depth : (first + wide) * depth, :],
            (((1,), (1,)), ((), ())),
            preferred_element_type=F32,
        ).astype(BF)
        for m in range(wide):
            forms_ref[first + m] = made[:, m * depth : (m + 1) * depth]


def prepare(parts, column, matrix):
    count, size, width = parts[0].shape
    depth = size * len(parts)
    rows = matrix.shape[0] // PREPARE_STEPS
    in_specs = [pl.BlockSpec(part.shape, lambda i, column: (0, 0, 0)) for part in parts]
    in_specs.append(pl.BlockSpec((rows, width), lambda i, column: (i, 0)))
    return pl.pallas_call(
        prepare_kernel,
        out_shape=jax.ShapeDtypeStruct((count, matrix.shape[0], depth), BF),
        grid_spec=pltpu.PrefetchScalarGridSpec(
            num_scalar_prefetch=1,
            grid=(PREPARE_STEPS,),
            in_specs=in_specs,
            out_specs=pl.BlockSpec((count, rows, depth), lambda i, column: (0, i, 0)),
            scratch_shapes=[pltpu.VMEM((count * depth, width), BF)],
        ),
        compiler_params=pltpu.CompilerParams(vmem_limit_bytes=VMEM_BYTES),
        cost_estimate=pl.CostEstimate(
            flops=2 * count * depth * width * matrix.shape[0],
            bytes_accessed=2 * count * depth * (width + matrix.shape[0]),
            transcendentals=0,
        ),
    )(column, *parts, matrix)


def amp_kernel(matrix_ref, *refs):
    tile_refs, out_ref = refs[:-1], refs[-1]
    blocks_here, pairs = out_ref.shape[0] // len(tile_refs), out_ref.shape[2]
    for by, ref in enumerate(tile_refs):
        made = jnp.dot(matrix_ref[...], ref[...], preferred_element_type=F32).astype(BF)
        for m in range(blocks_here):
            out_ref[by * blocks_here + m] = made[:, m * pairs : (m + 1) * pairs]


def prepare_amps(parts, blocks_here, matrix):
    levels, size = len(parts), parts[0].size
    pairs = parts[0].shape[1] // blocks_here
    return pl.pallas_call(
        amp_kernel,
        out_shape=jax.ShapeDtypeStruct((levels * blocks_here, ROWS, pairs), BF),
        compiler_params=pltpu.CompilerParams(vmem_limit_bytes=VMEM_BYTES),
        cost_estimate=pl.CostEstimate(
            flops=2 * levels * size * ROWS, bytes_accessed=4 * levels * size, transcendentals=0
        ),
    )(matrix, *parts)


def turned(ref, groups, by):
    numbers = [min(A * GROUP + (p - by) % GROUP, TV - 1) for A in groups for p in range(GROUP)]
    return jnp.concatenate([ref[x * PAD : (x + 1) * PAD, :] for x in numbers], axis=0)


def ladder_kernel(find, made, sources, column_ref, owners_ref, local_ref, *refs):
    factor_refs, amp_refs, refs = refs[:sources], refs[sources : sources + 2], refs[sources + 2 :]
    matrix_ref, refs = None if made else refs[0], refs[0 if made else 1 :]
    out_ref, v_ref, u_ref, acc_ref, c_buf, r_buf, amp_buf, sems = refs[:8]
    column, columns = pl.program_id(0), pl.num_programs(0)
    step, steps = pl.program_id(1), pl.num_programs(1)
    at = column * steps + step
    slot = at & 1

    def fetch(choices, source, index, part, buffer, to, sem):
        for n, ref in enumerate(choices):

            @pl.when(source == n)
            def _():
                tile = ref.at[index, pl.ds(part * ROWS, ROWS)] if part is not None else ref.at[index]
                pltpu.make_async_copy(tile, buffer.at[to], sem).start()

    def fetch_task(i, j, to):
        places = find(i, j, column_ref, owners_ref, local_ref)
        fetch(factor_refs, *places["col"], 0 if made else None, c_buf, to, sems.at[to, 0])
        fetch(factor_refs, *places["row"], 1 if made else None, r_buf, to, sems.at[to, 1])

    @pl.when(at == 0)
    def _():
        fetch_task(0, 0, 0)

    @pl.when(at + 1 < columns * steps)
    def _():
        last = step == steps - 1
        fetch_task(jnp.where(last, column + 1, column), jnp.where(last, 0, step + 1), 1 - slot)

    @pl.when(step == 0)
    def _():
        acc_ref[...] = jnp.zeros_like(acc_ref)

    here = find(column, step, column_ref, owners_ref, local_ref)
    for core in range(2):

        @pl.when(here["amp"][0] == core)
        def _():
            amp_buf[...] = amp_refs[core][here["amp"][1]]

    for n, buffer in enumerate((c_buf, r_buf)):
        pltpu.make_async_copy(buffer.at[slot], buffer.at[slot], sems.at[slot, n]).wait()
    c_form, r_form, amp_form = c_buf.at[slot], r_buf.at[slot], amp_buf
    if not made:
        forms = refs[8]
        for i, tile in enumerate((c_form, r_form)):
            forms[i] = lax.dot_general(
                matrix_ref[i * ROWS : (i + 1) * ROWS, :],
                tile[...],
                (((1,), (1,)), ((), ())),
                preferred_element_type=F32,
            ).astype(BF)
        c_form, r_form = forms.at[0], forms.at[1]

    spot = lax.broadcasted_iota(jnp.int32, (PAD, LANES), 1) // PAD
    at_spot = [spot == p for p in range(GROUP)]
    nothing = jnp.zeros((PAD, LANES), F32)
    for first in range(0, GROUPS, 2):
        groups = range(first, min(first + 2, GROUPS))
        lanes = slice(groups[0] * LANES, (groups[-1] + 1) * LANES)
        for g in range(GROUP):
            v_ref[START[g] : START[g + 1], lanes] = lax.dot_general(
                c_form[START[g] : START[g + 1], :],
                turned(r_form, groups, g),
                (((1,), (1,)), ((), ())),
                preferred_element_type=F32,
            )
        for A in groups:
            for D in range(GROUPS):
                blocks = [
                    v_ref[START[g] + D * PAD : START[g] + (D + 1) * PAD, A * LANES : (A + 1) * LANES]
                    if D * GROUP + g < TV
                    else nothing
                    for g in range(GROUP)
                ]
                for i in range(min(GROUP, TV - A * GROUP)):
                    block = blocks[-i % GROUP]
                    for p in range(1, GROUP):
                        block = jnp.where(at_spot[p], blocks[(p - i) % GROUP], block)
                    u_ref[START[i] + A * PAD : START[i] + (A + 1) * PAD, D * LANES : (D + 1) * LANES] = block.astype(BF)
    out = local_ref[here["task"], 3]
    for i in range(GROUP):
        acc_ref[out, START[i] : START[i + 1], :] += jnp.dot(
            u_ref[START[i] : START[i + 1], :], turned(amp_form, range(GROUPS), i), preferred_element_type=F32
        )

    @pl.when(step == steps - 1)
    def _():
        for m in range(out_ref.shape[1]):
            rows = [acc_ref[m, PLACE[a] * PAD : PLACE[a] * PAD + TV, :] for a in range(TV)]
            out_ref[0, m] = jnp.concatenate(rows, axis=0).astype(BF)


def ladders(first, columns, levels, blocks_here, column, task_owners, task_local, tiles, amps, matrix):
    tasks = task_owners.shape[0] // (2 * levels)
    pairs = amps[0].shape[2]
    made = tiles[0].shape[1] == 2 * ROWS
    depth = tiles[0].shape[2] if made else tiles[0].shape[1]
    held = (ROWS, depth) if made else tiles[0].shape[1:]

    def find(i, j, column_ref, owners_ref, local_ref):
        level, core = column_ref[0] >> 1, column_ref[0] & 1
        above = level + first + i
        task = (2 * jnp.where(above >= levels, above - levels, above) + core) * tasks + j

        def place(kind):
            owner = owners_ref[task, kind]
            below = level - (owner >> 1)
            below = jnp.where(below < 0, below + levels, below)
            far = (owner & 1) ^ core
            return below, far, local_ref[task, kind]

        def factor(kind):
            below, far, m = place(kind)
            if not made:
                return 0, (below * 2 + far) * blocks_here + m
            return below * 2 + far, m

        below, far, m = place(2)
        return {"task": task, "row": factor(0), "col": factor(1), "amp": (far, below * blocks_here + m)}

    anywhere = pl.BlockSpec(memory_space=pl.ANY)
    operands = [*tiles, *amps]
    in_specs = [anywhere] * len(tiles) + [pl.BlockSpec(memory_space=pltpu.VMEM)] * 2
    scratch = [
        pltpu.VMEM((ROWS, WIDE), F32),
        pltpu.VMEM((ROWS, WIDE), BF),
        pltpu.VMEM((blocks_here, ROWS, pairs), F32),
        pltpu.VMEM((2, *held), BF),
        pltpu.VMEM((2, *held), BF),
        pltpu.VMEM((ROWS, pairs), BF),
        pltpu.SemaphoreType.DMA((2, 2)),
    ]
    if not made:
        in_specs.append(pl.BlockSpec(matrix.shape, lambda i, j, *tables: (0, 0)))
        scratch.append(pltpu.VMEM((2, ROWS, depth), BF))
        operands.append(matrix)
    return pl.pallas_call(
        functools.partial(ladder_kernel, find, made, len(tiles)),
        out_shape=jax.ShapeDtypeStruct((columns, blocks_here, TV * TV, pairs), BF),
        grid_spec=pltpu.PrefetchScalarGridSpec(
            num_scalar_prefetch=3,
            grid=(columns, tasks),
            in_specs=in_specs,
            out_specs=pl.BlockSpec((1, blocks_here, TV * TV, pairs), lambda i, j, *tables: (i, 0, 0, 0)),
            scratch_shapes=scratch,
        ),
        compiler_params=pltpu.CompilerParams(vmem_limit_bytes=VMEM_BYTES),
        cost_estimate=pl.CostEstimate(
            flops=2 * columns * tasks * ROWS * WIDE * (depth + pairs),
            bytes_accessed=2 * columns * tasks * ROWS * 2 * (depth + pairs),
            transcendentals=0,
        ),
    )(column, task_owners, task_local, *operands)


def after(values, done):
    return lax.optimization_barrier((values, done))[0]


def per_device(factor_blocks, amplitudes, residual_in, task_owners, task_local):
    pair_count = lax.axis_size("pair")
    task_count = lax.axis_size("task")
    column = lax.axis_index("task")
    blocks_here, depth_here, _ = factor_blocks.shape
    pairs = amplitudes.shape[1]
    levels = task_count // 2
    level = column // 2
    depth = depth_here // levels
    total = 2 * levels * blocks_here
    matrix = jnp.asarray(forms_matrix())
    other_core = lambda x: lax.ppermute(x, "task", [(c, c ^ 1) for c in range(task_count)])

    def around(x, by):
        return lax.ppermute(x, "task", [(c, (c + 2 * by) % task_count) for c in range(task_count)])

    same_core = [[2 * z + k for z in range(levels)] for k in range(2)]
    slices = factor_blocks.reshape(blocks_here, levels, depth, -1)
    mine = [lax.dynamic_index_in_dim(slices, (level + by) % levels, 1, keepdims=False) for by in range(levels)]
    if pair_count == 4 and levels == 4:
        sides = [
            [(p * task_count + c, (p ^ (1 if c % 2 == turn else 2)) * task_count + c) for p in range(4) for c in range(task_count)]
            for turn in range(2)
        ]
        first_side = lambda x: lax.ppermute(x, ("pair", "task"), sides[0])
        second_side = lambda x: lax.ppermute(x, ("pair", "task"), sides[1])
        made_forms = lambda *parts: prepare(parts, column[None], matrix)
        own = amplitudes.transpose(2, 0, 1).reshape(TV * TV, blocks_here * pairs)
        amp1 = around(own, 1)
        part0 = mine[0]
        a0, b0, part1 = first_side(part0), second_side(part0), around(mine[1], 1)

        a0, b0, part0, part1, amp1, to2 = after((a0, b0, part0, part1, amp1, mine[2]), ())
        q0, a1, b1, part2 = second_side(a0), first_side(part1), second_side(part1), around(to2, 2)
        forms0 = made_forms(part0, a0, b0, q0)

        forms0, part1, a1, b1, part2, to3 = after((forms0, part1, a1, b1, part2, mine[3]), ())
        q1, a2, b2, part3 = second_side(a1), first_side(part2), second_side(part2), around(to3, 3)
        far0 = other_core(forms0)
        q1, amp1 = after((q1, amp1), ())
        amp2 = around(amp1, 1)
        forms1 = made_forms(part1, a1, b1, q1)

        forms1, part2, a2, b2, part3, amp2, far0 = after((forms1, part2, a2, b2, part3, amp2, far0), ())
        q2, a3, b3, amp3 = second_side(a2), first_side(part3), second_side(part3), around(amp2, 1)
        far1 = other_core(forms1)
        forms2 = made_forms(part2, a2, b2, q2)

        forms2, part3, a3, b3, amp3, far1 = after((forms2, part3, a3, b3, amp3, far1), ())
        q3, far2 = second_side(a3), other_core(forms2)
        far_parts = [other_core(x) for x in (part3, a3, b3, q3)]
        amps = prepare_amps([own, amp1, amp2, amp3], blocks_here, jnp.asarray(amp_matrix()))
        forms3 = made_forms(part3, a3, b3, q3)
        far3 = prepare(far_parts, (column ^ 1)[None], matrix)
        held = [forms0, far0, forms1, far1, forms2, far2, forms3, far3]
    else:
        parts = [mine[0]] + [around(mine[by], by) for by in range(1, levels)]
        tiles = amplitudes.reshape(blocks_here, pairs, TV, TV).transpose(0, 3, 2, 1)
        tiles = jnp.pad(tiles, ((0, 0), (0, 0), (0, PAD - TV), (0, 0))).reshape(blocks_here, ROWS, pairs)
        amps = lax.all_gather(tiles, "task", axis=0, axis_index_groups=same_core)
        amps = amps[(level - jnp.arange(levels)) % levels].reshape(levels * blocks_here, ROWS, pairs)
        held = lax.all_gather(jnp.stack(parts), "pair", axis=2, tiled=True)
        held = [jnp.stack([held, other_core(held)], axis=1).reshape(total, depth * pair_count, -1)]
    amps = (amps, other_core(amps))

    ladder = None
    calls = min(levels, 4)
    width = levels // calls
    order = list(reversed(range(calls)))
    for call in order:
        first = call * width
        sums = ladders(first, width, levels, blocks_here, column[None], task_owners, task_local, held, amps, matrix)
        for i in range(width):
            term = (around(sums[i], first + i) if first + i else sums[i]).astype(F32)
            ladder = term if ladder is None else ladder + term
    return residual_in + ladder.transpose(0, 2, 1)


def solution(mesh):
    placed = (P("task", "pair", None), P("task", "pair", None), P("task", "pair", None), P(), P())
    return jax.shard_map(
        per_device, mesh=mesh, in_specs=placed, out_specs=P("task", "pair", None), check_vma=False
    )
```

```python
import functools

import jax
import jax.numpy as jnp
import numpy as np
from jax import lax
from jax.experimental import pallas as pl
from jax.experimental.pallas import tpu as pltpu
from jax.sharding import PartitionSpec as P

TV = 25
PAD = 32
GROUP = 4
LANES = PAD * GROUP
GROUPS = -(-TV // GROUP)
ROWS = TV * PAD
WIDE = GROUPS * LANES
ORDER = [x for g in range(GROUP) for x in range(g, TV, GROUP)]
START = [ORDER.index(g) * PAD for g in range(GROUP)] + [ROWS]
PLACE = np.argsort(ORDER)
PREPARE_STEPS = 2
BF = jnp.bfloat16
F32 = jnp.float32
VMEM_BYTES = 48 * 1024 * 1024


def spread(spots, rows):
    return (np.arange(rows)[:, None] == spots[None, :]).astype(jnp.bfloat16)


def forms_matrix():
    x, y = np.divmod(np.arange(TV * TV), TV)
    return np.concatenate([spread(PLACE[y] * PAD + x, ROWS), spread(x * PAD + y, ROWS)], axis=0)


def amp_matrix():
    c, d = np.divmod(np.arange(TV * TV), TV)
    return spread(d * PAD + c, ROWS)


def prepare_kernel(column_ref, *refs):
    tile_refs, matrix_ref, forms_ref, all_ref = refs[:4], refs[4], refs[5], refs[6]
    count, size, _ = tile_refs[0].shape
    depth = forms_ref.shape[2]

    @pl.when(pl.program_id(0) == 0)
    def _():
        core = lax.rem(column_ref[0], 2)
        for m in range(count):
            for place, ref in zip((0, 1 + core, 2 - core, 3), tile_refs):
                start = pl.multiple_of(m * depth + place * size, size)
                all_ref[pl.ds(start, size), :] = ref[m]

    wide = 2 if depth % LANES == 0 and count % 2 == 0 else 1
    for first in range(0, count, wide):
        made = lax.dot_general(
            matrix_ref[...],
            all_ref[first * depth : (first + wide) * depth, :],
            (((1,), (1,)), ((), ())),
            preferred_element_type=F32,
        ).astype(BF)
        for m in range(wide):
            forms_ref[first + m] = made[:, m * depth : (m + 1) * depth]


def prepare(parts, column, matrix):
    count, size, width = parts[0].shape
    depth = size * len(parts)
    rows = matrix.shape[0] // PREPARE_STEPS
    in_specs = [pl.BlockSpec(part.shape, lambda i, column: (0, 0, 0)) for part in parts]
    in_specs.append(pl.BlockSpec((rows, width), lambda i, column: (i, 0)))
    return pl.pallas_call(
        prepare_kernel,
        out_shape=jax.ShapeDtypeStruct((count, matrix.shape[0], depth), BF),
        grid_spec=pltpu.PrefetchScalarGridSpec(
            num_scalar_prefetch=1,
            grid=(PREPARE_STEPS,),
            in_specs=in_specs,
            out_specs=pl.BlockSpec((count, rows, depth), lambda i, column: (0, i, 0)),
            scratch_shapes=[pltpu.VMEM((count * depth, width), BF)],
        ),
        compiler_params=pltpu.CompilerParams(vmem_limit_bytes=VMEM_BYTES),
        cost_estimate=pl.CostEstimate(
            flops=2 * count * depth * width * matrix.shape[0],
            bytes_accessed=2 * count * depth * (width + matrix.shape[0]),
            transcendentals=0,
        ),
    )(column, *parts, matrix)


def amp_kernel(matrix_ref, *refs):
    tile_refs, out_ref = refs[:-1], refs[-1]
    blocks_here, pairs = out_ref.shape[0] // len(tile_refs), out_ref.shape[2]
    for by, ref in enumerate(tile_refs):
        made = jnp.dot(matrix_ref[...], ref[...], preferred_element_type=F32).astype(BF)
        for m in range(blocks_here):
            out_ref[by * blocks_here + m] = made[:, m * pairs : (m + 1) * pairs]


def prepare_amps(parts, blocks_here, matrix):
    levels, size = len(parts), parts[0].size
    pairs = parts[0].shape[1] // blocks_here
    return pl.pallas_call(
        amp_kernel,
        out_shape=jax.ShapeDtypeStruct((levels * blocks_here, ROWS, pairs), BF),
        compiler_params=pltpu.CompilerParams(vmem_limit_bytes=VMEM_BYTES),
        cost_estimate=pl.CostEstimate(
            flops=2 * levels * size * ROWS, bytes_accessed=4 * levels * size, transcendentals=0
        ),
    )(matrix, *parts)


def turned(ref, groups, by):
    numbers = [min(A * GROUP + (p - by) % GROUP, TV - 1) for A in groups for p in range(GROUP)]
    return jnp.concatenate([ref[x * PAD : (x + 1) * PAD, :] for x in numbers], axis=0)


def pick_blocks(blocks, low, even):
    b0, b1, b2, b3 = blocks
    x, y = jnp.where(low, b0, b2), jnp.where(low, b2, b0)
    z, w = jnp.where(low, b1, b3), jnp.where(low, b3, b1)
    return jnp.where(even, x, z), jnp.where(even, w, x), jnp.where(even, y, w), jnp.where(even, z, y)


def ladder_kernel(find, made, sources, column_ref, owners_ref, local_ref, *refs):
    factors, both = sources
    factor_refs, amp_refs, refs = refs[:factors], refs[factors:both], refs[both:]
    matrix_ref, refs = None if made else refs[0], refs[0 if made else 1 :]
    out_ref, v_ref, u_ref, acc_ref, c_buf, r_buf, amp_buf, sems = refs[:8]
    column, columns = pl.program_id(0), pl.num_programs(0)
    step, steps = pl.program_id(1), pl.num_programs(1)
    at = column * steps + step
    slot = at & 1

    def fetch(choices, source, index, part, buffer, to, sem):
        for n, ref in enumerate(choices):

            @pl.when(source == n)
            def _():
                tile = ref.at[index, pl.ds(part * ROWS, ROWS)] if part is not None else ref.at[index]
                pltpu.make_async_copy(tile, buffer.at[to], sem).start()

    def fetch_task(i, j, to):
        places = find(i, j, column_ref, owners_ref, local_ref)
        fetch(factor_refs, *places["col"], 0 if made else None, c_buf, to, sems.at[to, 0])
        fetch(factor_refs, *places["row"], 1 if made else None, r_buf, to, sems.at[to, 1])

    @pl.when(at == 0)
    def _():
        fetch_task(0, 0, 0)

    @pl.when(at + 1 < columns * steps)
    def _():
        last = step == steps - 1
        fetch_task(jnp.where(last, column + 1, column), jnp.where(last, 0, step + 1), 1 - slot)

    @pl.when(step == 0)
    def _():
        acc_ref[...] = jnp.zeros_like(acc_ref)

    here = find(column, step, column_ref, owners_ref, local_ref)
    for n, ref in enumerate(amp_refs):

        @pl.when(here["amp"][0] == n)
        def _():
            amp_buf[...] = ref[here["amp"][1]]

    for n, buffer in enumerate((c_buf, r_buf)):
        pltpu.make_async_copy(buffer.at[slot], buffer.at[slot], sems.at[slot, n]).wait()
    c_form, r_form, amp_form = c_buf.at[slot], r_buf.at[slot], amp_buf
    if not made:
        forms = refs[8]
        for i, tile in enumerate((c_form, r_form)):
            forms[i] = lax.dot_general(
                matrix_ref[i * ROWS : (i + 1) * ROWS, :],
                tile[...],
                (((1,), (1,)), ((), ())),
                preferred_element_type=F32,
            ).astype(BF)
        c_form, r_form = forms.at[0], forms.at[1]

    spot = lax.broadcasted_iota(jnp.int32, (PAD, LANES), 1) // PAD
    low, even = spot < 2, spot % 2 == 0
    nothing = jnp.zeros((PAD, LANES), F32)
    for first in range(0, GROUPS, 2):
        groups = range(first, min(first + 2, GROUPS))
        lanes = slice(groups[0] * LANES, (groups[-1] + 1) * LANES)
        for g in range(GROUP):
            v_ref[START[g] : START[g + 1], lanes] = lax.dot_general(
                c_form[START[g] : START[g + 1], :],
                turned(r_form, groups, g),
                (((1,), (1,)), ((), ())),
                preferred_element_type=F32,
            )
        for A in groups:
            for D in range(GROUPS):
                blocks = [
                    v_ref[START[g] + D * PAD : START[g] + (D + 1) * PAD, A * LANES : (A + 1) * LANES]
                    if D * GROUP + g < TV
                    else nothing
                    for g in range(GROUP)
                ]
                for i, block in enumerate(pick_blocks(blocks, low, even)[: TV - A * GROUP]):
                    u_ref[START[i] + A * PAD : START[i] + (A + 1) * PAD, D * LANES : (D + 1) * LANES] = block.astype(BF)
    out = local_ref[here["task"], 3]
    for i in range(GROUP):
        acc_ref[out, START[i] : START[i + 1], :] += jnp.dot(
            u_ref[START[i] : START[i + 1], :], turned(amp_form, range(GROUPS), i), preferred_element_type=F32
        )

    @pl.when(step == steps - 1)
    def _():
        for m in range(out_ref.shape[1]):
            rows = [acc_ref[m, PLACE[a] * PAD : PLACE[a] * PAD + TV, :] for a in range(TV)]
            out_ref[0, m] = jnp.concatenate(rows, axis=0).astype(BF)


def ladders(first, columns, levels, blocks_here, column, task_owners, task_local, tiles, amps, matrix):
    tasks = task_owners.shape[0] // (2 * levels)
    pairs = amps[0].shape[2]
    made = tiles[0].shape[1] == 2 * ROWS
    depth = tiles[0].shape[2] if made else tiles[0].shape[1]
    held = (ROWS, depth) if made else tiles[0].shape[1:]

    def find(i, j, column_ref, owners_ref, local_ref):
        level, core = column_ref[0] >> 1, column_ref[0] & 1
        above = level + first + i
        task = (2 * jnp.where(above >= levels, above - levels, above) + core) * tasks + j

        def place(kind):
            owner = owners_ref[task, kind]
            below = level - (owner >> 1)
            below = jnp.where(below < 0, below + levels, below)
            far = (owner & 1) ^ core
            return below, far, local_ref[task, kind]

        def factor(kind):
            below, far, m = place(kind)
            if not made:
                return 0, (below * 2 + far) * blocks_here + m
            return below * 2 + far, m

        below, far, m = place(2)
        if len(amps) == 4:
            amp = ((below >> 1) * 2 + far, (below & 1) * blocks_here + m)
        else:
            amp = (far, below * blocks_here + m)
        return {"task": task, "row": factor(0), "col": factor(1), "amp": amp}

    anywhere = pl.BlockSpec(memory_space=pl.ANY)
    operands = [*tiles, *amps]
    in_specs = [anywhere] * len(tiles) + [pl.BlockSpec(memory_space=pltpu.VMEM)] * len(amps)
    scratch = [
        pltpu.VMEM((ROWS, WIDE), F32),
        pltpu.VMEM((ROWS, WIDE), BF),
        pltpu.VMEM((blocks_here, ROWS, pairs), F32),
        pltpu.VMEM((2, *held), BF),
        pltpu.VMEM((2, *held), BF),
        pltpu.VMEM((ROWS, pairs), BF),
        pltpu.SemaphoreType.DMA((2, 2)),
    ]
    if not made:
        in_specs.append(pl.BlockSpec(matrix.shape, lambda i, j, *tables: (0, 0)))
        scratch.append(pltpu.VMEM((2, ROWS, depth), BF))
        operands.append(matrix)
    return pl.pallas_call(
        functools.partial(ladder_kernel, find, made, (len(tiles), len(tiles) + len(amps))),
        out_shape=jax.ShapeDtypeStruct((columns, blocks_here, TV * TV, pairs), BF),
        grid_spec=pltpu.PrefetchScalarGridSpec(
            num_scalar_prefetch=3,
            grid=(columns, tasks),
            in_specs=in_specs,
            out_specs=pl.BlockSpec((1, blocks_here, TV * TV, pairs), lambda i, j, *tables: (i, 0, 0, 0)),
            scratch_shapes=scratch,
        ),
        compiler_params=pltpu.CompilerParams(vmem_limit_bytes=VMEM_BYTES),
        cost_estimate=pl.CostEstimate(
            flops=2 * columns * tasks * ROWS * WIDE * (depth + pairs),
            bytes_accessed=2 * columns * tasks * ROWS * 2 * (depth + pairs),
            transcendentals=0,
        ),
    )(column, task_owners, task_local, *operands)


def after(values, done):
    return lax.optimization_barrier((values, done))[0]


def per_device(factor_blocks, amplitudes, residual_in, task_owners, task_local):
    pair_count = lax.axis_size("pair")
    task_count = lax.axis_size("task")
    column = lax.axis_index("task")
    blocks_here, depth_here, _ = factor_blocks.shape
    pairs = amplitudes.shape[1]
    levels = task_count // 2
    level = column // 2
    depth = depth_here // levels
    total = 2 * levels * blocks_here
    matrix = jnp.asarray(forms_matrix())
    other_core = lambda x: lax.ppermute(x, "task", [(c, c ^ 1) for c in range(task_count)])

    def around(x, by):
        return lax.ppermute(x, "task", [(c, (c + 2 * by) % task_count) for c in range(task_count)])

    same_core = [[2 * z + k for z in range(levels)] for k in range(2)]
    slices = factor_blocks.reshape(blocks_here, levels, depth, -1)
    mine = [lax.dynamic_index_in_dim(slices, (level + by) % levels, 1, keepdims=False) for by in range(levels)]
    if pair_count == 4 and levels == 4:
        sides = [
            [(p * task_count + c, (p ^ (1 if c % 2 == turn else 2)) * task_count + c) for p in range(4) for c in range(task_count)]
            for turn in range(2)
        ]
        first_side = lambda x: lax.ppermute(x, ("pair", "task"), sides[0])
        second_side = lambda x: lax.ppermute(x, ("pair", "task"), sides[1])
        made_forms = lambda *parts: prepare(parts, column[None], matrix)
        own = amplitudes.transpose(2, 0, 1).reshape(TV * TV, blocks_here * pairs)
        amp_rows = jnp.asarray(amp_matrix())
        amp1 = around(own, 1)
        part0 = mine[0]
        a0, b0, part1 = first_side(part0), second_side(part0), around(mine[1], 1)

        a0, b0, part0, part1, amp1, to2 = after((a0, b0, part0, part1, amp1, mine[2]), ())
        q0, a1, b1, part2 = second_side(a0), first_side(part1), second_side(part1), around(to2, 2)
        forms0 = made_forms(part0, a0, b0, q0)

        forms0, part1, a1, b1, part2, to3 = after((forms0, part1, a1, b1, part2, mine[3]), ())
        q1, a2, b2, part3 = second_side(a1), first_side(part2), second_side(part2), around(to3, 3)
        far0 = other_core(forms0)
        forms1 = made_forms(part1, a1, b1, q1)

        forms1, part2, a2, b2, part3, amp1, far0 = after((forms1, part2, a2, b2, part3, amp1, far0), ())
        q2, a3, b3, amp2 = second_side(a2), first_side(part3), second_side(part3), around(amp1, 1)
        far1 = other_core(forms1)
        forms2 = made_forms(part2, a2, b2, q2)
        near = prepare_amps([own, amp1], blocks_here, amp_rows)

        forms2, part3, a3, b3, amp2, far1, near = after((forms2, part3, a3, b3, amp2, far1, near), ())
        q3, amp3 = second_side(a3), around(amp2, 1)
        far2, far_near = other_core(forms2), other_core(near)
        forms3 = made_forms(part3, a3, b3, q3)

        forms3, amp3, far2, far_near = after((forms3, amp3, far2, far_near), ())
        far3 = other_core(forms3)
        rest = prepare_amps([amp2, amp3], blocks_here, amp_rows)
        amps = [near, far_near, rest, other_core(rest)]
        held = [forms0, far0, forms1, far1, forms2, far2, forms3, far3]
    else:
        parts = [mine[0]] + [around(mine[by], by) for by in range(1, levels)]
        tiles = amplitudes.reshape(blocks_here, pairs, TV, TV).transpose(0, 3, 2, 1)
        tiles = jnp.pad(tiles, ((0, 0), (0, 0), (0, PAD - TV), (0, 0))).reshape(blocks_here, ROWS, pairs)
        amps = lax.all_gather(tiles, "task", axis=0, axis_index_groups=same_core)
        amps = amps[(level - jnp.arange(levels)) % levels].reshape(levels * blocks_here, ROWS, pairs)
        held = lax.all_gather(jnp.stack(parts), "pair", axis=2, tiled=True)
        amps = [amps, other_core(amps)]
        held = [jnp.stack([held, other_core(held)], axis=1).reshape(total, depth * pair_count, -1)]
    ladder = None
    calls = min(levels, 4)
    width = levels // calls
    order = list(reversed(range(calls)))
    for call in order:
        first = call * width
        sums = ladders(first, width, levels, blocks_here, column[None], task_owners, task_local, held, amps, matrix)
        for i in range(width):
            term = (around(sums[i], first + i) if first + i else sums[i]).astype(F32)
            ladder = term if ladder is None else ladder + term
    return residual_in + ladder.transpose(0, 2, 1)


def solution(mesh):
    placed = (P("task", "pair", None), P("task", "pair", None), P("task", "pair", None), P(), P())
    return jax.shard_map(
        per_device, mesh=mesh, in_specs=placed, out_specs=P("task", "pair", None), check_vma=False
    )
```

```python
import functools

import jax
import jax.numpy as jnp
import numpy as np
from jax import lax
from jax.experimental import pallas as pl
from jax.experimental.pallas import tpu as pltpu
from jax.sharding import PartitionSpec as P

TV = 25
PAD = 32
GROUP = 4
LANES = PAD * GROUP
GROUPS = -(-TV // GROUP)
ROWS = TV * PAD
WIDE = GROUPS * LANES
ORDER = [x for g in range(GROUP) for x in range(g, TV, GROUP)]
START = [ORDER.index(g) * PAD for g in range(GROUP)] + [ROWS]
PLACE = np.argsort(ORDER)
PREPARE_STEPS = 2
BF = jnp.bfloat16
F32 = jnp.float32
VMEM_BYTES = 48 * 1024 * 1024
LADDER_VMEM_BYTES = 54 * 1024 * 1024


def spread(spots, rows):
    return (np.arange(rows)[:, None] == spots[None, :]).astype(jnp.bfloat16)


def forms_matrix():
    x, y = np.divmod(np.arange(TV * TV), TV)
    return np.concatenate([spread(PLACE[y] * PAD + x, ROWS), spread(x * PAD + y, ROWS)], axis=0)


def amp_matrix():
    c, d = np.divmod(np.arange(TV * TV), TV)
    return spread(d * PAD + c, ROWS)


def prepare_kernel(column_ref, *refs):
    tile_refs, matrix_ref, forms_ref, all_ref = refs[:4], refs[4], refs[5], refs[6]
    count, size, _ = tile_refs[0].shape
    depth = forms_ref.shape[2]

    @pl.when(pl.program_id(0) == 0)
    def _():
        core = lax.rem(column_ref[0], 2)
        for m in range(count):
            for place, ref in zip((0, 1 + core, 2 - core, 3), tile_refs):
                start = pl.multiple_of(m * depth + place * size, size)
                all_ref[pl.ds(start, size), :] = ref[m]

    wide = 2 if depth % LANES == 0 and count % 2 == 0 else 1
    for first in range(0, count, wide):
        made = lax.dot_general(
            matrix_ref[...],
            all_ref[first * depth : (first + wide) * depth, :],
            (((1,), (1,)), ((), ())),
            preferred_element_type=F32,
        ).astype(BF)
        for m in range(wide):
            forms_ref[first + m] = made[:, m * depth : (m + 1) * depth]


def prepare(parts, column, matrix):
    count, size, width = parts[0].shape
    depth = size * len(parts)
    rows = matrix.shape[0] // PREPARE_STEPS
    in_specs = [pl.BlockSpec(part.shape, lambda i, column: (0, 0, 0)) for part in parts]
    in_specs.append(pl.BlockSpec((rows, width), lambda i, column: (i, 0)))
    return pl.pallas_call(
        prepare_kernel,
        out_shape=jax.ShapeDtypeStruct((count, matrix.shape[0], depth), BF),
        grid_spec=pltpu.PrefetchScalarGridSpec(
            num_scalar_prefetch=1,
            grid=(PREPARE_STEPS,),
            in_specs=in_specs,
            out_specs=pl.BlockSpec((count, rows, depth), lambda i, column: (0, i, 0)),
            scratch_shapes=[pltpu.VMEM((count * depth, width), BF)],
        ),
        compiler_params=pltpu.CompilerParams(vmem_limit_bytes=VMEM_BYTES),
        cost_estimate=pl.CostEstimate(
            flops=2 * count * depth * width * matrix.shape[0],
            bytes_accessed=2 * count * depth * (width + matrix.shape[0]),
            transcendentals=0,
        ),
    )(column, *parts, matrix)


def amp_kernel(matrix_ref, *refs):
    tile_refs, out_ref = refs[:-1], refs[-1]
    blocks_here, pairs = out_ref.shape[0] // len(tile_refs), out_ref.shape[2]
    for by, ref in enumerate(tile_refs):
        made = jnp.dot(matrix_ref[...], ref[...], preferred_element_type=F32).astype(BF)
        for m in range(blocks_here):
            out_ref[by * blocks_here + m] = made[:, m * pairs : (m + 1) * pairs]


def prepare_amps(parts, blocks_here, matrix):
    levels, size = len(parts), parts[0].size
    pairs = parts[0].shape[1] // blocks_here
    return pl.pallas_call(
        amp_kernel,
        out_shape=jax.ShapeDtypeStruct((levels * blocks_here, ROWS, pairs), BF),
        compiler_params=pltpu.CompilerParams(vmem_limit_bytes=VMEM_BYTES),
        cost_estimate=pl.CostEstimate(
            flops=2 * levels * size * ROWS, bytes_accessed=4 * levels * size, transcendentals=0
        ),
    )(matrix, *parts)


def turned(ref, groups, by):
    numbers = [min(A * GROUP + (p - by) % GROUP, TV - 1) for A in groups for p in range(GROUP)]
    return jnp.concatenate([ref[x * PAD : (x + 1) * PAD, :] for x in numbers], axis=0)


def pick_blocks(blocks, low, even):
    b0, b1, b2, b3 = blocks
    x, y = jnp.where(low, b0, b2), jnp.where(low, b2, b0)
    z, w = jnp.where(low, b1, b3), jnp.where(low, b3, b1)
    return jnp.where(even, x, z), jnp.where(even, w, x), jnp.where(even, y, w), jnp.where(even, z, y)


def ladder_kernel(find, made, sources, column_ref, owners_ref, local_ref, *refs):
    factor_refs, amp_refs, refs = refs[:sources], refs[sources : sources + 2], refs[sources + 2 :]
    matrix_ref, refs = None if made else refs[0], refs[0 if made else 1 :]
    out_ref, v_ref, u_ref, acc_ref, c_buf, r_buf, amp_buf, sems = refs[:8]
    column, columns = pl.program_id(0), pl.num_programs(0)
    step, steps = pl.program_id(1), pl.num_programs(1)
    at = column * steps + step
    slot = at & 1

    def fetch(choices, source, index, part, buffer, to, sem):
        for n, ref in enumerate(choices):

            @pl.when(source == n)
            def _():
                tile = ref.at[index, pl.ds(part * ROWS, ROWS)] if part is not None else ref.at[index]
                pltpu.make_async_copy(tile, buffer.at[to], sem).start()

    def fetch_task(i, j, to):
        places = find(i, j, column_ref, owners_ref, local_ref)
        fetch(factor_refs, *places["col"], 0 if made else None, c_buf, to, sems.at[to, 0])
        fetch(factor_refs, *places["row"], 1 if made else None, r_buf, to, sems.at[to, 1])

    @pl.when(at == 0)
    def _():
        fetch_task(0, 0, 0)

    @pl.when(at + 1 < columns * steps)
    def _():
        last = step == steps - 1
        fetch_task(jnp.where(last, column + 1, column), jnp.where(last, 0, step + 1), 1 - slot)

    @pl.when(step == 0)
    def _():
        acc_ref[...] = jnp.zeros_like(acc_ref)

    here = find(column, step, column_ref, owners_ref, local_ref)
    for core in range(2):

        @pl.when(here["amp"][0] == core)
        def _():
            amp_buf[...] = amp_refs[core][here["amp"][1]]

    for n, buffer in enumerate((c_buf, r_buf)):
        pltpu.make_async_copy(buffer.at[slot], buffer.at[slot], sems.at[slot, n]).wait()
    c_form, r_form, amp_form = c_buf.at[slot], r_buf.at[slot], amp_buf
    if not made:
        forms = refs[8]
        for i, tile in enumerate((c_form, r_form)):
            forms[i] = lax.dot_general(
                matrix_ref[i * ROWS : (i + 1) * ROWS, :],
                tile[...],
                (((1,), (1,)), ((), ())),
                preferred_element_type=F32,
            ).astype(BF)
        c_form, r_form = forms.at[0], forms.at[1]

    spot = lax.broadcasted_iota(jnp.int32, (PAD, LANES), 1) // PAD
    low, even = spot < 2, spot % 2 == 0
    nothing = jnp.zeros((PAD, LANES), F32)
    for first in range(0, GROUPS, 2):
        groups = range(first, min(first + 2, GROUPS))
        lanes = slice(groups[0] * LANES, (groups[-1] + 1) * LANES)
        for g in range(GROUP):
            v_ref[START[g] : START[g + 1], lanes] = lax.dot_general(
                c_form[START[g] : START[g + 1], :],
                turned(r_form, groups, g),
                (((1,), (1,)), ((), ())),
                preferred_element_type=F32,
            )
        for A in groups:
            for D in range(GROUPS):
                blocks = [
                    v_ref[START[g] + D * PAD : START[g] + (D + 1) * PAD, A * LANES : (A + 1) * LANES]
                    if D * GROUP + g < TV
                    else nothing
                    for g in range(GROUP)
                ]
                for i, block in enumerate(pick_blocks(blocks, low, even)[: TV - A * GROUP]):
                    u_ref[START[i] + A * PAD : START[i] + (A + 1) * PAD, D * LANES : (D + 1) * LANES] = block.astype(BF)
    out = local_ref[here["task"], 3]
    for i in range(GROUP):
        acc_ref[out, START[i] : START[i + 1], :] += jnp.dot(
            u_ref[START[i] : START[i + 1], :], turned(amp_form, range(GROUPS), i), preferred_element_type=F32
        )

    @pl.when(step == steps - 1)
    def _():
        for m in range(out_ref.shape[1]):
            rows = [acc_ref[m, PLACE[a] * PAD : PLACE[a] * PAD + TV, :] for a in range(TV)]
            out_ref[0, m] = jnp.concatenate(rows, axis=0).astype(BF)


def ladders(first, columns, levels, blocks_here, column, task_owners, task_local, tiles, amps, matrix):
    tasks = task_owners.shape[0] // (2 * levels)
    pairs = amps[0].shape[2]
    made = tiles[0].shape[1] == 2 * ROWS
    depth = tiles[0].shape[2] if made else tiles[0].shape[1]
    held = (ROWS, depth) if made else tiles[0].shape[1:]

    def find(i, j, column_ref, owners_ref, local_ref):
        level, core = column_ref[0] >> 1, column_ref[0] & 1
        above = level + first + i
        task = (2 * jnp.where(above >= levels, above - levels, above) + core) * tasks + j

        def place(kind):
            owner = owners_ref[task, kind]
            below = level - (owner >> 1)
            below = jnp.where(below < 0, below + levels, below)
            far = (owner & 1) ^ core
            return below, far, local_ref[task, kind]

        def factor(kind):
            below, far, m = place(kind)
            if not made:
                return 0, (below * 2 + far) * blocks_here + m
            return below * 2 + far, m

        below, far, m = place(2)
        return {"task": task, "row": factor(0), "col": factor(1), "amp": (far, below * blocks_here + m)}

    anywhere = pl.BlockSpec(memory_space=pl.ANY)
    operands = [*tiles, *amps]
    in_specs = [anywhere] * len(tiles) + [pl.BlockSpec(memory_space=pltpu.VMEM)] * 2
    scratch = [
        pltpu.VMEM((ROWS, WIDE), F32),
        pltpu.VMEM((ROWS, WIDE), BF),
        pltpu.VMEM((blocks_here, ROWS, pairs), F32),
        pltpu.VMEM((2, *held), BF),
        pltpu.VMEM((2, *held), BF),
        pltpu.VMEM((ROWS, pairs), BF),
        pltpu.SemaphoreType.DMA((2, 2)),
    ]
    if not made:
        in_specs.append(pl.BlockSpec(matrix.shape, lambda i, j, *tables: (0, 0)))
        scratch.append(pltpu.VMEM((2, ROWS, depth), BF))
        operands.append(matrix)
    return pl.pallas_call(
        functools.partial(ladder_kernel, find, made, len(tiles)),
        out_shape=jax.ShapeDtypeStruct((columns, blocks_here, TV * TV, pairs), BF),
        grid_spec=pltpu.PrefetchScalarGridSpec(
            num_scalar_prefetch=3,
            grid=(columns, tasks),
            in_specs=in_specs,
            out_specs=pl.BlockSpec((1, blocks_here, TV * TV, pairs), lambda i, j, *tables: (i, 0, 0, 0)),
            scratch_shapes=scratch,
        ),
        compiler_params=pltpu.CompilerParams(vmem_limit_bytes=LADDER_VMEM_BYTES),
        cost_estimate=pl.CostEstimate(
            flops=2 * columns * tasks * ROWS * WIDE * (depth + pairs),
            bytes_accessed=2 * columns * tasks * ROWS * 2 * (depth + pairs),
            transcendentals=0,
        ),
    )(column, task_owners, task_local, *operands)


def after(values, done):
    return lax.optimization_barrier((values, done))[0]


def per_device(factor_blocks, amplitudes, residual_in, task_owners, task_local):
    pair_count = lax.axis_size("pair")
    task_count = lax.axis_size("task")
    column = lax.axis_index("task")
    blocks_here, depth_here, _ = factor_blocks.shape
    pairs = amplitudes.shape[1]
    levels = task_count // 2
    level = column // 2
    depth = depth_here // levels
    total = 2 * levels * blocks_here
    matrix = jnp.asarray(forms_matrix())
    other_core = lambda x: lax.ppermute(x, "task", [(c, c ^ 1) for c in range(task_count)])

    def around(x, by):
        return lax.ppermute(x, "task", [(c, (c + 2 * by) % task_count) for c in range(task_count)])

    same_core = [[2 * z + k for z in range(levels)] for k in range(2)]
    slices = factor_blocks.reshape(blocks_here, levels, depth, -1)
    mine = [lax.dynamic_index_in_dim(slices, (level + by) % levels, 1, keepdims=False) for by in range(levels)]
    if pair_count == 4 and levels == 4:
        sides = [
            [(p * task_count + c, (p ^ (1 if c % 2 == turn else 2)) * task_count + c) for p in range(4) for c in range(task_count)]
            for turn in range(2)
        ]
        first_side = lambda x: lax.ppermute(x, ("pair", "task"), sides[0])
        second_side = lambda x: lax.ppermute(x, ("pair", "task"), sides[1])
        made_forms = lambda *parts: prepare(parts, column[None], matrix)
        own = amplitudes.transpose(2, 0, 1).reshape(TV * TV, blocks_here * pairs)
        amp1 = around(own, 1)
        part0 = mine[0]
        a0, b0, part1 = first_side(part0), second_side(part0), around(mine[1], 1)

        a0, b0, part0, part1, amp1, to2 = after((a0, b0, part0, part1, amp1, mine[2]), ())
        q0, a1, b1, part2 = second_side(a0), first_side(part1), second_side(part1), around(to2, 2)
        forms0 = made_forms(part0, a0, b0, q0)

        forms0, part1, a1, b1, part2, to3 = after((forms0, part1, a1, b1, part2, mine[3]), ())
        q1, a2, b2, part3 = second_side(a1), first_side(part2), second_side(part2), around(to3, 3)
        far0 = other_core(forms0)
        forms1 = made_forms(part1, a1, b1, q1)

        forms1, part2, a2, b2, part3, amp1, far0 = after((forms1, part2, a2, b2, part3, amp1, far0), ())
        q2, a3, b3, amp2 = second_side(a2), first_side(part3), second_side(part3), around(amp1, 1)
        far1 = other_core(forms1)
        forms2 = made_forms(part2, a2, b2, q2)

        forms2, part3, a3, b3, amp2, far1 = after((forms2, part3, a3, b3, amp2, far1), ())
        q3, amp3 = second_side(a3), around(amp2, 1)
        far2 = other_core(after(forms2, q3))
        forms3 = made_forms(part3, a3, b3, q3)

        forms3, amp3 = after((forms3, amp3), ())
        far3 = other_core(forms3)
        amps = prepare_amps([own, amp1, amp2, amp3], blocks_here, jnp.asarray(amp_matrix()))
        held = [forms0, far0, forms1, far1, forms2, far2, forms3, far3]
    else:
        parts = [mine[0]] + [around(mine[by], by) for by in range(1, levels)]
        tiles = amplitudes.reshape(blocks_here, pairs, TV, TV).transpose(0, 3, 2, 1)
        tiles = jnp.pad(tiles, ((0, 0), (0, 0), (0, PAD - TV), (0, 0))).reshape(blocks_here, ROWS, pairs)
        amps = lax.all_gather(tiles, "task", axis=0, axis_index_groups=same_core)
        amps = amps[(level - jnp.arange(levels)) % levels].reshape(levels * blocks_here, ROWS, pairs)
        held = lax.all_gather(jnp.stack(parts), "pair", axis=2, tiled=True)
        held = [jnp.stack([held, other_core(held)], axis=1).reshape(total, depth * pair_count, -1)]
    amps = (amps, other_core(amps))

    ladder = None
    calls = min(levels, 4)
    width = levels // calls
    order = list(reversed(range(calls)))
    for call in order:
        first = call * width
        sums = ladders(first, width, levels, blocks_here, column[None], task_owners, task_local, held, amps, matrix)
        for i in range(width):
            term = (around(sums[i], first + i) if first + i else sums[i]).astype(F32)
            ladder = term if ladder is None else ladder + term
    return residual_in + ladder.transpose(0, 2, 1)


def solution(mesh):
    placed = (P("task", "pair", None), P("task", "pair", None), P("task", "pair", None), P(), P())
    return jax.shard_map(
        per_device, mesh=mesh, in_specs=placed, out_specs=P("task", "pair", None), check_vma=False
    )
```

```python
import functools

import jax
import jax.numpy as jnp
import numpy as np
from jax import lax
from jax.experimental import pallas as pl
from jax.experimental.pallas import tpu as pltpu
from jax.sharding import PartitionSpec as P

TV = 25
PAD = 32
GROUP = 4
LANES = PAD * GROUP
GROUPS = -(-TV // GROUP)
ROWS = TV * PAD
WIDE = GROUPS * LANES
ORDER = [x for g in range(GROUP) for x in range(g, TV, GROUP)]
START = [ORDER.index(g) * PAD for g in range(GROUP)] + [ROWS]
PLACE = np.argsort(ORDER)
PREPARE_STEPS = 2
BF = jnp.bfloat16
F32 = jnp.float32
VMEM_BYTES = 48 * 1024 * 1024
LADDER_VMEM_BYTES = 48 * 1024 * 1024


def spread(spots, rows):
    return (np.arange(rows)[:, None] == spots[None, :]).astype(jnp.bfloat16)


def forms_matrix():
    x, y = np.divmod(np.arange(TV * TV), TV)
    return np.concatenate([spread(PLACE[y] * PAD + x, ROWS), spread(x * PAD + y, ROWS)], axis=0)


def amp_matrix():
    c, d = np.divmod(np.arange(TV * TV), TV)
    return spread(d * PAD + c, ROWS)


def prepare_kernel(column_ref, *refs):
    tile_refs, matrix_ref, forms_ref, all_ref = refs[:4], refs[4], refs[5], refs[6]
    count, size, _ = tile_refs[0].shape
    depth = forms_ref.shape[2]

    @pl.when(pl.program_id(0) == 0)
    def _():
        core = lax.rem(column_ref[0], 2)
        for m in range(count):
            for place, ref in zip((0, 1 + core, 2 - core, 3), tile_refs):
                start = pl.multiple_of(m * depth + place * size, size)
                all_ref[pl.ds(start, size), :] = ref[m]

    wide = 2 if depth % LANES == 0 and count % 2 == 0 else 1
    for first in range(0, count, wide):
        made = lax.dot_general(
            matrix_ref[...],
            all_ref[first * depth : (first + wide) * depth, :],
            (((1,), (1,)), ((), ())),
            preferred_element_type=F32,
        ).astype(BF)
        for m in range(wide):
            forms_ref[first + m] = made[:, m * depth : (m + 1) * depth]


def prepare(parts, column, matrix):
    count, size, width = parts[0].shape
    depth = size * len(parts)
    rows = matrix.shape[0] // PREPARE_STEPS
    in_specs = [pl.BlockSpec(part.shape, lambda i, column: (0, 0, 0)) for part in parts]
    in_specs.append(pl.BlockSpec((rows, width), lambda i, column: (i, 0)))
    return pl.pallas_call(
        prepare_kernel,
        out_shape=jax.ShapeDtypeStruct((count, matrix.shape[0], depth), BF),
        grid_spec=pltpu.PrefetchScalarGridSpec(
            num_scalar_prefetch=1,
            grid=(PREPARE_STEPS,),
            in_specs=in_specs,
            out_specs=pl.BlockSpec((count, rows, depth), lambda i, column: (0, i, 0)),
            scratch_shapes=[pltpu.VMEM((count * depth, width), BF)],
        ),
        compiler_params=pltpu.CompilerParams(vmem_limit_bytes=VMEM_BYTES),
        cost_estimate=pl.CostEstimate(
            flops=2 * count * depth * width * matrix.shape[0],
            bytes_accessed=2 * count * depth * (width + matrix.shape[0]),
            transcendentals=0,
        ),
    )(column, *parts, matrix)


def amp_kernel(matrix_ref, *refs):
    tile_refs, out_ref = refs[:-1], refs[-1]
    blocks_here, pairs = out_ref.shape[0] // len(tile_refs), out_ref.shape[2]
    for by, ref in enumerate(tile_refs):
        made = jnp.dot(matrix_ref[...], ref[...], preferred_element_type=F32).astype(BF)
        for m in range(blocks_here):
            out_ref[by * blocks_here + m] = made[:, m * pairs : (m + 1) * pairs]


def prepare_amps(parts, blocks_here, matrix):
    levels, size = len(parts), parts[0].size
    pairs = parts[0].shape[1] // blocks_here
    return pl.pallas_call(
        amp_kernel,
        out_shape=jax.ShapeDtypeStruct((levels * blocks_here, ROWS, pairs), BF),
        compiler_params=pltpu.CompilerParams(vmem_limit_bytes=VMEM_BYTES),
        cost_estimate=pl.CostEstimate(
            flops=2 * levels * size * ROWS, bytes_accessed=4 * levels * size, transcendentals=0
        ),
    )(matrix, *parts)


def turned(ref, groups, by):
    numbers = [min(A * GROUP + (p - by) % GROUP, TV - 1) for A in groups for p in range(GROUP)]
    return jnp.concatenate([ref[x * PAD : (x + 1) * PAD, :] for x in numbers], axis=0)


def pick_blocks(blocks, low, even):
    b0, b1, b2, b3 = blocks
    x, y = jnp.where(low, b0, b2), jnp.where(low, b2, b0)
    z, w = jnp.where(low, b1, b3), jnp.where(low, b3, b1)
    return jnp.where(even, x, z), jnp.where(even, w, x), jnp.where(even, y, w), jnp.where(even, z, y)


def ladder_kernel(find, made, sources, column_ref, owners_ref, local_ref, *refs):
    factor_refs, amp_refs, refs = refs[:sources], refs[sources : sources + 2], refs[sources + 2 :]
    matrix_ref, refs = None if made else refs[0], refs[0 if made else 1 :]
    out_ref, v_ref, u_ref, acc_ref, c_buf, r_buf, amp_buf, sems = refs[:8]
    column, columns = pl.program_id(0), pl.num_programs(0)
    step, steps = pl.program_id(1), pl.num_programs(1)
    at = column * steps + step
    slot = at & 1

    def fetch(choices, source, index, part, buffer, to, sem):
        for n, ref in enumerate(choices):

            @pl.when(source == n)
            def _():
                tile = ref.at[index, pl.ds(part * ROWS, ROWS)] if part is not None else ref.at[index]
                pltpu.make_async_copy(tile, buffer.at[to], sem).start()

    def fetch_task(i, j, to):
        places = find(i, j, column_ref, owners_ref, local_ref)
        fetch(factor_refs, *places["col"], 0 if made else None, c_buf, to, sems.at[to, 0])
        fetch(factor_refs, *places["row"], 1 if made else None, r_buf, to, sems.at[to, 1])

    @pl.when(at == 0)
    def _():
        fetch_task(0, 0, 0)

    @pl.when(at + 1 < columns * steps)
    def _():
        last = step == steps - 1
        fetch_task(jnp.where(last, column + 1, column), jnp.where(last, 0, step + 1), 1 - slot)

    @pl.when(step == 0)
    def _():
        acc_ref[...] = jnp.zeros_like(acc_ref)

    here = find(column, step, column_ref, owners_ref, local_ref)
    for core in range(2):

        @pl.when(here["amp"][0] == core)
        def _():
            amp_buf[...] = amp_refs[core][here["amp"][1]]

    for n, buffer in enumerate((c_buf, r_buf)):
        pltpu.make_async_copy(buffer.at[slot], buffer.at[slot], sems.at[slot, n]).wait()
    c_form, r_form, amp_form = c_buf.at[slot], r_buf.at[slot], amp_buf
    if not made:
        forms = refs[8]
        for i, tile in enumerate((c_form, r_form)):
            forms[i] = lax.dot_general(
                matrix_ref[i * ROWS : (i + 1) * ROWS, :],
                tile[...],
                (((1,), (1,)), ((), ())),
                preferred_element_type=F32,
            ).astype(BF)
        c_form, r_form = forms.at[0], forms.at[1]

    spot = lax.broadcasted_iota(jnp.int32, (PAD, LANES), 1) // PAD
    low, even = spot < 2, spot % 2 == 0
    nothing = jnp.zeros((PAD, LANES), F32)
    for first in range(0, GROUPS, 2):
        groups = range(first, min(first + 2, GROUPS))
        lanes = slice(groups[0] * LANES, (groups[-1] + 1) * LANES)
        for g in range(GROUP):
            v_ref[START[g] : START[g + 1], lanes] = lax.dot_general(
                c_form[START[g] : START[g + 1], :],
                turned(r_form, groups, g),
                (((1,), (1,)), ((), ())),
                preferred_element_type=F32,
            )
        for A in groups:
            for D in range(GROUPS):
                blocks = [
                    v_ref[START[g] + D * PAD : START[g] + (D + 1) * PAD, A * LANES : (A + 1) * LANES]
                    if D * GROUP + g < TV
                    else nothing
                    for g in range(GROUP)
                ]
                for i, block in enumerate(pick_blocks(blocks, low, even)[: TV - A * GROUP]):
                    u_ref[START[i] + A * PAD : START[i] + (A + 1) * PAD, D * LANES : (D + 1) * LANES] = block.astype(BF)
    out = local_ref[here["task"], 3]
    for i in range(GROUP):
        acc_ref[out, START[i] : START[i + 1], :] += jnp.dot(
            u_ref[START[i] : START[i + 1], :], turned(amp_form, range(GROUPS), i), preferred_element_type=F32
        )

    @pl.when(step == steps - 1)
    def _():
        for m in range(out_ref.shape[1]):
            rows = [acc_ref[m, PLACE[a] * PAD : PLACE[a] * PAD + TV, :] for a in range(TV)]
            out_ref[0, m] = jnp.concatenate(rows, axis=0).astype(BF)


def ladders(first, columns, levels, blocks_here, column, task_owners, task_local, tiles, amps, matrix):
    tasks = task_owners.shape[0] // (2 * levels)
    pairs = amps[0].shape[2]
    made = tiles[0].shape[1] == 2 * ROWS
    depth = tiles[0].shape[2] if made else tiles[0].shape[1]
    held = (ROWS, depth) if made else tiles[0].shape[1:]

    def find(i, j, column_ref, owners_ref, local_ref):
        level, core = column_ref[0] >> 1, column_ref[0] & 1
        above = level + first + i
        task = (2 * jnp.where(above >= levels, above - levels, above) + core) * tasks + j

        def place(kind):
            owner = owners_ref[task, kind]
            below = level - (owner >> 1)
            below = jnp.where(below < 0, below + levels, below)
            far = (owner & 1) ^ core
            return below, far, local_ref[task, kind]

        def factor(kind):
            below, far, m = place(kind)
            if not made:
                return 0, (below * 2 + far) * blocks_here + m
            return below * 2 + far, m

        below, far, m = place(2)
        return {"task": task, "row": factor(0), "col": factor(1), "amp": (far, below * blocks_here + m)}

    anywhere = pl.BlockSpec(memory_space=pl.ANY)
    operands = [*tiles, *amps]
    in_specs = [anywhere] * len(tiles) + [pl.BlockSpec(memory_space=pltpu.VMEM)] * 2
    scratch = [
        pltpu.VMEM((ROWS, WIDE), F32),
        pltpu.VMEM((ROWS, WIDE), BF),
        pltpu.VMEM((blocks_here, ROWS, pairs), F32),
        pltpu.VMEM((2, *held), BF),
        pltpu.VMEM((2, *held), BF),
        pltpu.VMEM((ROWS, pairs), BF),
        pltpu.SemaphoreType.DMA((2, 2)),
    ]
    if not made:
        in_specs.append(pl.BlockSpec(matrix.shape, lambda i, j, *tables: (0, 0)))
        scratch.append(pltpu.VMEM((2, ROWS, depth), BF))
        operands.append(matrix)
    return pl.pallas_call(
        functools.partial(ladder_kernel, find, made, len(tiles)),
        out_shape=jax.ShapeDtypeStruct((columns, blocks_here, TV * TV, pairs), BF),
        grid_spec=pltpu.PrefetchScalarGridSpec(
            num_scalar_prefetch=3,
            grid=(columns, tasks),
            in_specs=in_specs,
            out_specs=pl.BlockSpec((1, blocks_here, TV * TV, pairs), lambda i, j, *tables: (i, 0, 0, 0)),
            scratch_shapes=scratch,
        ),
        compiler_params=pltpu.CompilerParams(vmem_limit_bytes=LADDER_VMEM_BYTES),
        cost_estimate=pl.CostEstimate(
            flops=2 * columns * tasks * ROWS * WIDE * (depth + pairs),
            bytes_accessed=2 * columns * tasks * ROWS * 2 * (depth + pairs),
            transcendentals=0,
        ),
    )(column, task_owners, task_local, *operands)


def after(values, done):
    return lax.optimization_barrier((values, done))[0]


def per_device(factor_blocks, amplitudes, residual_in, task_owners, task_local):
    pair_count = lax.axis_size("pair")
    task_count = lax.axis_size("task")
    column = lax.axis_index("task")
    blocks_here, depth_here, _ = factor_blocks.shape
    pairs = amplitudes.shape[1]
    levels = task_count // 2
    level = column // 2
    depth = depth_here // levels
    total = 2 * levels * blocks_here
    matrix = jnp.asarray(forms_matrix())
    other_core = lambda x: lax.ppermute(x, "task", [(c, c ^ 1) for c in range(task_count)])

    def around(x, by):
        return lax.ppermute(x, "task", [(c, (c + 2 * by) % task_count) for c in range(task_count)])

    same_core = [[2 * z + k for z in range(levels)] for k in range(2)]
    slices = factor_blocks.reshape(blocks_here, levels, depth, -1)
    mine = [lax.dynamic_index_in_dim(slices, (level + by) % levels, 1, keepdims=False) for by in range(levels)]
    if pair_count == 4 and levels == 4:
        sides = [
            [(p * task_count + c, (p ^ (1 if c % 2 == turn else 2)) * task_count + c) for p in range(4) for c in range(task_count)]
            for turn in range(2)
        ]
        first_side = lambda x: lax.ppermute(x, ("pair", "task"), sides[0])
        second_side = lambda x: lax.ppermute(x, ("pair", "task"), sides[1])
        made_forms = lambda *parts: prepare(parts, column[None], matrix)
        own = amplitudes.transpose(2, 0, 1).reshape(TV * TV, blocks_here * pairs)
        amp1 = around(own, 1)
        part0 = mine[0]
        a0, b0, part1 = first_side(part0), second_side(part0), around(mine[1], 1)

        a0, b0, part0, part1, amp1, to2 = after((a0, b0, part0, part1, amp1, mine[2]), ())
        q0, a1, b1, part2 = second_side(a0), first_side(part1), second_side(part1), around(to2, 2)
        forms0 = made_forms(part0, a0, b0, q0)

        forms0, part1, a1, b1, part2, to3 = after((forms0, part1, a1, b1, part2, mine[3]), ())
        q1, a2, b2, part3 = second_side(a1), first_side(part2), second_side(part2), around(to3, 3)
        far0 = other_core(forms0)
        forms1 = made_forms(part1, a1, b1, q1)

        forms1, part2, a2, b2, part3, amp1, far0 = after((forms1, part2, a2, b2, part3, amp1, far0), ())
        q2, a3, b3, amp2 = second_side(a2), first_side(part3), second_side(part3), around(amp1, 1)
        far1 = other_core(forms1)
        forms2 = made_forms(part2, a2, b2, q2)

        forms2, part3, a3, b3, amp2, far1 = after((forms2, part3, a3, b3, amp2, far1), ())
        q3, amp3 = second_side(a3), around(amp2, 1)
        far2 = other_core(after(forms2, q3))
        forms3 = made_forms(part3, a3, b3, q3)

        forms3, amp3 = after((forms3, amp3), ())
        far3 = other_core(forms3)
        amps = prepare_amps([own, amp1, amp2, amp3], blocks_here, jnp.asarray(amp_matrix()))
        held = [forms0, far0, forms1, far1, forms2, far2, forms3, far3]
    else:
        parts = [mine[0]] + [around(mine[by], by) for by in range(1, levels)]
        tiles = amplitudes.reshape(blocks_here, pairs, TV, TV).transpose(0, 3, 2, 1)
        tiles = jnp.pad(tiles, ((0, 0), (0, 0), (0, PAD - TV), (0, 0))).reshape(blocks_here, ROWS, pairs)
        amps = lax.all_gather(tiles, "task", axis=0, axis_index_groups=same_core)
        amps = amps[(level - jnp.arange(levels)) % levels].reshape(levels * blocks_here, ROWS, pairs)
        held = lax.all_gather(jnp.stack(parts), "pair", axis=2, tiled=True)
        held = [jnp.stack([held, other_core(held)], axis=1).reshape(total, depth * pair_count, -1)]
    amps = (amps, other_core(amps))

    ladder = None
    calls = min(levels, 4)
    width = levels // calls
    order = list(reversed(range(calls)))
    for call in order:
        first = call * width
        sums = ladders(first, width, levels, blocks_here, column[None], task_owners, task_local, held, amps, matrix)
        for i in range(width):
            term = (around(sums[i], first + i) if first + i else sums[i]).astype(F32)
            ladder = term if ladder is None else ladder + term
    return residual_in + ladder.transpose(0, 2, 1)


def solution(mesh):
    placed = (P("task", "pair", None), P("task", "pair", None), P("task", "pair", None), P(), P())
    return jax.shard_map(
        per_device, mesh=mesh, in_specs=placed, out_specs=P("task", "pair", None), check_vma=False
    )
```

```python
import functools

import jax
import jax.numpy as jnp
import numpy as np
from jax import lax
from jax.experimental import pallas as pl
from jax.experimental.pallas import tpu as pltpu
from jax.sharding import PartitionSpec as P

TV = 25
PAD = 32
GROUP = 4
LANES = PAD * GROUP
GROUPS = -(-TV // GROUP)
ROWS = TV * PAD
WIDE = GROUPS * LANES
ORDER = [x for g in range(GROUP) for x in range(g, TV, GROUP)]
START = [ORDER.index(g) * PAD for g in range(GROUP)] + [ROWS]
PLACE = np.argsort(ORDER)
PREPARE_STEPS = 2
BF = jnp.bfloat16
F32 = jnp.float32
VMEM_BYTES = 48 * 1024 * 1024
LADDER_VMEM_BYTES = 52 * 1024 * 1024


def spread(spots, rows):
    return (np.arange(rows)[:, None] == spots[None, :]).astype(jnp.bfloat16)


def forms_matrix():
    x, y = np.divmod(np.arange(TV * TV), TV)
    return np.concatenate([spread(PLACE[y] * PAD + x, ROWS), spread(x * PAD + y, ROWS)], axis=0)


def amp_matrix():
    c, d = np.divmod(np.arange(TV * TV), TV)
    return spread(d * PAD + c, ROWS)


def prepare_kernel(column_ref, *refs):
    tile_refs, matrix_ref, forms_ref, all_ref = refs[:4], refs[4], refs[5], refs[6]
    count, size, _ = tile_refs[0].shape
    depth = forms_ref.shape[2]

    @pl.when(pl.program_id(0) == 0)
    def _():
        core = lax.rem(column_ref[0], 2)
        for m in range(count):
            for place, ref in zip((0, 1 + core, 2 - core, 3), tile_refs):
                start = pl.multiple_of(m * depth + place * size, size)
                all_ref[pl.ds(start, size), :] = ref[m]

    wide = 2 if depth % LANES == 0 and count % 2 == 0 else 1
    for first in range(0, count, wide):
        made = lax.dot_general(
            matrix_ref[...],
            all_ref[first * depth : (first + wide) * depth, :],
            (((1,), (1,)), ((), ())),
            preferred_element_type=F32,
        ).astype(BF)
        for m in range(wide):
            forms_ref[first + m] = made[:, m * depth : (m + 1) * depth]


def prepare(parts, column, matrix):
    count, size, width = parts[0].shape
    depth = size * len(parts)
    rows = matrix.shape[0] // PREPARE_STEPS
    in_specs = [pl.BlockSpec(part.shape, lambda i, column: (0, 0, 0)) for part in parts]
    in_specs.append(pl.BlockSpec((rows, width), lambda i, column: (i, 0)))
    return pl.pallas_call(
        prepare_kernel,
        out_shape=jax.ShapeDtypeStruct((count, matrix.shape[0], depth), BF),
        grid_spec=pltpu.PrefetchScalarGridSpec(
            num_scalar_prefetch=1,
            grid=(PREPARE_STEPS,),
            in_specs=in_specs,
            out_specs=pl.BlockSpec((count, rows, depth), lambda i, column: (0, i, 0)),
            scratch_shapes=[pltpu.VMEM((count * depth, width), BF)],
        ),
        compiler_params=pltpu.CompilerParams(vmem_limit_bytes=VMEM_BYTES),
        cost_estimate=pl.CostEstimate(
            flops=2 * count * depth * width * matrix.shape[0],
            bytes_accessed=2 * count * depth * (width + matrix.shape[0]),
            transcendentals=0,
        ),
    )(column, *parts, matrix)


def amp_kernel(matrix_ref, *refs):
    tile_refs, out_ref = refs[:-1], refs[-1]
    blocks_here, pairs = out_ref.shape[0] // len(tile_refs), out_ref.shape[2]
    for by, ref in enumerate(tile_refs):
        made = jnp.dot(matrix_ref[...], ref[...], preferred_element_type=F32).astype(BF)
        for m in range(blocks_here):
            out_ref[by * blocks_here + m] = made[:, m * pairs : (m + 1) * pairs]


def prepare_amps(parts, blocks_here, matrix):
    levels, size = len(parts), parts[0].size
    pairs = parts[0].shape[1] // blocks_here
    return pl.pallas_call(
        amp_kernel,
        out_shape=jax.ShapeDtypeStruct((levels * blocks_here, ROWS, pairs), BF),
        compiler_params=pltpu.CompilerParams(vmem_limit_bytes=VMEM_BYTES),
        cost_estimate=pl.CostEstimate(
            flops=2 * levels * size * ROWS, bytes_accessed=4 * levels * size, transcendentals=0
        ),
    )(matrix, *parts)


def turned(ref, groups, by):
    numbers = [min(A * GROUP + (p - by) % GROUP, TV - 1) for A in groups for p in range(GROUP)]
    return jnp.concatenate([ref[x * PAD : (x + 1) * PAD, :] for x in numbers], axis=0)


def pick_blocks(blocks, low, even):
    b0, b1, b2, b3 = blocks
    x, y = jnp.where(low, b0, b2), jnp.where(low, b2, b0)
    z, w = jnp.where(low, b1, b3), jnp.where(low, b3, b1)
    return jnp.where(even, x, z), jnp.where(even, w, x), jnp.where(even, y, w), jnp.where(even, z, y)


def ladder_kernel(find, made, sources, column_ref, owners_ref, local_ref, *refs):
    factor_refs, amp_refs, refs = refs[:sources], refs[sources : sources + 2], refs[sources + 2 :]
    matrix_ref, refs = None if made else refs[0], refs[0 if made else 1 :]
    out_ref, v_ref, u_ref, acc_ref, c_buf, r_buf, amp_buf, sems = refs[:8]
    column, columns = pl.program_id(0), pl.num_programs(0)
    step, steps = pl.program_id(1), pl.num_programs(1)
    at = column * steps + step
    slot = at & 1

    def fetch(choices, source, index, part, buffer, to, sem):
        for n, ref in enumerate(choices):

            @pl.when(source == n)
            def _():
                tile = ref.at[index, pl.ds(part * ROWS, ROWS)] if part is not None else ref.at[index]
                pltpu.make_async_copy(tile, buffer.at[to], sem).start()

    def fetch_task(i, j, to):
        places = find(i, j, column_ref, owners_ref, local_ref)
        fetch(factor_refs, *places["col"], 0 if made else None, c_buf, to, sems.at[to, 0])
        fetch(factor_refs, *places["row"], 1 if made else None, r_buf, to, sems.at[to, 1])

    @pl.when(at == 0)
    def _():
        fetch_task(0, 0, 0)

    @pl.when(at + 1 < columns * steps)
    def _():
        last = step == steps - 1
        fetch_task(jnp.where(last, column + 1, column), jnp.where(last, 0, step + 1), 1 - slot)

    @pl.when(step == 0)
    def _():
        acc_ref[...] = jnp.zeros_like(acc_ref)

    here = find(column, step, column_ref, owners_ref, local_ref)
    for core in range(2):

        @pl.when(here["amp"][0] == core)
        def _():
            amp_buf[...] = amp_refs[core][here["amp"][1]]

    for n, buffer in enumerate((c_buf, r_buf)):
        pltpu.make_async_copy(buffer.at[slot], buffer.at[slot], sems.at[slot, n]).wait()
    c_form, r_form, amp_form = c_buf.at[slot], r_buf.at[slot], amp_buf
    if not made:
        forms = refs[8]
        for i, tile in enumerate((c_form, r_form)):
            forms[i] = lax.dot_general(
                matrix_ref[i * ROWS : (i + 1) * ROWS, :],
                tile[...],
                (((1,), (1,)), ((), ())),
                preferred_element_type=F32,
            ).astype(BF)
        c_form, r_form = forms.at[0], forms.at[1]

    spot = lax.broadcasted_iota(jnp.int32, (PAD, LANES), 1) // PAD
    low, even = spot < 2, spot % 2 == 0
    nothing = jnp.zeros((PAD, LANES), F32)
    for first in range(0, GROUPS, 2):
        groups = range(first, min(first + 2, GROUPS))
        lanes = slice(groups[0] * LANES, (groups[-1] + 1) * LANES)
        for g in range(GROUP):
            v_ref[START[g] : START[g + 1], lanes] = lax.dot_general(
                c_form[START[g] : START[g + 1], :],
                turned(r_form, groups, g),
                (((1,), (1,)), ((), ())),
                preferred_element_type=F32,
            )
        for A in groups:
            for D in range(GROUPS):
                blocks = [
                    v_ref[START[g] + D * PAD : START[g] + (D + 1) * PAD, A * LANES : (A + 1) * LANES]
                    if D * GROUP + g < TV
                    else nothing
                    for g in range(GROUP)
                ]
                for i, block in enumerate(pick_blocks(blocks, low, even)[: TV - A * GROUP]):
                    u_ref[START[i] + A * PAD : START[i] + (A + 1) * PAD, D * LANES : (D + 1) * LANES] = block.astype(BF)
    out = local_ref[here["task"], 3]
    for i in range(GROUP):
        acc_ref[out, START[i] : START[i + 1], :] += jnp.dot(
            u_ref[START[i] : START[i + 1], :], turned(amp_form, range(GROUPS), i), preferred_element_type=F32
        )

    @pl.when(step == steps - 1)
    def _():
        for m in range(out_ref.shape[1]):
            rows = [acc_ref[m, PLACE[a] * PAD : PLACE[a] * PAD + TV, :] for a in range(TV)]
            out_ref[0, m] = jnp.concatenate(rows, axis=0).astype(BF)


def ladders(first, columns, levels, blocks_here, column, task_owners, task_local, tiles, amps, matrix):
    tasks = task_owners.shape[0] // (2 * levels)
    pairs = amps[0].shape[2]
    made = tiles[0].shape[1] == 2 * ROWS
    depth = tiles[0].shape[2] if made else tiles[0].shape[1]
    held = (ROWS, depth) if made else tiles[0].shape[1:]

    def find(i, j, column_ref, owners_ref, local_ref):
        level, core = column_ref[0] >> 1, column_ref[0] & 1
        above = level + first + i
        task = (2 * jnp.where(above >= levels, above - levels, above) + core) * tasks + j

        def place(kind):
            owner = owners_ref[task, kind]
            below = level - (owner >> 1)
            below = jnp.where(below < 0, below + levels, below)
            far = (owner & 1) ^ core
            return below, far, local_ref[task, kind]

        def factor(kind):
            below, far, m = place(kind)
            if not made:
                return 0, (below * 2 + far) * blocks_here + m
            return below * 2 + far, m

        below, far, m = place(2)
        return {"task": task, "row": factor(0), "col": factor(1), "amp": (far, below * blocks_here + m)}

    anywhere = pl.BlockSpec(memory_space=pl.ANY)
    operands = [*tiles, *amps]
    in_specs = [anywhere] * len(tiles) + [pl.BlockSpec(memory_space=pltpu.VMEM)] * 2
    scratch = [
        pltpu.VMEM((ROWS, WIDE), F32),
        pltpu.VMEM((ROWS, WIDE), BF),
        pltpu.VMEM((blocks_here, ROWS, pairs), F32),
        pltpu.VMEM((2, *held), BF),
        pltpu.VMEM((2, *held), BF),
        pltpu.VMEM((ROWS, pairs), BF),
        pltpu.SemaphoreType.DMA((2, 2)),
    ]
    if not made:
        in_specs.append(pl.BlockSpec(matrix.shape, lambda i, j, *tables: (0, 0)))
        scratch.append(pltpu.VMEM((2, ROWS, depth), BF))
        operands.append(matrix)
    return pl.pallas_call(
        functools.partial(ladder_kernel, find, made, len(tiles)),
        out_shape=jax.ShapeDtypeStruct((columns, blocks_here, TV * TV, pairs), BF),
        grid_spec=pltpu.PrefetchScalarGridSpec(
            num_scalar_prefetch=3,
            grid=(columns, tasks),
            in_specs=in_specs,
            out_specs=pl.BlockSpec((1, blocks_here, TV * TV, pairs), lambda i, j, *tables: (i, 0, 0, 0)),
            scratch_shapes=scratch,
        ),
        compiler_params=pltpu.CompilerParams(vmem_limit_bytes=LADDER_VMEM_BYTES),
        cost_estimate=pl.CostEstimate(
            flops=2 * columns * tasks * ROWS * WIDE * (depth + pairs),
            bytes_accessed=2 * columns * tasks * ROWS * 2 * (depth + pairs),
            transcendentals=0,
        ),
    )(column, task_owners, task_local, *operands)


def after(values, done):
    return lax.optimization_barrier((values, done))[0]


def per_device(factor_blocks, amplitudes, residual_in, task_owners, task_local):
    pair_count = lax.axis_size("pair")
    task_count = lax.axis_size("task")
    column = lax.axis_index("task")
    blocks_here, depth_here, _ = factor_blocks.shape
    pairs = amplitudes.shape[1]
    levels = task_count // 2
    level = column // 2
    depth = depth_here // levels
    total = 2 * levels * blocks_here
    matrix = jnp.asarray(forms_matrix())
    other_core = lambda x: lax.ppermute(x, "task", [(c, c ^ 1) for c in range(task_count)])

    def around(x, by):
        return lax.ppermute(x, "task", [(c, (c + 2 * by) % task_count) for c in range(task_count)])

    same_core = [[2 * z + k for z in range(levels)] for k in range(2)]
    slices = factor_blocks.reshape(blocks_here, levels, depth, -1)
    mine = [lax.dynamic_index_in_dim(slices, (level + by) % levels, 1, keepdims=False) for by in range(levels)]
    if pair_count == 4 and levels == 4:
        sides = [
            [(p * task_count + c, (p ^ (1 if c % 2 == turn else 2)) * task_count + c) for p in range(4) for c in range(task_count)]
            for turn in range(2)
        ]
        first_side = lambda x: lax.ppermute(x, ("pair", "task"), sides[0])
        second_side = lambda x: lax.ppermute(x, ("pair", "task"), sides[1])
        made_forms = lambda *parts: prepare(parts, column[None], matrix)
        own = amplitudes.transpose(2, 0, 1).reshape(TV * TV, blocks_here * pairs)
        amp1 = around(own, 1)
        part0 = mine[0]
        a0, b0, part1 = first_side(part0), second_side(part0), around(mine[1], 1)

        a0, b0, part0, part1, amp1, to2 = after((a0, b0, part0, part1, amp1, mine[2]), ())
        q0, a1, b1, part2 = second_side(a0), first_side(part1), second_side(part1), around(to2, 2)
        forms0 = made_forms(part0, a0, b0, q0)

        forms0, part1, a1, b1, part2, to3 = after((forms0, part1, a1, b1, part2, mine[3]), ())
        q1, a2, b2, part3 = second_side(a1), first_side(part2), second_side(part2), around(to3, 3)
        far0 = other_core(forms0)
        forms1 = made_forms(part1, a1, b1, q1)

        forms1, part2, a2, b2, part3, amp1, far0 = after((forms1, part2, a2, b2, part3, amp1, far0), ())
        q2, a3, b3, amp2 = second_side(a2), first_side(part3), second_side(part3), around(amp1, 1)
        far1 = other_core(forms1)
        forms2 = made_forms(part2, a2, b2, q2)

        forms2, part3, a3, b3, amp2, far1 = after((forms2, part3, a3, b3, amp2, far1), ())
        q3, amp3 = second_side(a3), around(amp2, 1)
        far2 = other_core(after(forms2, q3))
        forms3 = made_forms(part3, a3, b3, q3)

        forms3, amp3 = after((forms3, amp3), ())
        far3 = other_core(forms3)
        amps = prepare_amps([own, amp1, amp2, amp3], blocks_here, jnp.asarray(amp_matrix()))
        held = [forms0, far0, forms1, far1, forms2, far2, forms3, far3]
    else:
        parts = [mine[0]] + [around(mine[by], by) for by in range(1, levels)]
        tiles = amplitudes.reshape(blocks_here, pairs, TV, TV).transpose(0, 3, 2, 1)
        tiles = jnp.pad(tiles, ((0, 0), (0, 0), (0, PAD - TV), (0, 0))).reshape(blocks_here, ROWS, pairs)
        amps = lax.all_gather(tiles, "task", axis=0, axis_index_groups=same_core)
        amps = amps[(level - jnp.arange(levels)) % levels].reshape(levels * blocks_here, ROWS, pairs)
        held = lax.all_gather(jnp.stack(parts), "pair", axis=2, tiled=True)
        held = [jnp.stack([held, other_core(held)], axis=1).reshape(total, depth * pair_count, -1)]
    amps = (amps, other_core(amps))

    ladder = None
    calls = min(levels, 4)
    width = levels // calls
    order = list(reversed(range(calls)))
    for call in order:
        first = call * width
        sums = ladders(first, width, levels, blocks_here, column[None], task_owners, task_local, held, amps, matrix)
        for i in range(width):
            term = (around(sums[i], first + i) if first + i else sums[i]).astype(F32)
            ladder = term if ladder is None else ladder + term
    return residual_in + ladder.transpose(0, 2, 1)


def solution(mesh):
    placed = (P("task", "pair", None), P("task", "pair", None), P("task", "pair", None), P(), P())
    return jax.shard_map(
        per_device, mesh=mesh, in_specs=placed, out_specs=P("task", "pair", None), check_vma=False
    )
```

```python
import functools

import jax
import jax.numpy as jnp
import numpy as np
from jax import lax
from jax.experimental import pallas as pl
from jax.experimental.pallas import tpu as pltpu
from jax.sharding import PartitionSpec as P

TV = 25
PAD = 32
GROUP = 4
LANES = PAD * GROUP
GROUPS = -(-TV // GROUP)
ROWS = TV * PAD
WIDE = GROUPS * LANES
ORDER = [x for g in range(GROUP) for x in range(g, TV, GROUP)]
START = [ORDER.index(g) * PAD for g in range(GROUP)] + [ROWS]
PLACE = np.argsort(ORDER)
PREPARE_STEPS = 2
BF = jnp.bfloat16
F32 = jnp.float32
VMEM_BYTES = 48 * 1024 * 1024
LADDER_VMEM_BYTES = 50 * 1024 * 1024


def spread(spots, rows):
    return (np.arange(rows)[:, None] == spots[None, :]).astype(jnp.bfloat16)


def forms_matrix():
    x, y = np.divmod(np.arange(TV * TV), TV)
    return np.concatenate([spread(PLACE[y] * PAD + x, ROWS), spread(x * PAD + y, ROWS)], axis=0)


def amp_matrix():
    c, d = np.divmod(np.arange(TV * TV), TV)
    return spread(d * PAD + c, ROWS)


def prepare_kernel(column_ref, *refs):
    tile_refs, matrix_ref, forms_ref, all_ref = refs[:4], refs[4], refs[5], refs[6]
    count, size, _ = tile_refs[0].shape
    depth = forms_ref.shape[2]

    @pl.when(pl.program_id(0) == 0)
    def _():
        core = lax.rem(column_ref[0], 2)
        for m in range(count):
            for place, ref in zip((0, 1 + core, 2 - core, 3), tile_refs):
                start = pl.multiple_of(m * depth + place * size, size)
                all_ref[pl.ds(start, size), :] = ref[m]

    wide = 2 if depth % LANES == 0 and count % 2 == 0 else 1
    for first in range(0, count, wide):
        made = lax.dot_general(
            matrix_ref[...],
            all_ref[first * depth : (first + wide) * depth, :],
            (((1,), (1,)), ((), ())),
            preferred_element_type=F32,
        ).astype(BF)
        for m in range(wide):
            forms_ref[first + m] = made[:, m * depth : (m + 1) * depth]


def prepare(parts, column, matrix):
    count, size, width = parts[0].shape
    depth = size * len(parts)
    rows = matrix.shape[0] // PREPARE_STEPS
    in_specs = [pl.BlockSpec(part.shape, lambda i, column: (0, 0, 0)) for part in parts]
    in_specs.append(pl.BlockSpec((rows, width), lambda i, column: (i, 0)))
    return pl.pallas_call(
        prepare_kernel,
        out_shape=jax.ShapeDtypeStruct((count, matrix.shape[0], depth), BF),
        grid_spec=pltpu.PrefetchScalarGridSpec(
            num_scalar_prefetch=1,
            grid=(PREPARE_STEPS,),
            in_specs=in_specs,
            out_specs=pl.BlockSpec((count, rows, depth), lambda i, column: (0, i, 0)),
            scratch_shapes=[pltpu.VMEM((count * depth, width), BF)],
        ),
        compiler_params=pltpu.CompilerParams(vmem_limit_bytes=VMEM_BYTES),
        cost_estimate=pl.CostEstimate(
            flops=2 * count * depth * width * matrix.shape[0],
            bytes_accessed=2 * count * depth * (width + matrix.shape[0]),
            transcendentals=0,
        ),
    )(column, *parts, matrix)


def amp_kernel(matrix_ref, *refs):
    tile_refs, out_ref = refs[:-1], refs[-1]
    blocks_here, pairs = out_ref.shape[0] // len(tile_refs), out_ref.shape[2]
    for by, ref in enumerate(tile_refs):
        made = jnp.dot(matrix_ref[...], ref[...], preferred_element_type=F32).astype(BF)
        for m in range(blocks_here):
            out_ref[by * blocks_here + m] = made[:, m * pairs : (m + 1) * pairs]


def prepare_amps(parts, blocks_here, matrix):
    levels, size = len(parts), parts[0].size
    pairs = parts[0].shape[1] // blocks_here
    return pl.pallas_call(
        amp_kernel,
        out_shape=jax.ShapeDtypeStruct((levels * blocks_here, ROWS, pairs), BF),
        compiler_params=pltpu.CompilerParams(vmem_limit_bytes=VMEM_BYTES),
        cost_estimate=pl.CostEstimate(
            flops=2 * levels * size * ROWS, bytes_accessed=4 * levels * size, transcendentals=0
        ),
    )(matrix, *parts)


def turned(ref, groups, by):
    numbers = [min(A * GROUP + (p - by) % GROUP, TV - 1) for A in groups for p in range(GROUP)]
    return jnp.concatenate([ref[x * PAD : (x + 1) * PAD, :] for x in numbers], axis=0)


def pick_blocks(blocks, low, even):
    b0, b1, b2, b3 = blocks
    x, y = jnp.where(low, b0, b2), jnp.where(low, b2, b0)
    z, w = jnp.where(low, b1, b3), jnp.where(low, b3, b1)
    return jnp.where(even, x, z), jnp.where(even, w, x), jnp.where(even, y, w), jnp.where(even, z, y)


def ladder_kernel(find, made, sources, column_ref, owners_ref, local_ref, *refs):
    factor_refs, amp_refs, refs = refs[:sources], refs[sources : sources + 2], refs[sources + 2 :]
    matrix_ref, refs = None if made else refs[0], refs[0 if made else 1 :]
    out_ref, v_ref, u_ref, acc_ref, c_buf, r_buf, amp_buf, sems = refs[:8]
    column, columns = pl.program_id(0), pl.num_programs(0)
    step, steps = pl.program_id(1), pl.num_programs(1)
    at = column * steps + step
    slot = at & 1

    def fetch(choices, source, index, part, buffer, to, sem):
        for n, ref in enumerate(choices):

            @pl.when(source == n)
            def _():
                tile = ref.at[index, pl.ds(part * ROWS, ROWS)] if part is not None else ref.at[index]
                pltpu.make_async_copy(tile, buffer.at[to], sem).start()

    def fetch_task(i, j, to):
        places = find(i, j, column_ref, owners_ref, local_ref)
        fetch(factor_refs, *places["col"], 0 if made else None, c_buf, to, sems.at[to, 0])
        fetch(factor_refs, *places["row"], 1 if made else None, r_buf, to, sems.at[to, 1])

    @pl.when(at == 0)
    def _():
        fetch_task(0, 0, 0)

    @pl.when(at + 1 < columns * steps)
    def _():
        last = step == steps - 1
        fetch_task(jnp.where(last, column + 1, column), jnp.where(last, 0, step + 1), 1 - slot)

    @pl.when(step == 0)
    def _():
        acc_ref[...] = jnp.zeros_like(acc_ref)

    here = find(column, step, column_ref, owners_ref, local_ref)
    for core in range(2):

        @pl.when(here["amp"][0] == core)
        def _():
            amp_buf[...] = amp_refs[core][here["amp"][1]]

    for n, buffer in enumerate((c_buf, r_buf)):
        pltpu.make_async_copy(buffer.at[slot], buffer.at[slot], sems.at[slot, n]).wait()
    c_form, r_form, amp_form = c_buf.at[slot], r_buf.at[slot], amp_buf
    if not made:
        forms = refs[8]
        for i, tile in enumerate((c_form, r_form)):
            forms[i] = lax.dot_general(
                matrix_ref[i * ROWS : (i + 1) * ROWS, :],
                tile[...],
                (((1,), (1,)), ((), ())),
                preferred_element_type=F32,
            ).astype(BF)
        c_form, r_form = forms.at[0], forms.at[1]

    spot = lax.broadcasted_iota(jnp.int32, (PAD, LANES), 1) // PAD
    low, even = spot < 2, spot % 2 == 0
    nothing = jnp.zeros((PAD, LANES), F32)
    for first in range(0, GROUPS, 2):
        groups = range(first, min(first + 2, GROUPS))
        lanes = slice(groups[0] * LANES, (groups[-1] + 1) * LANES)
        for g in range(GROUP):
            v_ref[START[g] : START[g + 1], lanes] = lax.dot_general(
                c_form[START[g] : START[g + 1], :],
                turned(r_form, groups, g),
                (((1,), (1,)), ((), ())),
                preferred_element_type=F32,
            )
        for A in groups:
            for D in range(GROUPS):
                blocks = [
                    v_ref[START[g] + D * PAD : START[g] + (D + 1) * PAD, A * LANES : (A + 1) * LANES]
                    if D * GROUP + g < TV
                    else nothing
                    for g in range(GROUP)
                ]
                for i, block in enumerate(pick_blocks(blocks, low, even)[: TV - A * GROUP]):
                    u_ref[START[i] + A * PAD : START[i] + (A + 1) * PAD, D * LANES : (D + 1) * LANES] = block.astype(BF)
    out = local_ref[here["task"], 3]
    for i in range(GROUP):
        acc_ref[out, START[i] : START[i + 1], :] += jnp.dot(
            u_ref[START[i] : START[i + 1], :], turned(amp_form, range(GROUPS), i), preferred_element_type=F32
        )

    @pl.when(step == steps - 1)
    def _():
        for m in range(out_ref.shape[1]):
            rows = [acc_ref[m, PLACE[a] * PAD : PLACE[a] * PAD + TV, :] for a in range(TV)]
            out_ref[0, m] = jnp.concatenate(rows, axis=0).astype(BF)


def ladders(first, columns, levels, blocks_here, column, task_owners, task_local, tiles, amps, matrix):
    tasks = task_owners.shape[0] // (2 * levels)
    pairs = amps[0].shape[2]
    made = tiles[0].shape[1] == 2 * ROWS
    depth = tiles[0].shape[2] if made else tiles[0].shape[1]
    held = (ROWS, depth) if made else tiles[0].shape[1:]

    def find(i, j, column_ref, owners_ref, local_ref):
        level, core = column_ref[0] >> 1, column_ref[0] & 1
        above = level + first + i
        task = (2 * jnp.where(above >= levels, above - levels, above) + core) * tasks + j

        def place(kind):
            owner = owners_ref[task, kind]
            below = level - (owner >> 1)
            below = jnp.where(below < 0, below + levels, below)
            far = (owner & 1) ^ core
            return below, far, local_ref[task, kind]

        def factor(kind):
            below, far, m = place(kind)
            if not made:
                return 0, (below * 2 + far) * blocks_here + m
            return below * 2 + far, m

        below, far, m = place(2)
        return {"task": task, "row": factor(0), "col": factor(1), "amp": (far, below * blocks_here + m)}

    anywhere = pl.BlockSpec(memory_space=pl.ANY)
    operands = [*tiles, *amps]
    in_specs = [anywhere] * len(tiles) + [pl.BlockSpec(memory_space=pltpu.VMEM)] * 2
    scratch = [
        pltpu.VMEM((ROWS, WIDE), F32),
        pltpu.VMEM((ROWS, WIDE), BF),
        pltpu.VMEM((blocks_here, ROWS, pairs), F32),
        pltpu.VMEM((2, *held), BF),
        pltpu.VMEM((2, *held), BF),
        pltpu.VMEM((ROWS, pairs), BF),
        pltpu.SemaphoreType.DMA((2, 2)),
    ]
    if not made:
        in_specs.append(pl.BlockSpec(matrix.shape, lambda i, j, *tables: (0, 0)))
        scratch.append(pltpu.VMEM((2, ROWS, depth), BF))
        operands.append(matrix)
    return pl.pallas_call(
        functools.partial(ladder_kernel, find, made, len(tiles)),
        out_shape=jax.ShapeDtypeStruct((columns, blocks_here, TV * TV, pairs), BF),
        grid_spec=pltpu.PrefetchScalarGridSpec(
            num_scalar_prefetch=3,
            grid=(columns, tasks),
            in_specs=in_specs,
            out_specs=pl.BlockSpec((1, blocks_here, TV * TV, pairs), lambda i, j, *tables: (i, 0, 0, 0)),
            scratch_shapes=scratch,
        ),
        compiler_params=pltpu.CompilerParams(vmem_limit_bytes=LADDER_VMEM_BYTES),
        cost_estimate=pl.CostEstimate(
            flops=2 * columns * tasks * ROWS * WIDE * (depth + pairs),
            bytes_accessed=2 * columns * tasks * ROWS * 2 * (depth + pairs),
            transcendentals=0,
        ),
    )(column, task_owners, task_local, *operands)


def after(values, done):
    return lax.optimization_barrier((values, done))[0]


def per_device(factor_blocks, amplitudes, residual_in, task_owners, task_local):
    pair_count = lax.axis_size("pair")
    task_count = lax.axis_size("task")
    column = lax.axis_index("task")
    blocks_here, depth_here, _ = factor_blocks.shape
    pairs = amplitudes.shape[1]
    levels = task_count // 2
    level = column // 2
    depth = depth_here // levels
    total = 2 * levels * blocks_here
    matrix = jnp.asarray(forms_matrix())
    other_core = lambda x: lax.ppermute(x, "task", [(c, c ^ 1) for c in range(task_count)])

    def around(x, by):
        return lax.ppermute(x, "task", [(c, (c + 2 * by) % task_count) for c in range(task_count)])

    same_core = [[2 * z + k for z in range(levels)] for k in range(2)]
    slices = factor_blocks.reshape(blocks_here, levels, depth, -1)
    mine = [lax.dynamic_index_in_dim(slices, (level + by) % levels, 1, keepdims=False) for by in range(levels)]
    if pair_count == 4 and levels == 4:
        sides = [
            [(p * task_count + c, (p ^ (1 if c % 2 == turn else 2)) * task_count + c) for p in range(4) for c in range(task_count)]
            for turn in range(2)
        ]
        first_side = lambda x: lax.ppermute(x, ("pair", "task"), sides[0])
        second_side = lambda x: lax.ppermute(x, ("pair", "task"), sides[1])
        made_forms = lambda *parts: prepare(parts, column[None], matrix)
        own = amplitudes.transpose(2, 0, 1).reshape(TV * TV, blocks_here * pairs)
        amp1 = around(own, 1)
        part0 = mine[0]
        a0, b0, part1 = first_side(part0), second_side(part0), around(mine[1], 1)

        a0, b0, part0, part1, amp1, to2 = after((a0, b0, part0, part1, amp1, mine[2]), ())
        q0, a1, b1, part2 = second_side(a0), first_side(part1), second_side(part1), around(to2, 2)
        forms0 = made_forms(part0, a0, b0, q0)

        forms0, part1, a1, b1, part2, to3 = after((forms0, part1, a1, b1, part2, mine[3]), ())
        q1, a2, b2, part3 = second_side(a1), first_side(part2), second_side(part2), around(to3, 3)
        far0 = other_core(forms0)
        forms1 = made_forms(part1, a1, b1, q1)

        forms1, part2, a2, b2, part3, amp1, far0 = after((forms1, part2, a2, b2, part3, amp1, far0), ())
        q2, a3, b3, amp2 = second_side(a2), first_side(part3), second_side(part3), around(amp1, 1)
        far1 = other_core(forms1)
        forms2 = made_forms(part2, a2, b2, q2)

        forms2, part3, a3, b3, amp2, far1 = after((forms2, part3, a3, b3, amp2, far1), ())
        q3, amp3 = second_side(a3), around(amp2, 1)
        far2 = other_core(after(forms2, q3))
        forms3 = made_forms(part3, a3, b3, q3)

        forms3, amp3 = after((forms3, amp3), ())
        far3 = other_core(forms3)
        amps = prepare_amps([own, amp1, amp2, amp3], blocks_here, jnp.asarray(amp_matrix()))
        held = [forms0, far0, forms1, far1, forms2, far2, forms3, far3]
    else:
        parts = [mine[0]] + [around(mine[by], by) for by in range(1, levels)]
        tiles = amplitudes.reshape(blocks_here, pairs, TV, TV).transpose(0, 3, 2, 1)
        tiles = jnp.pad(tiles, ((0, 0), (0, 0), (0, PAD - TV), (0, 0))).reshape(blocks_here, ROWS, pairs)
        amps = lax.all_gather(tiles, "task", axis=0, axis_index_groups=same_core)
        amps = amps[(level - jnp.arange(levels)) % levels].reshape(levels * blocks_here, ROWS, pairs)
        held = lax.all_gather(jnp.stack(parts), "pair", axis=2, tiled=True)
        held = [jnp.stack([held, other_core(held)], axis=1).reshape(total, depth * pair_count, -1)]
    amps = (amps, other_core(amps))

    ladder = None
    calls = min(levels, 4)
    width = levels // calls
    order = list(reversed(range(calls)))
    for call in order:
        first = call * width
        sums = ladders(first, width, levels, blocks_here, column[None], task_owners, task_local, held, amps, matrix)
        for i in range(width):
            term = (around(sums[i], first + i) if first + i else sums[i]).astype(F32)
            ladder = term if ladder is None else ladder + term
    return residual_in + ladder.transpose(0, 2, 1)


def solution(mesh):
    placed = (P("task", "pair", None), P("task", "pair", None), P("task", "pair", None), P(), P())
    return jax.shard_map(
        per_device, mesh=mesh, in_specs=placed, out_specs=P("task", "pair", None), check_vma=False
    )
```

```python
import functools

import jax
import jax.numpy as jnp
import numpy as np
from jax import lax
from jax.experimental import pallas as pl
from jax.experimental.pallas import tpu as pltpu
from jax.sharding import PartitionSpec as P

TV = 25
PAD = 32
GROUP = 4
LANES = PAD * GROUP
GROUPS = -(-TV // GROUP)
ROWS = TV * PAD
WIDE = GROUPS * LANES
ORDER = [x for g in range(GROUP) for x in range(g, TV, GROUP)]
START = [ORDER.index(g) * PAD for g in range(GROUP)] + [ROWS]
PLACE = np.argsort(ORDER)
PREPARE_STEPS = 2
BF = jnp.bfloat16
F32 = jnp.float32
VMEM_BYTES = 32 * 1024 * 1024
LADDER_VMEM_BYTES = 50 * 1024 * 1024


def spread(spots, rows):
    return (np.arange(rows)[:, None] == spots[None, :]).astype(jnp.bfloat16)


def forms_matrix():
    x, y = np.divmod(np.arange(TV * TV), TV)
    return np.concatenate([spread(PLACE[y] * PAD + x, ROWS), spread(x * PAD + y, ROWS)], axis=0)


def amp_matrix():
    c, d = np.divmod(np.arange(TV * TV), TV)
    return spread(d * PAD + c, ROWS)


def prepare_kernel(column_ref, *refs):
    tile_refs, matrix_ref, forms_ref, all_ref = refs[:4], refs[4], refs[5], refs[6]
    count, size, _ = tile_refs[0].shape
    depth = forms_ref.shape[2]

    @pl.when(pl.program_id(0) == 0)
    def _():
        core = lax.rem(column_ref[0], 2)
        for m in range(count):
            for place, ref in zip((0, 1 + core, 2 - core, 3), tile_refs):
                start = pl.multiple_of(m * depth + place * size, size)
                all_ref[pl.ds(start, size), :] = ref[m]

    wide = 2 if depth % LANES == 0 and count % 2 == 0 else 1
    for first in range(0, count, wide):
        made = lax.dot_general(
            matrix_ref[...],
            all_ref[first * depth : (first + wide) * depth, :],
            (((1,), (1,)), ((), ())),
            preferred_element_type=F32,
        ).astype(BF)
        for m in range(wide):
            forms_ref[first + m] = made[:, m * depth : (m + 1) * depth]


def prepare(parts, column, matrix):
    count, size, width = parts[0].shape
    depth = size * len(parts)
    rows = matrix.shape[0] // PREPARE_STEPS
    in_specs = [pl.BlockSpec(part.shape, lambda i, column: (0, 0, 0)) for part in parts]
    in_specs.append(pl.BlockSpec((rows, width), lambda i, column: (i, 0)))
    return pl.pallas_call(
        prepare_kernel,
        out_shape=jax.ShapeDtypeStruct((count, matrix.shape[0], depth), BF),
        grid_spec=pltpu.PrefetchScalarGridSpec(
            num_scalar_prefetch=1,
            grid=(PREPARE_STEPS,),
            in_specs=in_specs,
            out_specs=pl.BlockSpec((count, rows, depth), lambda i, column: (0, i, 0)),
            scratch_shapes=[pltpu.VMEM((count * depth, width), BF)],
        ),
        compiler_params=pltpu.CompilerParams(vmem_limit_bytes=VMEM_BYTES),
        cost_estimate=pl.CostEstimate(
            flops=2 * count * depth * width * matrix.shape[0],
            bytes_accessed=2 * count * depth * (width + matrix.shape[0]),
            transcendentals=0,
        ),
    )(column, *parts, matrix)


def amp_kernel(matrix_ref, *refs):
    tile_refs, out_ref = refs[:-1], refs[-1]
    blocks_here, pairs = out_ref.shape[0] // len(tile_refs), out_ref.shape[2]
    for by, ref in enumerate(tile_refs):
        made = jnp.dot(matrix_ref[...], ref[...], preferred_element_type=F32).astype(BF)
        for m in range(blocks_here):
            out_ref[by * blocks_here + m] = made[:, m * pairs : (m + 1) * pairs]


def prepare_amps(parts, blocks_here, matrix):
    levels, size = len(parts), parts[0].size
    pairs = parts[0].shape[1] // blocks_here
    return pl.pallas_call(
        amp_kernel,
        out_shape=jax.ShapeDtypeStruct((levels * blocks_here, ROWS, pairs), BF),
        compiler_params=pltpu.CompilerParams(vmem_limit_bytes=VMEM_BYTES),
        cost_estimate=pl.CostEstimate(
            flops=2 * levels * size * ROWS, bytes_accessed=4 * levels * size, transcendentals=0
        ),
    )(matrix, *parts)


def turned(ref, groups, by):
    numbers = [min(A * GROUP + (p - by) % GROUP, TV - 1) for A in groups for p in range(GROUP)]
    return jnp.concatenate([ref[x * PAD : (x + 1) * PAD, :] for x in numbers], axis=0)


def pick_blocks(blocks, low, even):
    b0, b1, b2, b3 = blocks
    x, y = jnp.where(low, b0, b2), jnp.where(low, b2, b0)
    z, w = jnp.where(low, b1, b3), jnp.where(low, b3, b1)
    return jnp.where(even, x, z), jnp.where(even, w, x), jnp.where(even, y, w), jnp.where(even, z, y)


def ladder_kernel(find, made, sources, column_ref, owners_ref, local_ref, *refs):
    factor_refs, amp_refs, refs = refs[:sources], refs[sources : sources + 2], refs[sources + 2 :]
    matrix_ref, refs = None if made else refs[0], refs[0 if made else 1 :]
    out_ref, v_ref, u_ref, acc_ref, c_buf, r_buf, amp_buf, sems = refs[:8]
    column, columns = pl.program_id(0), pl.num_programs(0)
    step, steps = pl.program_id(1), pl.num_programs(1)
    at = column * steps + step
    slot = at & 1

    def fetch(choices, source, index, part, buffer, to, sem):
        for n, ref in enumerate(choices):

            @pl.when(source == n)
            def _():
                tile = ref.at[index, pl.ds(part * ROWS, ROWS)] if part is not None else ref.at[index]
                pltpu.make_async_copy(tile, buffer.at[to], sem).start()

    def fetch_task(i, j, to):
        places = find(i, j, column_ref, owners_ref, local_ref)
        fetch(factor_refs, *places["col"], 0 if made else None, c_buf, to, sems.at[to, 0])
        fetch(factor_refs, *places["row"], 1 if made else None, r_buf, to, sems.at[to, 1])

    @pl.when(at == 0)
    def _():
        fetch_task(0, 0, 0)

    @pl.when(at + 1 < columns * steps)
    def _():
        last = step == steps - 1
        fetch_task(jnp.where(last, column + 1, column), jnp.where(last, 0, step + 1), 1 - slot)

    @pl.when(step == 0)
    def _():
        acc_ref[...] = jnp.zeros_like(acc_ref)

    here = find(column, step, column_ref, owners_ref, local_ref)
    for core in range(2):

        @pl.when(here["amp"][0] == core)
        def _():
            amp_buf[...] = amp_refs[core][here["amp"][1]]

    for n, buffer in enumerate((c_buf, r_buf)):
        pltpu.make_async_copy(buffer.at[slot], buffer.at[slot], sems.at[slot, n]).wait()
    c_form, r_form, amp_form = c_buf.at[slot], r_buf.at[slot], amp_buf
    if not made:
        forms = refs[8]
        for i, tile in enumerate((c_form, r_form)):
            forms[i] = lax.dot_general(
                matrix_ref[i * ROWS : (i + 1) * ROWS, :],
                tile[...],
                (((1,), (1,)), ((), ())),
                preferred_element_type=F32,
            ).astype(BF)
        c_form, r_form = forms.at[0], forms.at[1]

    spot = lax.broadcasted_iota(jnp.int32, (PAD, LANES), 1) // PAD
    low, even = spot < 2, spot % 2 == 0
    nothing = jnp.zeros((PAD, LANES), F32)
    for first in range(0, GROUPS, 2):
        groups = range(first, min(first + 2, GROUPS))
        lanes = slice(groups[0] * LANES, (groups[-1] + 1) * LANES)
        for g in range(GROUP):
            v_ref[START[g] : START[g + 1], lanes] = lax.dot_general(
                c_form[START[g] : START[g + 1], :],
                turned(r_form, groups, g),
                (((1,), (1,)), ((), ())),
                preferred_element_type=F32,
            )
        for A in groups:
            for D in range(GROUPS):
                blocks = [
                    v_ref[START[g] + D * PAD : START[g] + (D + 1) * PAD, A * LANES : (A + 1) * LANES]
                    if D * GROUP + g < TV
                    else nothing
                    for g in range(GROUP)
                ]
                for i, block in enumerate(pick_blocks(blocks, low, even)[: TV - A * GROUP]):
                    u_ref[START[i] + A * PAD : START[i] + (A + 1) * PAD, D * LANES : (D + 1) * LANES] = block.astype(BF)
    out = local_ref[here["task"], 3]
    for i in range(GROUP):
        acc_ref[out, START[i] : START[i + 1], :] += jnp.dot(
            u_ref[START[i] : START[i + 1], :], turned(amp_form, range(GROUPS), i), preferred_element_type=F32
        )

    @pl.when(step == steps - 1)
    def _():
        for m in range(out_ref.shape[1]):
            rows = [acc_ref[m, PLACE[a] * PAD : PLACE[a] * PAD + TV, :] for a in range(TV)]
            out_ref[0, m] = jnp.concatenate(rows, axis=0).astype(BF)


def ladders(first, columns, levels, blocks_here, column, task_owners, task_local, tiles, amps, matrix):
    tasks = task_owners.shape[0] // (2 * levels)
    pairs = amps[0].shape[2]
    made = tiles[0].shape[1] == 2 * ROWS
    depth = tiles[0].shape[2] if made else tiles[0].shape[1]
    held = (ROWS, depth) if made else tiles[0].shape[1:]

    def find(i, j, column_ref, owners_ref, local_ref):
        level, core = column_ref[0] >> 1, column_ref[0] & 1
        above = level + first + i
        task = (2 * jnp.where(above >= levels, above - levels, above) + core) * tasks + j

        def place(kind):
            owner = owners_ref[task, kind]
            below = level - (owner >> 1)
            below = jnp.where(below < 0, below + levels, below)
            far = (owner & 1) ^ core
            return below, far, local_ref[task, kind]

        def factor(kind):
            below, far, m = place(kind)
            if not made:
                return 0, (below * 2 + far) * blocks_here + m
            return below * 2 + far, m

        below, far, m = place(2)
        return {"task": task, "row": factor(0), "col": factor(1), "amp": (far, below * blocks_here + m)}

    anywhere = pl.BlockSpec(memory_space=pl.ANY)
    operands = [*tiles, *amps]
    in_specs = [anywhere] * len(tiles) + [pl.BlockSpec(memory_space=pltpu.VMEM)] * 2
    scratch = [
        pltpu.VMEM((ROWS, WIDE), F32),
        pltpu.VMEM((ROWS, WIDE), BF),
        pltpu.VMEM((blocks_here, ROWS, pairs), F32),
        pltpu.VMEM((2, *held), BF),
        pltpu.VMEM((2, *held), BF),
        pltpu.VMEM((ROWS, pairs), BF),
        pltpu.SemaphoreType.DMA((2, 2)),
    ]
    if not made:
        in_specs.append(pl.BlockSpec(matrix.shape, lambda i, j, *tables: (0, 0)))
        scratch.append(pltpu.VMEM((2, ROWS, depth), BF))
        operands.append(matrix)
    return pl.pallas_call(
        functools.partial(ladder_kernel, find, made, len(tiles)),
        out_shape=jax.ShapeDtypeStruct((columns, blocks_here, TV * TV, pairs), BF),
        grid_spec=pltpu.PrefetchScalarGridSpec(
            num_scalar_prefetch=3,
            grid=(columns, tasks),
            in_specs=in_specs,
            out_specs=pl.BlockSpec((1, blocks_here, TV * TV, pairs), lambda i, j, *tables: (i, 0, 0, 0)),
            scratch_shapes=scratch,
        ),
        compiler_params=pltpu.CompilerParams(vmem_limit_bytes=LADDER_VMEM_BYTES),
        cost_estimate=pl.CostEstimate(
            flops=2 * columns * tasks * ROWS * WIDE * (depth + pairs),
            bytes_accessed=2 * columns * tasks * ROWS * 2 * (depth + pairs),
            transcendentals=0,
        ),
    )(column, task_owners, task_local, *operands)


def after(values, done):
    return lax.optimization_barrier((values, done))[0]


def per_device(factor_blocks, amplitudes, residual_in, task_owners, task_local):
    pair_count = lax.axis_size("pair")
    task_count = lax.axis_size("task")
    column = lax.axis_index("task")
    blocks_here, depth_here, _ = factor_blocks.shape
    pairs = amplitudes.shape[1]
    levels = task_count // 2
    level = column // 2
    depth = depth_here // levels
    total = 2 * levels * blocks_here
    matrix = jnp.asarray(forms_matrix())
    other_core = lambda x: lax.ppermute(x, "task", [(c, c ^ 1) for c in range(task_count)])

    def around(x, by):
        return lax.ppermute(x, "task", [(c, (c + 2 * by) % task_count) for c in range(task_count)])

    same_core = [[2 * z + k for z in range(levels)] for k in range(2)]
    slices = factor_blocks.reshape(blocks_here, levels, depth, -1)
    mine = [lax.dynamic_index_in_dim(slices, (level + by) % levels, 1, keepdims=False) for by in range(levels)]
    if pair_count == 4 and levels == 4:
        sides = [
            [(p * task_count + c, (p ^ (1 if c % 2 == turn else 2)) * task_count + c) for p in range(4) for c in range(task_count)]
            for turn in range(2)
        ]
        first_side = lambda x: lax.ppermute(x, ("pair", "task"), sides[0])
        second_side = lambda x: lax.ppermute(x, ("pair", "task"), sides[1])
        made_forms = lambda *parts: prepare(parts, column[None], matrix)
        own = amplitudes.transpose(2, 0, 1).reshape(TV * TV, blocks_here * pairs)
        amp1 = around(own, 1)
        part0 = mine[0]
        a0, b0, part1 = first_side(part0), second_side(part0), around(mine[1], 1)

        a0, b0, part0, part1, amp1, to2 = after((a0, b0, part0, part1, amp1, mine[2]), ())
        q0, a1, b1, part2 = second_side(a0), first_side(part1), second_side(part1), around(to2, 2)
        forms0 = made_forms(part0, a0, b0, q0)

        forms0, part1, a1, b1, part2, to3 = after((forms0, part1, a1, b1, part2, mine[3]), ())
        q1, a2, b2, part3 = second_side(a1), first_side(part2), second_side(part2), around(to3, 3)
        far0 = other_core(forms0)
        forms1 = made_forms(part1, a1, b1, q1)

        forms1, part2, a2, b2, part3, amp1, far0 = after((forms1, part2, a2, b2, part3, amp1, far0), ())
        q2, a3, b3, amp2 = second_side(a2), first_side(part3), second_side(part3), around(amp1, 1)
        far1 = other_core(forms1)
        forms2 = made_forms(part2, a2, b2, q2)

        forms2, part3, a3, b3, amp2, far1 = after((forms2, part3, a3, b3, amp2, far1), ())
        q3, amp3 = second_side(a3), around(amp2, 1)
        far2 = other_core(after(forms2, q3))
        forms3 = made_forms(part3, a3, b3, q3)

        forms3, amp3 = after((forms3, amp3), ())
        far3 = other_core(forms3)
        amps = prepare_amps([own, amp1, amp2, amp3], blocks_here, jnp.asarray(amp_matrix()))
        held = [forms0, far0, forms1, far1, forms2, far2, forms3, far3]
    else:
        parts = [mine[0]] + [around(mine[by], by) for by in range(1, levels)]
        tiles = amplitudes.reshape(blocks_here, pairs, TV, TV).transpose(0, 3, 2, 1)
        tiles = jnp.pad(tiles, ((0, 0), (0, 0), (0, PAD - TV), (0, 0))).reshape(blocks_here, ROWS, pairs)
        amps = lax.all_gather(tiles, "task", axis=0, axis_index_groups=same_core)
        amps = amps[(level - jnp.arange(levels)) % levels].reshape(levels * blocks_here, ROWS, pairs)
        held = lax.all_gather(jnp.stack(parts), "pair", axis=2, tiled=True)
        held = [jnp.stack([held, other_core(held)], axis=1).reshape(total, depth * pair_count, -1)]
    amps = (amps, other_core(amps))

    ladder = None
    calls = min(levels, 4)
    width = levels // calls
    order = list(reversed(range(calls)))
    for call in order:
        first = call * width
        sums = ladders(first, width, levels, blocks_here, column[None], task_owners, task_local, held, amps, matrix)
        for i in range(width):
            term = (around(sums[i], first + i) if first + i else sums[i]).astype(F32)
            ladder = term if ladder is None else ladder + term
    return residual_in + ladder.transpose(0, 2, 1)


def solution(mesh):
    placed = (P("task", "pair", None), P("task", "pair", None), P("task", "pair", None), P(), P())
    return jax.shard_map(
        per_device, mesh=mesh, in_specs=placed, out_specs=P("task", "pair", None), check_vma=False
    )
```

```python
import functools

import jax
import jax.numpy as jnp
import numpy as np
from jax import lax
from jax.experimental import pallas as pl
from jax.experimental.pallas import tpu as pltpu
from jax.sharding import PartitionSpec as P

TV = 25
PAD = 32
GROUP = 4
LANES = PAD * GROUP
GROUPS = -(-TV // GROUP)
ROWS = TV * PAD
WIDE = GROUPS * LANES
ORDER = [x for g in range(GROUP) for x in range(g, TV, GROUP)]
START = [ORDER.index(g) * PAD for g in range(GROUP)] + [ROWS]
PLACE = np.argsort(ORDER)
PREPARE_STEPS = 2
BF = jnp.bfloat16
F32 = jnp.float32
VMEM_BYTES = 48 * 1024 * 1024
LADDER_VMEM_BYTES = 50 * 1024 * 1024


def spread(spots, rows):
    return (np.arange(rows)[:, None] == spots[None, :]).astype(jnp.bfloat16)


def forms_matrix():
    x, y = np.divmod(np.arange(TV * TV), TV)
    return np.concatenate([spread(PLACE[y] * PAD + x, ROWS), spread(x * PAD + y, ROWS)], axis=0)


def amp_matrix():
    c, d = np.divmod(np.arange(TV * TV), TV)
    return spread(d * PAD + c, ROWS)


def prepare_kernel(column_ref, *refs):
    tile_refs, matrix_ref, forms_ref, all_ref = refs[:4], refs[4], refs[5], refs[6]
    count, size, _ = tile_refs[0].shape
    depth = forms_ref.shape[2]

    @pl.when(pl.program_id(0) == 0)
    def _():
        core = lax.rem(column_ref[0], 2)
        for m in range(count):
            for place, ref in zip((0, 1 + core, 2 - core, 3), tile_refs):
                start = pl.multiple_of(m * depth + place * size, size)
                all_ref[pl.ds(start, size), :] = ref[m]

    wide = 2 if depth % LANES == 0 and count % 2 == 0 else 1
    for first in range(0, count, wide):
        made = lax.dot_general(
            matrix_ref[...],
            all_ref[first * depth : (first + wide) * depth, :],
            (((1,), (1,)), ((), ())),
            preferred_element_type=F32,
        ).astype(BF)
        for m in range(wide):
            forms_ref[first + m] = made[:, m * depth : (m + 1) * depth]


def prepare(parts, column, matrix):
    count, size, width = parts[0].shape
    depth = size * len(parts)
    rows = matrix.shape[0] // PREPARE_STEPS
    in_specs = [pl.BlockSpec(part.shape, lambda i, column: (0, 0, 0)) for part in parts]
    in_specs.append(pl.BlockSpec((rows, width), lambda i, column: (i, 0)))
    return pl.pallas_call(
        prepare_kernel,
        out_shape=jax.ShapeDtypeStruct((count, matrix.shape[0], depth), BF),
        grid_spec=pltpu.PrefetchScalarGridSpec(
            num_scalar_prefetch=1,
            grid=(PREPARE_STEPS,),
            in_specs=in_specs,
            out_specs=pl.BlockSpec((count, rows, depth), lambda i, column: (0, i, 0)),
            scratch_shapes=[pltpu.VMEM((count * depth, width), BF)],
        ),
        compiler_params=pltpu.CompilerParams(vmem_limit_bytes=VMEM_BYTES),
        cost_estimate=pl.CostEstimate(
            flops=2 * count * depth * width * matrix.shape[0],
            bytes_accessed=2 * count * depth * (width + matrix.shape[0]),
            transcendentals=0,
        ),
    )(column, *parts, matrix)


def amp_kernel(matrix_ref, *refs):
    tile_refs, out_ref = refs[:-1], refs[-1]
    blocks_here, pairs = out_ref.shape[0] // len(tile_refs), out_ref.shape[2]
    for by, ref in enumerate(tile_refs):
        made = jnp.dot(matrix_ref[...], ref[...], preferred_element_type=F32).astype(BF)
        for m in range(blocks_here):
            out_ref[by * blocks_here + m] = made[:, m * pairs : (m + 1) * pairs]


def prepare_amps(parts, blocks_here, matrix):
    levels, size = len(parts), parts[0].size
    pairs = parts[0].shape[1] // blocks_here
    return pl.pallas_call(
        amp_kernel,
        out_shape=jax.ShapeDtypeStruct((levels * blocks_here, ROWS, pairs), BF),
        compiler_params=pltpu.CompilerParams(vmem_limit_bytes=VMEM_BYTES),
        cost_estimate=pl.CostEstimate(
            flops=2 * levels * size * ROWS, bytes_accessed=4 * levels * size, transcendentals=0
        ),
    )(matrix, *parts)


def turned(ref, groups, by):
    numbers = [min(A * GROUP + (p - by) % GROUP, TV - 1) for A in groups for p in range(GROUP)]
    return jnp.concatenate([ref[x * PAD : (x + 1) * PAD, :] for x in numbers], axis=0)


def pick_blocks(blocks, low, even):
    b0, b1, b2, b3 = blocks
    x, y = jnp.where(low, b0, b2), jnp.where(low, b2, b0)
    z, w = jnp.where(low, b1, b3), jnp.where(low, b3, b1)
    return jnp.where(even, x, z), jnp.where(even, w, x), jnp.where(even, y, w), jnp.where(even, z, y)


def ladder_kernel(find, made, sources, column_ref, owners_ref, local_ref, *refs):
    factor_refs, amp_refs, refs = refs[:sources], refs[sources : sources + 2], refs[sources + 2 :]
    matrix_ref, refs = None if made else refs[0], refs[0 if made else 1 :]
    out_ref, v_ref, u_ref, acc_ref, c_buf, r_buf, amp_buf, sems = refs[:8]
    column, columns = pl.program_id(0), pl.num_programs(0)
    step, steps = pl.program_id(1), pl.num_programs(1)
    at = column * steps + step
    slot = at & 1

    def fetch(choices, source, index, part, buffer, to, sem):
        for n, ref in enumerate(choices):

            @pl.when(source == n)
            def _():
                tile = ref.at[index, pl.ds(part * ROWS, ROWS)] if part is not None else ref.at[index]
                pltpu.make_async_copy(tile, buffer.at[to], sem).start()

    def fetch_task(i, j, to):
        places = find(i, j, column_ref, owners_ref, local_ref)
        fetch(factor_refs, *places["col"], 0 if made else None, c_buf, to, sems.at[to, 0])
        fetch(factor_refs, *places["row"], 1 if made else None, r_buf, to, sems.at[to, 1])

    @pl.when(at == 0)
    def _():
        fetch_task(0, 0, 0)

    @pl.when(at + 1 < columns * steps)
    def _():
        last = step == steps - 1
        fetch_task(jnp.where(last, column + 1, column), jnp.where(last, 0, step + 1), 1 - slot)

    @pl.when(step == 0)
    def _():
        acc_ref[...] = jnp.zeros_like(acc_ref)

    here = find(column, step, column_ref, owners_ref, local_ref)
    for core in range(2):

        @pl.when(here["amp"][0] == core)
        def _():
            amp_buf[...] = amp_refs[core][here["amp"][1]]

    for n, buffer in enumerate((c_buf, r_buf)):
        pltpu.make_async_copy(buffer.at[slot], buffer.at[slot], sems.at[slot, n]).wait()
    c_form, r_form, amp_form = c_buf.at[slot], r_buf.at[slot], amp_buf
    if not made:
        forms = refs[8]
        for i, tile in enumerate((c_form, r_form)):
            forms[i] = lax.dot_general(
                matrix_ref[i * ROWS : (i + 1) * ROWS, :],
                tile[...],
                (((1,), (1,)), ((), ())),
                preferred_element_type=F32,
            ).astype(BF)
        c_form, r_form = forms.at[0], forms.at[1]

    spot = lax.broadcasted_iota(jnp.int32, (PAD, LANES), 1) // PAD
    low, even = spot < 2, spot % 2 == 0
    nothing = jnp.zeros((PAD, LANES), F32)
    for first in range(0, GROUPS, 2):
        groups = range(first, min(first + 2, GROUPS))
        lanes = slice(groups[0] * LANES, (groups[-1] + 1) * LANES)
        for g in range(GROUP):
            v_ref[START[g] : START[g + 1], lanes] = lax.dot_general(
                c_form[START[g] : START[g + 1], :],
                turned(r_form, groups, g),
                (((1,), (1,)), ((), ())),
                preferred_element_type=F32,
            )
        for A in groups:
            for D in range(GROUPS):
                blocks = [
                    v_ref[START[g] + D * PAD : START[g] + (D + 1) * PAD, A * LANES : (A + 1) * LANES]
                    if D * GROUP + g < TV
                    else nothing
                    for g in range(GROUP)
                ]
                for i, block in enumerate(pick_blocks(blocks, low, even)[: TV - A * GROUP]):
                    u_ref[START[i] + A * PAD : START[i] + (A + 1) * PAD, D * LANES : (D + 1) * LANES] = block.astype(BF)
    out = local_ref[here["task"], 3]
    for i in range(GROUP):
        acc_ref[out, START[i] : START[i + 1], :] += jnp.dot(
            u_ref[START[i] : START[i + 1], :], turned(amp_form, range(GROUPS), i), preferred_element_type=F32
        )

    @pl.when(step == steps - 1)
    def _():
        for m in range(out_ref.shape[1]):
            rows = [acc_ref[m, PLACE[a] * PAD : PLACE[a] * PAD + TV, :] for a in range(TV)]
            out_ref[0, m] = jnp.concatenate(rows, axis=0).astype(BF)


def ladders(first, columns, levels, blocks_here, column, task_owners, task_local, tiles, amps, matrix):
    tasks = task_owners.shape[0] // (2 * levels)
    pairs = amps[0].shape[2]
    made = tiles[0].shape[1] == 2 * ROWS
    depth = tiles[0].shape[2] if made else tiles[0].shape[1]
    held = (ROWS, depth) if made else tiles[0].shape[1:]

    def find(i, j, column_ref, owners_ref, local_ref):
        level, core = column_ref[0] >> 1, column_ref[0] & 1
        above = level + first + i
        task = (2 * jnp.where(above >= levels, above - levels, above) + core) * tasks + j

        def place(kind):
            owner = owners_ref[task, kind]
            below = level - (owner >> 1)
            below = jnp.where(below < 0, below + levels, below)
            far = (owner & 1) ^ core
            return below, far, local_ref[task, kind]

        def factor(kind):
            below, far, m = place(kind)
            if not made:
                return 0, (below * 2 + far) * blocks_here + m
            return below * 2 + far, m

        below, far, m = place(2)
        return {"task": task, "row": factor(0), "col": factor(1), "amp": (far, below * blocks_here + m)}

    anywhere = pl.BlockSpec(memory_space=pl.ANY)
    operands = [*tiles, *amps]
    in_specs = [anywhere] * len(tiles) + [pl.BlockSpec(memory_space=pltpu.VMEM)] * 2
    scratch = [
        pltpu.VMEM((ROWS, WIDE), F32),
        pltpu.VMEM((ROWS, WIDE), BF),
        pltpu.VMEM((blocks_here, ROWS, pairs), F32),
        pltpu.VMEM((2, *held), BF),
        pltpu.VMEM((2, *held), BF),
        pltpu.VMEM((ROWS, pairs), BF),
        pltpu.SemaphoreType.DMA((2, 2)),
    ]
    if not made:
        in_specs.append(pl.BlockSpec(matrix.shape, lambda i, j, *tables: (0, 0)))
        scratch.append(pltpu.VMEM((2, ROWS, depth), BF))
        operands.append(matrix)
    return pl.pallas_call(
        functools.partial(ladder_kernel, find, made, len(tiles)),
        out_shape=jax.ShapeDtypeStruct((columns, blocks_here, TV * TV, pairs), BF),
        grid_spec=pltpu.PrefetchScalarGridSpec(
            num_scalar_prefetch=3,
            grid=(columns, tasks),
            in_specs=in_specs,
            out_specs=pl.BlockSpec((1, blocks_here, TV * TV, pairs), lambda i, j, *tables: (i, 0, 0, 0)),
            scratch_shapes=scratch,
        ),
        compiler_params=pltpu.CompilerParams(vmem_limit_bytes=LADDER_VMEM_BYTES),
        cost_estimate=pl.CostEstimate(
            flops=2 * columns * tasks * ROWS * WIDE * (depth + pairs),
            bytes_accessed=2 * columns * tasks * ROWS * 2 * (depth + pairs),
            transcendentals=0,
        ),
    )(column, task_owners, task_local, *operands)


def after(values, done):
    return lax.optimization_barrier((values, done))[0]


def per_device(factor_blocks, amplitudes, residual_in, task_owners, task_local):
    pair_count = lax.axis_size("pair")
    task_count = lax.axis_size("task")
    column = lax.axis_index("task")
    blocks_here, depth_here, _ = factor_blocks.shape
    pairs = amplitudes.shape[1]
    levels = task_count // 2
    level = column // 2
    depth = depth_here // levels
    total = 2 * levels * blocks_here
    matrix = jnp.asarray(forms_matrix())
    other_core = lambda x: lax.ppermute(x, "task", [(c, c ^ 1) for c in range(task_count)])

    def around(x, by):
        return lax.ppermute(x, "task", [(c, (c + 2 * by) % task_count) for c in range(task_count)])

    same_core = [[2 * z + k for z in range(levels)] for k in range(2)]
    slices = factor_blocks.reshape(blocks_here, levels, depth, -1)
    mine = [lax.dynamic_index_in_dim(slices, (level + by) % levels, 1, keepdims=False) for by in range(levels)]
    if pair_count == 4 and levels == 4:
        sides = [
            [(p * task_count + c, (p ^ (1 if c % 2 == turn else 2)) * task_count + c) for p in range(4) for c in range(task_count)]
            for turn in range(2)
        ]
        first_side = lambda x: lax.ppermute(x, ("pair", "task"), sides[0])
        second_side = lambda x: lax.ppermute(x, ("pair", "task"), sides[1])
        made_forms = lambda *parts: prepare(parts, column[None], matrix)
        own = amplitudes.transpose(2, 0, 1).reshape(TV * TV, blocks_here * pairs)
        amp1 = around(own, 1)
        part0 = mine[0]
        a0, b0, part1 = first_side(part0), second_side(part0), around(mine[1], 1)

        a0, b0, part0, part1, amp1, to2 = after((a0, b0, part0, part1, amp1, mine[2]), ())
        q0, a1, b1, part2 = second_side(a0), first_side(part1), second_side(part1), around(to2, 2)
        forms0 = made_forms(part0, a0, b0, q0)

        forms0, part1, a1, b1, part2, to3 = after((forms0, part1, a1, b1, part2, mine[3]), ())
        q1, a2, b2, part3 = second_side(a1), first_side(part2), second_side(part2), around(to3, 3)
        far0 = other_core(after(forms0, q1))
        forms1 = made_forms(part1, a1, b1, q1)

        forms1, part2, a2, b2, part3, amp1, far0 = after((forms1, part2, a2, b2, part3, amp1, far0), ())
        q2, a3, b3, amp2 = second_side(a2), first_side(part3), second_side(part3), around(amp1, 1)
        far1 = other_core(after(forms1, q2))
        forms2 = made_forms(part2, a2, b2, q2)

        forms2, part3, a3, b3, amp2, far1 = after((forms2, part3, a3, b3, amp2, far1), ())
        q3, amp3 = second_side(a3), around(amp2, 1)
        far2 = other_core(after(forms2, q3))
        forms3 = made_forms(part3, a3, b3, q3)

        forms3, amp3 = after((forms3, amp3), ())
        far3 = other_core(forms3)
        amps = prepare_amps([own, amp1, amp2, amp3], blocks_here, jnp.asarray(amp_matrix()))
        held = [forms0, far0, forms1, far1, forms2, far2, forms3, far3]
    else:
        parts = [mine[0]] + [around(mine[by], by) for by in range(1, levels)]
        tiles = amplitudes.reshape(blocks_here, pairs, TV, TV).transpose(0, 3, 2, 1)
        tiles = jnp.pad(tiles, ((0, 0), (0, 0), (0, PAD - TV), (0, 0))).reshape(blocks_here, ROWS, pairs)
        amps = lax.all_gather(tiles, "task", axis=0, axis_index_groups=same_core)
        amps = amps[(level - jnp.arange(levels)) % levels].reshape(levels * blocks_here, ROWS, pairs)
        held = lax.all_gather(jnp.stack(parts), "pair", axis=2, tiled=True)
        held = [jnp.stack([held, other_core(held)], axis=1).reshape(total, depth * pair_count, -1)]
    amps = (amps, other_core(amps))

    ladder = None
    calls = min(levels, 4)
    width = levels // calls
    order = list(reversed(range(calls)))
    for call in order:
        first = call * width
        sums = ladders(first, width, levels, blocks_here, column[None], task_owners, task_local, held, amps, matrix)
        for i in range(width):
            term = (around(sums[i], first + i) if first + i else sums[i]).astype(F32)
            ladder = term if ladder is None else ladder + term
    return residual_in + ladder.transpose(0, 2, 1)


def solution(mesh):
    placed = (P("task", "pair", None), P("task", "pair", None), P("task", "pair", None), P(), P())
    return jax.shard_map(
        per_device, mesh=mesh, in_specs=placed, out_specs=P("task", "pair", None), check_vma=False
    )
```
